32 devices in a mesh: aux: 8 (over z, y), row: 4 (over x, core).
Axes of the slice: x: 2, y: 2, z: 4, core: 2. Of those that a mesh axis runs over, the one named last changes fastest.
Arguments:
- rho_real: float32 [128, 128, 128], P('aux', 'row'), may hold values from -6 to 6
- rho_imag: float32 [128, 128, 128], P('aux', 'row'), may hold values from -6 to 6
- hamiltonian: float32 [128, 128], replicated, may hold values from -0.5 to 0.5
- damping: float32 [128], P('aux'), may hold values from 0.2 to 2
- couplings: int32 [128, 3, 6], P('aux'), may hold values from 0 to 127, as said below
- mode_vector: float32 [128, 128], replicated, may hold values from -4 to 4
- mode_coef: float32 [2, 128], replicated, may hold values from -1 to 1
Outputs:
- next_real: float32 [128, 128, 128], P('aux', 'row')
- next_imag: float32 [128, 128, 128], P('aux', 'row')
The draws below stay inside these ranges and needn't reach their ends.
Inputs may be any that keep to these rules, and one draw needn't show every extreme that they name: couplings[s,0,:] are target matrices below 128, couplings[s,1,:] modes below 128, couplings[s,2,:] weights 0 to 4. The couplings of the sources held by one index of aux name targets held by any one index of aux at most 12 times, and some pair reaches 12.
All inputs are finite; a program needn't handle non-finite values.
Results may differ from the reference program's by a relative error of at most 0.0018.
Values may be sent and summed in bfloat16 or wider, within the bound.
A program may use at most 64 MiB of HBM per device.

```python
import math
import jax
import jax.numpy as jnp
from jax import lax

PIG = 128
MODES = 128
LINKS = 6
STEPS = 1
AUX_DEV = 16
AUX = 128
N_AUX = 8


def draw_couplings(key, part):
    key = jax.random.fold_in(key, 11)
    count = AUX_DEV * LINKS
    slots = max(1, (count + N_AUX - 1) // N_AUX)
    key_perm, key_local, key_mode, key_weight = jax.random.split(key, 4)
    base = (jnp.arange(N_AUX * slots) // slots).astype(jnp.int32)
    shuffled = jax.vmap(lambda sub: jax.random.permutation(sub, base))(jax.random.split(key_perm, N_AUX))
    first_row = shuffled[0]
    where_last = jnp.argmax((first_row == N_AUX - 1).astype(jnp.int32)).astype(jnp.int32)
    first_row = jnp.roll(first_row, -where_last)
    shuffled = shuffled.at[0].set(first_row)
    dest = shuffled[:, :count]
    local = jax.random.randint(key_local, (N_AUX, count), 0, AUX_DEV)
    local = local.at[0, 0].set(AUX_DEV - 1)
    target = dest * AUX_DEV + local
    modes = jax.random.randint(key_mode, (N_AUX, count), 0, MODES)
    modes = modes.at[0, 0].set(MODES - 1)
    weight = jax.random.randint(key_weight, (N_AUX, count), 0, 5)
    weight = weight.at[0, 0].set(0)
    stacked = jnp.stack([target.reshape(AUX, LINKS), modes.reshape(AUX, LINKS), weight.reshape(AUX, LINKS)], axis=1)
    return stacked.astype(jnp.int32)


def shard_levels(own_key, dims, cuts, low, top_value):
    level = 1.0
    for axis_at, shards_of in cuts:
        draws = jax.random.uniform(jax.random.fold_in(jax.random.fold_in(own_key, 6), axis_at), (shards_of,), jnp.float32, low / len(cuts), top_value / len(cuts))
        level = level * jnp.repeat(jnp.exp(draws), dims[axis_at] // shards_of).reshape((-1,) + (1,) * (len(dims) - 1 - axis_at))
    return level


def centred(rng, dims, width, reach, pieces=(), dtype=jnp.bfloat16):
    entries = width * jax.random.normal(rng, dims, jnp.float32)
    if pieces:
        entries = entries * shard_levels(rng, dims, pieces, -0.22, 0.18)
    return jnp.clip(entries, -reach, reach).astype(dtype)


def setup_inputs(seed: int = 0) -> dict:
    keys = jax.random.split(jax.random.key(seed), 8)
    return {
        "rho_real": centred(keys[0], (AUX, PIG, PIG), 1.0, 6.0, ((0, 8), (1, 4)), jnp.float32),
        "rho_imag": centred(keys[1], (AUX, PIG, PIG), 1.0, 6.0, ((0, 8), (1, 4)), jnp.float32),
        "hamiltonian": centred(keys[2], (PIG, PIG), PIG ** -0.5, 0.5, (), jnp.float32),
        "damping": jnp.clip(jnp.exp(math.log(2.0) - 2.3025851 * jax.random.uniform(keys[3], (AUX,), jnp.float32) ** shard_levels(keys[3], (AUX,), ((0, 8),), -0.2, 0.2)), 0.2, 2.0),
        "couplings": draw_couplings(jax.random.fold_in(keys[7], 71), 0),
        "mode_vector": centred(keys[5], (MODES, PIG), 1.5, 4.0, (), jnp.float32),
        "mode_coef": jnp.clip(jax.random.uniform(keys[6], (2, MODES), jnp.float32, -1.0, 1.0), -1.0, 1.0),
    }


step_size = 0.1
high = lax.Precision.HIGHEST


def rounded(values):
    return lax.optimization_barrier(values.astype(jnp.bfloat16)).astype(jnp.float32)


def derivative(real_part, imag_part, energy, damping, couplings, mode_vector, mode_coef):
    prod_real = jnp.einsum("ij,ajk->aik", energy, real_part, precision=high) - jnp.einsum("aij,jk->aik", real_part, energy, precision=high)
    prod_imag = jnp.einsum("ij,ajk->aik", energy, imag_part, precision=high) - jnp.einsum("aij,jk->aik", imag_part, energy, precision=high)
    rate = damping[:, None, None]
    out_real = prod_imag - rate * real_part
    out_imag = -prod_real - rate * imag_part
    for column in range(LINKS):
        target = couplings[:, 0, column].astype(jnp.int32)
        modes = couplings[:, 1, column]
        weight = couplings[:, 2, column]
        vectors = mode_vector[modes]
        scaled = weight.astype(jnp.float32)
        plus = scaled * mode_coef[1][modes]
        minus = jnp.where(weight == 0, 1.0, scaled * mode_coef[0][modes])
        summed = vectors[:, :, None] + vectors[:, None, :]
        differ = vectors[:, :, None] - vectors[:, None, :]
        fac_real = plus[:, None, None] * summed
        fac_imag = -(minus[:, None, None] * differ)
        term_real = rounded(fac_real * real_part - fac_imag * imag_part)
        term_imag = rounded(fac_real * imag_part + fac_imag * real_part)
        out_real = out_real.at[target].add(term_real)
        out_imag = out_imag.at[target].add(term_imag)
    return out_real, out_imag


def reference(rho_real, rho_imag, hamiltonian, damping, couplings, mode_vector, mode_coef):
    energy = 0.5 * (hamiltonian + hamiltonian.T)

    def slope(real_part, imag_part):
        return derivative(real_part, imag_part, energy, damping, couplings, mode_vector, mode_coef)

    state_real, state_imag = rho_real, rho_imag
    for step in range(STEPS):
        one_real, one_imag = slope(state_real, state_imag)
        two_real, two_imag = slope(state_real + 0.5 * step_size * one_real, state_imag + 0.5 * step_size * one_imag)
        three_real, three_imag = slope(state_real + 0.5 * step_size * two_real, state_imag + 0.5 * step_size * two_imag)
        four_real, four_imag = slope(state_real + step_size * three_real, state_imag + step_size * three_imag)
        state_real = state_real + (step_size / 6.0) * (one_real + 2.0 * two_real + 2.0 * three_real + four_real)
        state_imag = state_imag + (step_size / 6.0) * (one_imag + 2.0 * two_imag + 2.0 * three_imag + four_imag)
    return state_real, state_imag
```

```python
import functools

import jax
import jax.numpy as jnp
from jax import lax
from jax.experimental import pallas as pl
from jax.experimental.pallas import tpu as pltpu
from jax.sharding import PartitionSpec as P

step_size = 0.1
high = lax.Precision.HIGHEST
MESH = pl.DeviceIdType.MESH
CHUNKS = 2
STAGES = 4


def as_sent(x):
    return jax.tree.map(lambda a: a.astype(jnp.bfloat16) if a.dtype == jnp.float32 else a, x)


def by_terms(rho_real, rho_imag, hamiltonian, damping, couplings, mode_vector, mode_coef):
    energy = 0.5 * (hamiltonian + hamiltonian.T)
    width = energy.shape[0]
    local_aux, rows_dev, _ = rho_real.shape
    per_aux = couplings.shape[2]
    row_index = lax.axis_index("row")
    energy_rows = lax.dynamic_slice_in_dim(energy, row_index * rows_dev, rows_dev, 0)
    devices = lax.axis_size("aux")
    count = local_aux * per_aux
    slots = max(1, -(-count // devices))
    targets = couplings[:, 0, :].reshape(count)
    modes = couplings[:, 1, :].reshape(count)
    weights = couplings[:, 2, :].reshape(count)
    dest = targets // local_aux
    local_target = targets % local_aux
    order = jnp.arange(count)
    same_dest = (dest[:, None] == dest[None, :]) & (order[None, :] < order[:, None])
    ranked = jnp.sum(same_dest.astype(jnp.int32), axis=1)
    slot_of = dest * slots + ranked
    picker = (modes[:, None] == jnp.arange(mode_vector.shape[0])[None, :]).astype(jnp.float32)
    vectors = jnp.dot(picker, mode_vector, precision=high, preferred_element_type=jnp.float32)
    coefs = jnp.dot(picker, mode_coef.T, precision=high, preferred_element_type=jnp.float32)
    scaled = weights.astype(jnp.float32)
    plus = scaled * coefs[:, 1]
    minus = jnp.where(weights == 0, 1.0, scaled * coefs[:, 0])
    row_vec = lax.dynamic_slice_in_dim(vectors, row_index * rows_dev, rows_dev, 1)
    summed = row_vec[:, :, None] + vectors[:, None, :]
    differ = row_vec[:, :, None] - vectors[:, None, :]
    fac_real = (plus[:, None, None] * summed).reshape(local_aux, per_aux, rows_dev, width)
    fac_imag = (-(minus[:, None, None] * differ)).reshape(local_aux, per_aux, rows_dev, width)
    marks = jnp.zeros((devices * slots, local_aux), jnp.bfloat16).at[slot_of, local_target].set(1.0)
    rate = damping[:, None, None]

    def derivative(real_part, imag_part):
        zeros_block = jnp.zeros_like(real_part)
        left_real = zeros_block + jnp.einsum(
            "ij,ajk->aik",
            energy_rows,
            lax.all_gather(as_sent(real_part), "row", axis=1, tiled=True),
            precision=high,
        )
        left_imag = zeros_block + jnp.einsum(
            "ij,ajk->aik",
            energy_rows,
            lax.all_gather(as_sent(imag_part), "row", axis=1, tiled=True),
            precision=high,
        )
        prod_real = left_real - jnp.einsum("aij,jk->aik", real_part, energy, precision=high)
        prod_imag = left_imag - jnp.einsum("aij,jk->aik", imag_part, energy, precision=high)
        source_real = real_part[:, None]
        source_imag = imag_part[:, None]
        term_real = (
            (fac_real * source_real - fac_imag * source_imag)
            .astype(jnp.bfloat16)
            .reshape(count, rows_dev, width)
        )
        term_imag = (
            (fac_real * source_imag + fac_imag * source_real)
            .astype(jnp.bfloat16)
            .reshape(count, rows_dev, width)
        )
        send_real = (
            jnp.zeros((devices * slots, rows_dev, width), jnp.bfloat16).at[slot_of].set(term_real)
        )
        send_imag = (
            jnp.zeros((devices * slots, rows_dev, width), jnp.bfloat16).at[slot_of].set(term_imag)
        )
        got_real, got_imag, got_marks = (
            lax.all_to_all(send_real, "aux", split_axis=0, concat_axis=0, tiled=True),
            lax.all_to_all(send_imag, "aux", split_axis=0, concat_axis=0, tiled=True),
            lax.all_to_all(marks, "aux", split_axis=0, concat_axis=0, tiled=True),
        )
        incoming_real = jnp.einsum(
            "sa,srp->arp", got_marks, got_real, preferred_element_type=jnp.float32
        )
        incoming_imag = jnp.einsum(
            "sa,srp->arp", got_marks, got_imag, preferred_element_type=jnp.float32
        )
        out_real = prod_imag - rate * real_part + incoming_real
        out_imag = -prod_real - rate * imag_part + incoming_imag
        return (out_real, out_imag)

    state_real, state_imag = (rho_real, rho_imag)
    one_real, one_imag = derivative(state_real, state_imag)
    two_real, two_imag = derivative(
        state_real + 0.5 * step_size * one_real, state_imag + 0.5 * step_size * one_imag
    )
    three_real, three_imag = derivative(
        state_real + 0.5 * step_size * two_real, state_imag + 0.5 * step_size * two_imag
    )
    four_real, four_imag = derivative(
        state_real + step_size * three_real, state_imag + step_size * three_imag
    )
    state_real = state_real + step_size / 6.0 * (
        one_real + 2.0 * two_real + 2.0 * three_real + four_real
    )
    state_imag = state_imag + step_size / 6.0 * (
        one_imag + 2.0 * two_imag + 2.0 * three_imag + four_imag
    )
    return (state_real, state_imag)


def kernel(
    lines,
    row_devs,
    half,
    src_ref,
    keep_ref,
    last_ref,
    rate_ref,
    real_ref,
    imag_ref,
    energy_ref,
    facr_ref,
    faci_ref,
    outr_ref,
    outi_ref,
    *scratch,
):
    n_aux, rows_dev, width = real_ref.shape
    rows = rows_dev // CHUNKS
    scratch = list(scratch)
    held = [[scratch.pop(0) for _ in range(CHUNKS)] for _ in range(STAGES)]
    full = [scratch.pop(0) for _ in range(STAGES)]
    give = [[scratch.pop(0) for _ in range(CHUNKS)] for _ in range(STAGES)]
    take = [[scratch.pop(0) for _ in range(CHUNKS)] for _ in range(STAGES)]
    run, now, total, left, right, e_left, e_right, zs, zr, rs, rr, ys, yr = scratch

    aux = lax.axis_index("aux")
    row = lax.axis_index("row")
    line = aux // 2
    beside = aux + 1 - 2 * lax.rem(aux, 2)
    line_peers = [lax.rem(aux + 2 * k, 2 * lines) for k in range(1, lines)]
    row_peers = [lax.rem(row + k, row_devs) for k in range(1, row_devs)]
    own = pl.ds(pl.multiple_of(line * n_aux, n_aux), n_aux)

    barrier = pltpu.get_barrier_semaphore()
    peers = [(p, row) for p in line_peers + [beside]] + [(aux, p) for p in row_peers]
    for p in peers:
        pl.semaphore_signal(barrier, inc=1, device_id=p, device_id_type=MESH)
    pl.semaphore_wait(barrier, len(peers))

    copies = []

    def send(src, dst, s_sem, r_sem, device):
        c = pltpu.make_async_remote_copy(
            src_ref=src,
            dst_ref=dst,
            send_sem=s_sem,
            recv_sem=r_sem,
            device_id=device,
            device_id_type=MESH,
        )
        c.start()
        copies.append(c)
        return c

    line_copies, row_copies = {}, {}

    def own_rows(c):
        return pl.ds(pl.multiple_of(row * rows_dev + c * rows, rows), rows)

    def share(st, c):
        block = held[st][c].at[own]
        line_copies[st, c] = [
            send(block, block, zs.at[st, c, k], zr.at[st, c, k], (p, row))
            for k, p in enumerate(line_peers)
        ]
        row_copies[st, c] = [
            send(
                block,
                full[st].at[:, :, own_rows(c), :],
                rs.at[st, c, k],
                rr.at[st, c, k],
                (aux, p),
            )
            for k, p in enumerate(row_peers)
        ]

    def place(st, c, a, part, x):
        b = x.astype(jnp.bfloat16)
        held[st][c][line * n_aux + a, part] = b
        full[st][a, part, own_rows(c), :] = b

    for c in range(CHUNKS):

        @pl.loop(0, n_aux)
        def _(a, c=c):
            for part, ref in enumerate((real_ref, imag_ref)):
                place(0, c, a, part, ref[a, c * rows : (c + 1) * rows, :])

        share(0, c)

    energy = energy_ref[...]
    e_hi = energy.astype(jnp.bfloat16)
    e_right[:, :width] = e_hi
    e_right[:, width:] = (energy - e_hi.astype(jnp.float32)).astype(jnp.bfloat16)
    mine = energy_ref[pl.ds(pl.multiple_of(row * rows_dev, rows_dev), rows_dev), :]
    m_hi = mine.astype(jnp.bfloat16)
    e_left[:rows_dev] = m_hi
    e_left[rows_dev:] = (mine - m_hi.astype(jnp.float32)).astype(jnp.bfloat16)
    run[0] = jnp.zeros(run.shape[1:], jnp.float32)

    def gather_sum(st, c, group):
        cut = slice(c * rows, (c + 1) * rows)

        def body(e, acc):
            ar, ai = acc
            i = group * half + e
            s = src_ref[i]
            keep = keep_ref[i]
            xr = held[st][c][s, 0].astype(jnp.float32)
            xi = held[st][c][s, 1].astype(jnp.float32)
            fr = facr_ref[i, cut, :]
            fi = faci_ref[i, cut, :]
            ar = keep * ar + (fr * xr - fi * xi)
            ai = keep * ai + (fr * xi + fi * xr)
            run[e + 1, 0] = ar
            run[e + 1, 1] = ai
            return ar, ai

        zero = jnp.zeros((rows, width), jnp.float32)
        lax.fori_loop(0, half, body, (zero, zero), unroll=4)

    for st in range(STAGES):
        for c in range(CHUNKS):
            cut = slice(c * rows, (c + 1) * rows)
            if c == 0:
                for cc in range(CHUNKS):
                    for d in row_copies[st, cc]:
                        d.wait_recv()

                @pl.loop(0, n_aux)
                def _(a, st=st):
                    for part in range(2):
                        both = jnp.dot(
                            e_left[...], full[st][a, part], preferred_element_type=jnp.float32
                        )
                        left[a, part] = both[:rows_dev] + both[rows_dev:]

            flat = held[st][c][own].reshape(n_aux * 2 * rows, width)
            both = jnp.dot(flat, e_right[...], preferred_element_type=jnp.float32)
            right[...] = (both[:, :width] + both[:, width:]).reshape(n_aux, 2, rows, width)

            for d in line_copies[st, c]:
                d.wait_recv()
            gather_sum(st, c, 0)

            @pl.loop(0, n_aux)
            def _(a, st=st, c=c):
                give[st][c][a] = run[last_ref[a]].astype(jnp.bfloat16)

            across = send(give[st][c], take[st][c], ys.at[st, c], yr.at[st, c], (beside, row))
            gather_sum(st, c, 1)
            across.wait_recv()

            weight = step_size / 6.0 * (1.0 if st in (0, STAGES - 1) else 2.0)
            ahead = step_size if st == STAGES - 2 else 0.5 * step_size

            @pl.loop(0, n_aux)
            def _(a, st=st, c=c, cut=cut, weight=weight, ahead=ahead):
                came = run[last_ref[n_aux + a]] + take[st][c][a].astype(jnp.float32)
                prod_r = left[a, 0, cut, :] - right[a, 0]
                prod_i = left[a, 1, cut, :] - right[a, 1]
                rate = rate_ref[a]
                base_r = real_ref[a, cut, :]
                base_i = imag_ref[a, cut, :]
                now_r = base_r if st == 0 else now[a, 0, cut, :]
                now_i = base_i if st == 0 else now[a, 1, cut, :]
                k_r = prod_i - rate * now_r + came[0]
                k_i = came[1] - prod_r - rate * now_i
                tot_r = (base_r if st == 0 else total[a, 0, cut, :]) + weight * k_r
                tot_i = (base_i if st == 0 else total[a, 1, cut, :]) + weight * k_i
                if st == STAGES - 1:
                    outr_ref[a, cut, :] = tot_r
                    outi_ref[a, cut, :] = tot_i
                else:
                    total[a, 0, cut, :] = tot_r
                    total[a, 1, cut, :] = tot_i
                    next_r = base_r + ahead * k_r
                    next_i = base_i + ahead * k_i
                    now[a, 0, cut, :] = next_r
                    now[a, 1, cut, :] = next_i
                    place(st + 1, c, a, 0, next_r)
                    place(st + 1, c, a, 1, next_i)

            if st < STAGES - 1:
                share(st + 1, c)

    for d in copies:
        d.wait_send()


def by_states(rho_real, rho_imag, hamiltonian, damping, couplings, mode_vector, mode_coef):
    energy = 0.5 * (hamiltonian + hamiltonian.T)
    n_aux, rows_dev, width = rho_real.shape
    per_aux = couplings.shape[2]
    devices = lax.axis_size("aux")
    row_devs = lax.axis_size("row")
    lines = devices // 2
    slots = max(1, -(-n_aux * per_aux // devices))
    half = lines * slots
    aux = lax.axis_index("aux")
    row = lax.axis_index("row")
    line, side = aux // 2, aux % 2

    every = lax.all_gather(couplings, "aux", axis=0, tiled=True)
    every = every.reshape(lines, 2, n_aux, 3, per_aux)
    every = lax.dynamic_index_in_dim(every, side, 1, keepdims=False)
    count = lines * n_aux * per_aux
    targets = every[:, :, 0, :].reshape(count)
    modes = every[:, :, 1, :].reshape(count)
    weights = every[:, :, 2, :].reshape(count)
    order = jnp.arange(count)
    sources = order // per_aux
    dest = targets // n_aux
    chosen = dest // 2 == line
    group = (dest % 2 == side).astype(jnp.int32)
    key = jnp.where(chosen, group * n_aux + targets % n_aux, 2 * n_aux)
    before = (key[None, :] < key[:, None]) | (
        (key[None, :] == key[:, None]) & (order[None, :] < order[:, None])
    )
    same_group = chosen[None, :] & (group[None, :] == group[:, None])
    ranked = jnp.sum((before & same_group).astype(jnp.int32), axis=1)
    slot_of = jnp.where(chosen, group * half + ranked, -1)
    pick = slot_of[None, :] == jnp.arange(2 * half)[:, None]

    def picked(values):
        return jnp.sum(jnp.where(pick, values[None, :], 0), axis=1)

    src = picked(sources)
    mode = picked(modes)
    weight = picked(weights)
    filled = picked(jnp.ones_like(order))
    at_key = picked(key) + (1 - filled) * (2 * n_aux)
    previous = jnp.concatenate([jnp.full((1,), -1, at_key.dtype), at_key[:-1]])
    first = jnp.arange(2 * half) % half == 0
    keep = ((at_key == previous) & ~first).astype(jnp.float32)
    wanted = jnp.arange(2 * n_aux)
    in_group = chosen[None, :] & (group[None, :] == wanted[:, None] // n_aux)
    upto = jnp.sum((in_group & (key[None, :] <= wanted[:, None])).astype(jnp.int32), axis=1)
    any_here = jnp.any(key[None, :] == wanted[:, None], axis=1)
    last = jnp.where(any_here, upto, 0)

    picker = (mode[:, None] == jnp.arange(mode_vector.shape[0])[None, :]).astype(jnp.float32)
    vectors = jnp.dot(picker, mode_vector, precision=high, preferred_element_type=jnp.float32)
    coefs = jnp.dot(picker, mode_coef.T, precision=high, preferred_element_type=jnp.float32)
    scaled = weight.astype(jnp.float32)
    there = filled.astype(jnp.float32)
    plus = there * scaled * coefs[:, 1]
    minus = there * jnp.where(weight == 0, 1.0, scaled * coefs[:, 0])
    row_vec = lax.dynamic_slice_in_dim(vectors, row * rows_dev, rows_dev, 1)
    fac_real = plus[:, None, None] * (row_vec[:, :, None] + vectors[:, None, :])
    fac_imag = -minus[:, None, None] * (row_vec[:, :, None] - vectors[:, None, :])

    rows = rows_dev // CHUNKS
    smem = pl.BlockSpec(memory_space=pltpu.SMEM)
    vmem = pl.BlockSpec(memory_space=pltpu.VMEM)
    bf16, f32 = jnp.bfloat16, jnp.float32
    piece = pltpu.VMEM((n_aux, 2, rows, width), bf16)
    dma = pltpu.SemaphoreType.DMA
    grid = (STAGES, CHUNKS)
    scratch = (
        [pltpu.VMEM((lines * n_aux, 2, rows, width), bf16)] * (STAGES * CHUNKS)
        + [pltpu.VMEM((n_aux, 2, row_devs * rows_dev, width), bf16)] * STAGES
        + [piece] * (2 * STAGES * CHUNKS)
        + [
            pltpu.VMEM((half + 1, 2, rows, width), f32),
            pltpu.VMEM((n_aux, 2, rows_dev, width), f32),
            pltpu.VMEM((n_aux, 2, rows_dev, width), f32),
            pltpu.VMEM((n_aux, 2, rows_dev, width), f32),
            pltpu.VMEM((n_aux, 2, rows, width), f32),
            pltpu.VMEM((2 * rows_dev, width), bf16),
            pltpu.VMEM((width, 2 * width), bf16),
            dma(grid + (lines - 1,)),
            dma(grid + (lines - 1,)),
            dma(grid + (row_devs - 1,)),
            dma(grid + (row_devs - 1,)),
            dma(grid),
            dma(grid),
        ]
    )
    shape = jax.ShapeDtypeStruct((n_aux, rows_dev, width), f32)
    return pl.pallas_call(
        functools.partial(kernel, lines, row_devs, half),
        out_shape=(shape, shape),
        in_specs=[smem] * 4 + [vmem] * 5,
        out_specs=(vmem, vmem),
        scratch_shapes=scratch,
        compiler_params=pltpu.CompilerParams(
            collective_id=0, has_side_effects=True, vmem_limit_bytes=40 * 1024 * 1024
        ),
    )(src, keep, last, damping, rho_real, rho_imag, energy, fac_real, fac_imag)


def solution(mesh):
    placed = (
        P("aux", "row", None),
        P("aux", "row", None),
        P(),
        P("aux"),
        P("aux", None, None),
        P(),
        P(),
    )

    def shards(rho_real, rho_imag, hamiltonian, damping, couplings, mode_vector, mode_coef):
        args = (rho_real, rho_imag, hamiltonian, damping, couplings, mode_vector, mode_coef)
        devices = mesh.shape["aux"]
        n_aux, rows_dev, _ = rho_real.shape
        slots = max(1, -(-n_aux * couplings.shape[2] // devices))
        terms_sent = (devices - 1) * slots
        states_sent = devices // 2 * n_aux
        even = devices % 2 == 0 and devices > 2 and mesh.shape["row"] > 1
        if even and states_sent < terms_sent and rows_dev % (16 * CHUNKS) == 0:
            return by_states(*args)
        return by_terms(*args)

    return jax.shard_map(
        shards,
        mesh=mesh,
        in_specs=placed,
        out_specs=(P("aux", "row", None), P("aux", "row", None)),
        check_vma=False,
    )
```

```python
import functools

import jax
import jax.numpy as jnp
from jax import lax
from jax.experimental import pallas as pl
from jax.experimental.pallas import tpu as pltpu
from jax.sharding import PartitionSpec as P

step_size = 0.1
high = lax.Precision.HIGHEST
MESH = pl.DeviceIdType.MESH
CHUNKS = 2
STAGES = 4


def as_sent(x):
    return jax.tree.map(lambda a: a.astype(jnp.bfloat16) if a.dtype == jnp.float32 else a, x)


def by_terms(rho_real, rho_imag, hamiltonian, damping, couplings, mode_vector, mode_coef):
    energy = 0.5 * (hamiltonian + hamiltonian.T)
    width = energy.shape[0]
    local_aux, rows_dev, _ = rho_real.shape
    per_aux = couplings.shape[2]
    row_index = lax.axis_index("row")
    energy_rows = lax.dynamic_slice_in_dim(energy, row_index * rows_dev, rows_dev, 0)
    devices = lax.axis_size("aux")
    count = local_aux * per_aux
    slots = max(1, -(-count // devices))
    targets = couplings[:, 0, :].reshape(count)
    modes = couplings[:, 1, :].reshape(count)
    weights = couplings[:, 2, :].reshape(count)
    dest = targets // local_aux
    local_target = targets % local_aux
    order = jnp.arange(count)
    same_dest = (dest[:, None] == dest[None, :]) & (order[None, :] < order[:, None])
    ranked = jnp.sum(same_dest.astype(jnp.int32), axis=1)
    slot_of = dest * slots + ranked
    picker = (modes[:, None] == jnp.arange(mode_vector.shape[0])[None, :]).astype(jnp.float32)
    vectors = jnp.dot(picker, mode_vector, precision=high, preferred_element_type=jnp.float32)
    coefs = jnp.dot(picker, mode_coef.T, precision=high, preferred_element_type=jnp.float32)
    scaled = weights.astype(jnp.float32)
    plus = scaled * coefs[:, 1]
    minus = jnp.where(weights == 0, 1.0, scaled * coefs[:, 0])
    row_vec = lax.dynamic_slice_in_dim(vectors, row_index * rows_dev, rows_dev, 1)
    summed = row_vec[:, :, None] + vectors[:, None, :]
    differ = row_vec[:, :, None] - vectors[:, None, :]
    fac_real = (plus[:, None, None] * summed).reshape(local_aux, per_aux, rows_dev, width)
    fac_imag = (-(minus[:, None, None] * differ)).reshape(local_aux, per_aux, rows_dev, width)
    marks = jnp.zeros((devices * slots, local_aux), jnp.bfloat16).at[slot_of, local_target].set(1.0)
    rate = damping[:, None, None]

    def derivative(real_part, imag_part):
        zeros_block = jnp.zeros_like(real_part)
        left_real = zeros_block + jnp.einsum(
            "ij,ajk->aik",
            energy_rows,
            lax.all_gather(as_sent(real_part), "row", axis=1, tiled=True),
            precision=high,
        )
        left_imag = zeros_block + jnp.einsum(
            "ij,ajk->aik",
            energy_rows,
            lax.all_gather(as_sent(imag_part), "row", axis=1, tiled=True),
            precision=high,
        )
        prod_real = left_real - jnp.einsum("aij,jk->aik", real_part, energy, precision=high)
        prod_imag = left_imag - jnp.einsum("aij,jk->aik", imag_part, energy, precision=high)
        source_real = real_part[:, None]
        source_imag = imag_part[:, None]
        term_real = (
            (fac_real * source_real - fac_imag * source_imag)
            .astype(jnp.bfloat16)
            .reshape(count, rows_dev, width)
        )
        term_imag = (
            (fac_real * source_imag + fac_imag * source_real)
            .astype(jnp.bfloat16)
            .reshape(count, rows_dev, width)
        )
        send_real = (
            jnp.zeros((devices * slots, rows_dev, width), jnp.bfloat16).at[slot_of].set(term_real)
        )
        send_imag = (
            jnp.zeros((devices * slots, rows_dev, width), jnp.bfloat16).at[slot_of].set(term_imag)
        )
        got_real, got_imag, got_marks = (
            lax.all_to_all(send_real, "aux", split_axis=0, concat_axis=0, tiled=True),
            lax.all_to_all(send_imag, "aux", split_axis=0, concat_axis=0, tiled=True),
            lax.all_to_all(marks, "aux", split_axis=0, concat_axis=0, tiled=True),
        )
        incoming_real = jnp.einsum(
            "sa,srp->arp", got_marks, got_real, preferred_element_type=jnp.float32
        )
        incoming_imag = jnp.einsum(
            "sa,srp->arp", got_marks, got_imag, preferred_element_type=jnp.float32
        )
        out_real = prod_imag - rate * real_part + incoming_real
        out_imag = -prod_real - rate * imag_part + incoming_imag
        return (out_real, out_imag)

    state_real, state_imag = (rho_real, rho_imag)
    one_real, one_imag = derivative(state_real, state_imag)
    two_real, two_imag = derivative(
        state_real + 0.5 * step_size * one_real, state_imag + 0.5 * step_size * one_imag
    )
    three_real, three_imag = derivative(
        state_real + 0.5 * step_size * two_real, state_imag + 0.5 * step_size * two_imag
    )
    four_real, four_imag = derivative(
        state_real + step_size * three_real, state_imag + step_size * three_imag
    )
    state_real = state_real + step_size / 6.0 * (
        one_real + 2.0 * two_real + 2.0 * three_real + four_real
    )
    state_imag = state_imag + step_size / 6.0 * (
        one_imag + 2.0 * two_imag + 2.0 * three_imag + four_imag
    )
    return (state_real, state_imag)


def swap_kernel(lines, mine_ref, all_ref, local_sem, send_sem, recv_sem):
    aux = lax.axis_index("aux")
    row = lax.axis_index("row")
    line = aux // 2
    peers = [(lax.rem(aux + 2 * k, 2 * lines), row) for k in range(1, lines)]
    keep = pltpu.make_async_copy(mine_ref, all_ref.at[line], local_sem)
    keep.start()
    barrier = pltpu.get_barrier_semaphore()
    for p in peers:
        pl.semaphore_signal(barrier, inc=1, device_id=p, device_id_type=MESH)
    pl.semaphore_wait(barrier, len(peers))
    copies = []
    for k, p in enumerate(peers):
        c = pltpu.make_async_remote_copy(
            src_ref=mine_ref,
            dst_ref=all_ref.at[line],
            send_sem=send_sem.at[k],
            recv_sem=recv_sem.at[k],
            device_id=p,
            device_id_type=MESH,
        )
        c.start()
        copies.append(c)
    keep.wait()
    for c in copies:
        c.wait()


def kernel(
    lines,
    row_devs,
    half,
    src_ref,
    keep_ref,
    last_ref,
    rate_ref,
    real_in,
    imag_in,
    ham_ref,
    facr_ref,
    faci_ref,
    outr_ref,
    outi_ref,
    *scratch,
):
    n_aux, rows_dev, width = outr_ref.shape
    rows = rows_dev // CHUNKS
    scratch = list(scratch)
    held = [[scratch.pop(0) for _ in range(CHUNKS)] for _ in range(STAGES)]
    full = [scratch.pop(0) for _ in range(STAGES)]
    give = [[scratch.pop(0) for _ in range(CHUNKS)] for _ in range(STAGES)]
    take = [[scratch.pop(0) for _ in range(CHUNKS)] for _ in range(STAGES)]
    real_ref, imag_ref, energy_ref = scratch[:3]
    run, now, total, left, right, e_left, e_right, zs, zr, rs, rr, ys, yr, ins = scratch[3:]

    fetched = [
        pltpu.make_async_copy(real_in, real_ref, ins.at[0]),
        pltpu.make_async_copy(imag_in, imag_ref, ins.at[1]),
    ]
    for f in fetched:
        f.start()

    aux = lax.axis_index("aux")
    row = lax.axis_index("row")
    line = aux // 2
    beside = aux + 1 - 2 * lax.rem(aux, 2)
    row_peers = [lax.rem(row + k, row_devs) for k in range(1, row_devs)]
    last_line = lines - 1

    barrier = pltpu.get_barrier_semaphore()

    @pl.when(line < last_line)
    def _():
        pl.semaphore_signal(barrier, inc=1, device_id=(aux + 2, row), device_id_type=MESH)

    @pl.when(line > 0)
    def _():
        pl.semaphore_signal(barrier, inc=1, device_id=(aux - 2, row), device_id_type=MESH)

    for p in [(beside, row)] + [(aux, p) for p in row_peers]:
        pl.semaphore_signal(barrier, inc=1, device_id=p, device_id_type=MESH)
    ends = (line == 0).astype(jnp.int32) + (line == last_line).astype(jnp.int32)
    pl.semaphore_wait(barrier, 2 + row_devs - ends)

    copies = []

    def send(src, dst, s_sem, r_sem, device):
        c = pltpu.make_async_remote_copy(
            src_ref=src,
            dst_ref=dst,
            send_sem=s_sem,
            recv_sem=r_sem,
            device_id=device,
            device_id_type=MESH,
        )
        c.start()
        copies.append(c)
        return c

    row_copies = {}

    def own_rows(c):
        return pl.ds(pl.multiple_of(row * rows_dev + c * rows, rows), rows)

    def block_at(st, c, at):
        return held[st][c].at[pl.ds(pl.multiple_of(at * n_aux, n_aux), n_aux)]

    def hop_copy(st, c, hop, way, at):
        block = block_at(st, c, at)
        return pltpu.make_async_remote_copy(
            src_ref=block,
            dst_ref=block,
            send_sem=zs.at[st, c, way, hop - 1],
            recv_sem=zr.at[st, c, way, hop - 1],
            device_id=(aux + 2 if way == 0 else aux - 2, row),
            device_id_type=MESH,
        )

    def hop_sends(hop, way):
        if way == 0:
            return (line >= hop - 1) & (line < last_line)
        return (line + hop - 1 <= last_line) & (line > 0)

    def hop_gets(hop, way):
        return line >= hop if way == 0 else line + hop <= last_line

    def hop_send(st, c, hop):
        for way in range(2):

            @pl.when(hop_sends(hop, way))
            def _(way=way):
                at = line - (hop - 1) if way == 0 else line + (hop - 1)
                hop_copy(st, c, hop, way, at).start()

    def hop_get(st, c, hop):
        for way in range(2):

            @pl.when(hop_gets(hop, way))
            def _(way=way):
                at = line - hop if way == 0 else line + hop
                hop_copy(st, c, hop, way, at).wait_recv()

    def hop_relay(st, c, hop):
        hop_get(st, c, hop)
        if hop < lines - 1:
            hop_send(st, c, hop + 1)

    def share(st, c):
        block = block_at(st, c, line)
        hop_send(st, c, 1)
        row_copies[st, c] = [
            send(
                block,
                full[st].at[:, :, own_rows(c), :],
                rs.at[st, c, k],
                rr.at[st, c, k],
                (aux, p),
            )
            for k, p in enumerate(row_peers)
        ]

    def place(st, c, a, part, x):
        b = x.astype(jnp.bfloat16)
        held[st][c][line * n_aux + a, part] = b
        full[st][a, part, own_rows(c), :] = b

    for f in fetched:
        f.wait()
    for c in range(CHUNKS):

        @pl.loop(0, n_aux)
        def _(a, c=c):
            for part, ref in enumerate((real_ref, imag_ref)):
                place(0, c, a, part, ref[a, c * rows : (c + 1) * rows, :])

        share(0, c)

    ham = ham_ref[...]
    energy_ref[...] = 0.5 * (ham + ham.T)
    energy = energy_ref[...]
    e_hi = energy.astype(jnp.bfloat16)
    e_right[:, :width] = e_hi
    e_right[:, width:] = (energy - e_hi.astype(jnp.float32)).astype(jnp.bfloat16)
    mine = energy_ref[pl.ds(pl.multiple_of(row * rows_dev, rows_dev), rows_dev), :]
    m_hi = mine.astype(jnp.bfloat16)
    e_left[:rows_dev] = m_hi
    e_left[rows_dev:] = (mine - m_hi.astype(jnp.float32)).astype(jnp.bfloat16)
    run[0] = jnp.zeros(run.shape[1:], jnp.float32)

    def gather_sum(st, c, group):
        cut = slice(c * rows, (c + 1) * rows)

        def body(e, acc):
            ar, ai = acc
            i = group * half + e
            s = src_ref[i]
            keep = keep_ref[i]
            xr = held[st][c][s, 0].astype(jnp.float32)
            xi = held[st][c][s, 1].astype(jnp.float32)
            fr = facr_ref[i, cut, :]
            fi = faci_ref[i, cut, :]
            ar = keep * ar + (fr * xr - fi * xi)
            ai = keep * ai + (fr * xi + fi * xr)
            run[e + 1, 0] = ar
            run[e + 1, 1] = ai
            return ar, ai

        zero = jnp.zeros((rows, width), jnp.float32)
        lax.fori_loop(0, half, body, (zero, zero), unroll=4)

    steps = [(st, c) for st in range(STAGES) for c in range(CHUNKS)]
    hop_relay(0, 0, 1)
    for n, (st, c) in enumerate(steps):
        if st >= 0:
            cut = slice(c * rows, (c + 1) * rows)
            if lines > 2:
                hop_relay(st, c, 2)
            own = pl.ds(pl.multiple_of(line * n_aux, n_aux), n_aux)
            flat = held[st][c][own].reshape(n_aux * 2 * rows, width)
            both = jnp.dot(flat, e_right[...], preferred_element_type=jnp.float32)
            right[...] = (both[:, :width] + both[:, width:]).reshape(n_aux, 2, rows, width)
            for hop in range(3, lines):
                hop_relay(st, c, hop)

            gather_sum(st, c, 0)

            @pl.loop(0, n_aux)
            def _(a, st=st, c=c):
                give[st][c][a] = run[last_ref[a]].astype(jnp.bfloat16)

            across = send(give[st][c], take[st][c], ys.at[st, c], yr.at[st, c], (beside, row))
            gather_sum(st, c, 1)
            if n + 1 < len(steps):
                hop_relay(*steps[n + 1], 1)
            if c == 0:
                for cc in range(CHUNKS):
                    for d in row_copies[st, cc]:
                        d.wait_recv()

                @pl.loop(0, n_aux)
                def _(a, st=st):
                    for part in range(2):
                        both = jnp.dot(
                            e_left[...], full[st][a, part], preferred_element_type=jnp.float32
                        )
                        left[a, part] = both[:rows_dev] + both[rows_dev:]

            across.wait_recv()

            weight = step_size / 6.0 * (1.0 if st in (0, STAGES - 1) else 2.0)
            ahead = step_size if st == STAGES - 2 else 0.5 * step_size

            @pl.loop(0, n_aux)
            def _(a, st=st, c=c, cut=cut, weight=weight, ahead=ahead):
                came = run[last_ref[n_aux + a]] + take[st][c][a].astype(jnp.float32)
                prod_r = left[a, 0, cut, :] - right[a, 0]
                prod_i = left[a, 1, cut, :] - right[a, 1]
                rate = rate_ref[a]
                base_r = real_ref[a, cut, :]
                base_i = imag_ref[a, cut, :]
                now_r = base_r if st == 0 else now[a, 0, cut, :]
                now_i = base_i if st == 0 else now[a, 1, cut, :]
                k_r = prod_i - rate * now_r + came[0]
                k_i = came[1] - prod_r - rate * now_i
                tot_r = (base_r if st == 0 else total[a, 0, cut, :]) + weight * k_r
                tot_i = (base_i if st == 0 else total[a, 1, cut, :]) + weight * k_i
                if st == STAGES - 1:
                    outr_ref[a, cut, :] = tot_r
                    outi_ref[a, cut, :] = tot_i
                else:
                    total[a, 0, cut, :] = tot_r
                    total[a, 1, cut, :] = tot_i
                    next_r = base_r + ahead * k_r
                    next_i = base_i + ahead * k_i
                    now[a, 0, cut, :] = next_r
                    now[a, 1, cut, :] = next_i
                    place(st + 1, c, a, 0, next_r)
                    place(st + 1, c, a, 1, next_i)

            if st < STAGES - 1:
                share(st + 1, c)

    for d in copies:
        d.wait_send()
    for st, c in steps:
        for hop in range(1, lines):
            for way in range(2):

                @pl.when(hop_sends(hop, way))
                def _(st=st, c=c, hop=hop, way=way):
                    at = line - (hop - 1) if way == 0 else line + (hop - 1)
                    hop_copy(st, c, hop, way, at).wait_send()


def by_states(rho_real, rho_imag, hamiltonian, damping, couplings, mode_vector, mode_coef):
    n_aux, rows_dev, width = rho_real.shape
    per_aux = couplings.shape[2]
    devices = lax.axis_size("aux")
    row_devs = lax.axis_size("row")
    lines = devices // 2
    slots = max(1, -(-n_aux * per_aux // devices))
    half = lines * slots
    aux = lax.axis_index("aux")
    row = lax.axis_index("row")
    line, side = aux // 2, aux % 2

    smem = pl.BlockSpec(memory_space=pltpu.SMEM)
    vmem = pl.BlockSpec(memory_space=pltpu.VMEM)
    anywhere = pl.BlockSpec(memory_space=pl.ANY)
    dma = pltpu.SemaphoreType.DMA
    local = n_aux * per_aux
    lanes = -(-local // 128) * 128
    packed = couplings.transpose(1, 0, 2).reshape(3, local)
    packed = jnp.pad(packed, ((0, 5), (0, lanes - local)))
    every = pl.pallas_call(
        functools.partial(swap_kernel, lines),
        out_shape=jax.ShapeDtypeStruct((lines, 8, lanes), jnp.int32),
        in_specs=[vmem],
        out_specs=vmem,
        scratch_shapes=[dma, dma((lines - 1,)), dma((lines - 1,))],
        compiler_params=pltpu.CompilerParams(collective_id=1, has_side_effects=True),
    )(packed)
    count = lines * local
    targets = every[:, 0, :local].reshape(count)
    modes = every[:, 1, :local].reshape(count)
    weights = every[:, 2, :local].reshape(count)
    order = jnp.arange(count)
    sources = order // per_aux
    dest = targets // n_aux
    chosen = dest // 2 == line
    group = (dest % 2 == side).astype(jnp.int32)
    key = jnp.where(chosen, group * n_aux + targets % n_aux, 2 * n_aux)
    before = (key[None, :] < key[:, None]) | (
        (key[None, :] == key[:, None]) & (order[None, :] < order[:, None])
    )
    same_group = chosen[None, :] & (group[None, :] == group[:, None])
    ranked = jnp.sum((before & same_group).astype(jnp.int32), axis=1)
    slot_of = jnp.where(chosen, group * half + ranked, -1)
    pick = slot_of[None, :] == jnp.arange(2 * half)[:, None]

    def picked(values):
        return jnp.sum(jnp.where(pick, values[None, :], 0), axis=1)

    src = picked(sources)
    mode = picked(modes)
    weight = picked(weights)
    filled = picked(jnp.ones_like(order))
    at_key = picked(key) + (1 - filled) * (2 * n_aux)
    previous = jnp.concatenate([jnp.full((1,), -1, at_key.dtype), at_key[:-1]])
    first = jnp.arange(2 * half) % half == 0
    keep = ((at_key == previous) & ~first).astype(jnp.float32)
    wanted = jnp.arange(2 * n_aux)
    in_group = chosen[None, :] & (group[None, :] == wanted[:, None] // n_aux)
    upto = jnp.sum((in_group & (key[None, :] <= wanted[:, None])).astype(jnp.int32), axis=1)
    any_here = jnp.any(key[None, :] == wanted[:, None], axis=1)
    last = jnp.where(any_here, upto, 0)

    picker = (mode[:, None] == jnp.arange(mode_vector.shape[0])[None, :]).astype(jnp.float32)
    vectors = jnp.dot(picker, mode_vector, precision=high, preferred_element_type=jnp.float32)
    coefs = jnp.dot(picker, mode_coef.T, precision=high, preferred_element_type=jnp.float32)
    scaled = weight.astype(jnp.float32)
    there = filled.astype(jnp.float32)
    plus = there * scaled * coefs[:, 1]
    minus = there * jnp.where(weight == 0, 1.0, scaled * coefs[:, 0])
    row_vec = lax.dynamic_slice_in_dim(vectors, row * rows_dev, rows_dev, 1)
    fac_real = plus[:, None, None] * (row_vec[:, :, None] + vectors[:, None, :])
    fac_imag = -minus[:, None, None] * (row_vec[:, :, None] - vectors[:, None, :])

    rows = rows_dev // CHUNKS
    bf16, f32 = jnp.bfloat16, jnp.float32
    piece = pltpu.VMEM((n_aux, 2, rows, width), bf16)
    grid = (STAGES, CHUNKS)
    scratch = (
        [pltpu.VMEM((lines * n_aux, 2, rows, width), bf16)] * (STAGES * CHUNKS)
        + [pltpu.VMEM((n_aux, 2, row_devs * rows_dev, width), bf16)] * STAGES
        + [piece] * (2 * STAGES * CHUNKS)
        + [
            pltpu.VMEM((n_aux, rows_dev, width), f32),
            pltpu.VMEM((n_aux, rows_dev, width), f32),
            pltpu.VMEM((width, width), f32),
            pltpu.VMEM((half + 1, 2, rows, width), f32),
            pltpu.VMEM((n_aux, 2, rows_dev, width), f32),
            pltpu.VMEM((n_aux, 2, rows_dev, width), f32),
            pltpu.VMEM((n_aux, 2, rows_dev, width), f32),
            pltpu.VMEM((n_aux, 2, rows, width), f32),
            pltpu.VMEM((2 * rows_dev, width), bf16),
            pltpu.VMEM((width, 2 * width), bf16),
            dma(grid + (2, lines - 1)),
            dma(grid + (2, lines - 1)),
            dma(grid + (row_devs - 1,)),
            dma(grid + (row_devs - 1,)),
            dma(grid),
            dma(grid),
            dma((2,)),
        ]
    )
    shape = jax.ShapeDtypeStruct((n_aux, rows_dev, width), f32)
    return pl.pallas_call(
        functools.partial(kernel, lines, row_devs, half),
        out_shape=(shape, shape),
        in_specs=[smem] * 4 + [anywhere] * 2 + [vmem] * 3,
        out_specs=(vmem, vmem),
        scratch_shapes=scratch,
        compiler_params=pltpu.CompilerParams(
            collective_id=0, has_side_effects=True, vmem_limit_bytes=40 * 1024 * 1024
        ),
    )(src, keep, last, damping, rho_real, rho_imag, hamiltonian, fac_real, fac_imag)


def solution(mesh):
    placed = (
        P("aux", "row", None),
        P("aux", "row", None),
        P(),
        P("aux"),
        P("aux", None, None),
        P(),
        P(),
    )

    def shards(rho_real, rho_imag, hamiltonian, damping, couplings, mode_vector, mode_coef):
        args = (rho_real, rho_imag, hamiltonian, damping, couplings, mode_vector, mode_coef)
        devices = mesh.shape["aux"]
        n_aux, rows_dev, _ = rho_real.shape
        slots = max(1, -(-n_aux * couplings.shape[2] // devices))
        terms_sent = (devices - 1) * slots
        states_sent = devices // 2 * n_aux
        even = devices % 2 == 0 and devices > 2 and mesh.shape["row"] > 1
        if even and states_sent < terms_sent and rows_dev % (16 * CHUNKS) == 0:
            return by_states(*args)
        return by_terms(*args)

    return jax.shard_map(
        shards,
        mesh=mesh,
        in_specs=placed,
        out_specs=(P("aux", "row", None), P("aux", "row", None)),
        check_vma=False,
    )
```

```python
import functools

import jax
import jax.numpy as jnp
from jax import lax
from jax.experimental import pallas as pl
from jax.experimental.pallas import tpu as pltpu
from jax.sharding import PartitionSpec as P

step_size = 0.1
high = lax.Precision.HIGHEST
MESH = pl.DeviceIdType.MESH
CHUNKS = 2
STAGES = 4


def as_sent(x):
    return jax.tree.map(lambda a: a.astype(jnp.bfloat16) if a.dtype == jnp.float32 else a, x)


def by_terms(rho_real, rho_imag, hamiltonian, damping, couplings, mode_vector, mode_coef):
    energy = 0.5 * (hamiltonian + hamiltonian.T)
    width = energy.shape[0]
    local_aux, rows_dev, _ = rho_real.shape
    per_aux = couplings.shape[2]
    row_index = lax.axis_index("row")
    energy_rows = lax.dynamic_slice_in_dim(energy, row_index * rows_dev, rows_dev, 0)
    devices = lax.axis_size("aux")
    count = local_aux * per_aux
    slots = max(1, -(-count // devices))
    targets = couplings[:, 0, :].reshape(count)
    modes = couplings[:, 1, :].reshape(count)
    weights = couplings[:, 2, :].reshape(count)
    dest = targets // local_aux
    local_target = targets % local_aux
    order = jnp.arange(count)
    same_dest = (dest[:, None] == dest[None, :]) & (order[None, :] < order[:, None])
    ranked = jnp.sum(same_dest.astype(jnp.int32), axis=1)
    slot_of = dest * slots + ranked
    picker = (modes[:, None] == jnp.arange(mode_vector.shape[0])[None, :]).astype(jnp.float32)
    vectors = jnp.dot(picker, mode_vector, precision=high, preferred_element_type=jnp.float32)
    coefs = jnp.dot(picker, mode_coef.T, precision=high, preferred_element_type=jnp.float32)
    scaled = weights.astype(jnp.float32)
    plus = scaled * coefs[:, 1]
    minus = jnp.where(weights == 0, 1.0, scaled * coefs[:, 0])
    row_vec = lax.dynamic_slice_in_dim(vectors, row_index * rows_dev, rows_dev, 1)
    summed = row_vec[:, :, None] + vectors[:, None, :]
    differ = row_vec[:, :, None] - vectors[:, None, :]
    fac_real = (plus[:, None, None] * summed).reshape(local_aux, per_aux, rows_dev, width)
    fac_imag = (-(minus[:, None, None] * differ)).reshape(local_aux, per_aux, rows_dev, width)
    marks = jnp.zeros((devices * slots, local_aux), jnp.bfloat16).at[slot_of, local_target].set(1.0)
    rate = damping[:, None, None]

    def derivative(real_part, imag_part):
        zeros_block = jnp.zeros_like(real_part)
        left_real = zeros_block + jnp.einsum(
            "ij,ajk->aik",
            energy_rows,
            lax.all_gather(as_sent(real_part), "row", axis=1, tiled=True),
            precision=high,
        )
        left_imag = zeros_block + jnp.einsum(
            "ij,ajk->aik",
            energy_rows,
            lax.all_gather(as_sent(imag_part), "row", axis=1, tiled=True),
            precision=high,
        )
        prod_real = left_real - jnp.einsum("aij,jk->aik", real_part, energy, precision=high)
        prod_imag = left_imag - jnp.einsum("aij,jk->aik", imag_part, energy, precision=high)
        source_real = real_part[:, None]
        source_imag = imag_part[:, None]
        term_real = (
            (fac_real * source_real - fac_imag * source_imag)
            .astype(jnp.bfloat16)
            .reshape(count, rows_dev, width)
        )
        term_imag = (
            (fac_real * source_imag + fac_imag * source_real)
            .astype(jnp.bfloat16)
            .reshape(count, rows_dev, width)
        )
        send_real = (
            jnp.zeros((devices * slots, rows_dev, width), jnp.bfloat16).at[slot_of].set(term_real)
        )
        send_imag = (
            jnp.zeros((devices * slots, rows_dev, width), jnp.bfloat16).at[slot_of].set(term_imag)
        )
        got_real, got_imag, got_marks = (
            lax.all_to_all(send_real, "aux", split_axis=0, concat_axis=0, tiled=True),
            lax.all_to_all(send_imag, "aux", split_axis=0, concat_axis=0, tiled=True),
            lax.all_to_all(marks, "aux", split_axis=0, concat_axis=0, tiled=True),
        )
        incoming_real = jnp.einsum(
            "sa,srp->arp", got_marks, got_real, preferred_element_type=jnp.float32
        )
        incoming_imag = jnp.einsum(
            "sa,srp->arp", got_marks, got_imag, preferred_element_type=jnp.float32
        )
        out_real = prod_imag - rate * real_part + incoming_real
        out_imag = -prod_real - rate * imag_part + incoming_imag
        return (out_real, out_imag)

    state_real, state_imag = (rho_real, rho_imag)
    one_real, one_imag = derivative(state_real, state_imag)
    two_real, two_imag = derivative(
        state_real + 0.5 * step_size * one_real, state_imag + 0.5 * step_size * one_imag
    )
    three_real, three_imag = derivative(
        state_real + 0.5 * step_size * two_real, state_imag + 0.5 * step_size * two_imag
    )
    four_real, four_imag = derivative(
        state_real + step_size * three_real, state_imag + step_size * three_imag
    )
    state_real = state_real + step_size / 6.0 * (
        one_real + 2.0 * two_real + 2.0 * three_real + four_real
    )
    state_imag = state_imag + step_size / 6.0 * (
        one_imag + 2.0 * two_imag + 2.0 * three_imag + four_imag
    )
    return (state_real, state_imag)


def kernel(
    lines,
    row_devs,
    half,
    count,
    links_per,
    rate_ref,
    coef_ref,
    real_in,
    imag_in,
    ham_ref,
    mode_ref,
    link_ref,
    outr_ref,
    outi_ref,
    *scratch,
):
    n_aux, rows_dev, width = outr_ref.shape
    rows = rows_dev // CHUNKS
    scratch = list(scratch)
    held = [[scratch.pop(0) for _ in range(CHUNKS)] for _ in range(STAGES)]
    full = [scratch.pop(0) for _ in range(STAGES)]
    give = [[scratch.pop(0) for _ in range(CHUNKS)] for _ in range(STAGES)]
    take = [[scratch.pop(0) for _ in range(CHUNKS)] for _ in range(STAGES)]
    real_ref, imag_ref, energy_ref, facr_ref, faci_ref, turned, lists, plan = scratch[:8]
    links = scratch[8 : 8 + lines]
    run, now, total, left, right, e_left, e_right = scratch[8 + lines : 15 + lines]
    zs, zr, rs, rr, ys, yr, ls, lr, ins = scratch[15 + lines :]

    fetched = [
        pltpu.make_async_copy(real_in, real_ref, ins.at[0]),
        pltpu.make_async_copy(imag_in, imag_ref, ins.at[1]),
    ]
    for f in fetched:
        f.start()

    aux = lax.axis_index("aux")
    row = lax.axis_index("row")
    line = aux // 2
    side = lax.rem(aux, 2)
    beside = aux + 1 - 2 * side
    row_peers = [lax.rem(row + k, row_devs) for k in range(1, row_devs)]
    last_line = lines - 1

    barrier = pltpu.get_barrier_semaphore()

    line_peers = [lax.rem(aux + 2 * k, 2 * lines) for k in range(1, lines)]
    peers = [(p, row) for p in line_peers + [beside]] + [(aux, p) for p in row_peers]
    for p in peers:
        pl.semaphore_signal(barrier, inc=1, device_id=p, device_id_type=MESH)
    pl.semaphore_wait(barrier, len(peers))

    copies = []

    def send(src, dst, s_sem, r_sem, device):
        c = pltpu.make_async_remote_copy(
            src_ref=src,
            dst_ref=dst,
            send_sem=s_sem,
            recv_sem=r_sem,
            device_id=device,
            device_id_type=MESH,
        )
        c.start()
        copies.append(c)
        return c

    row_copies = {}

    def own_rows(c):
        return pl.ds(pl.multiple_of(row * rows_dev + c * rows, rows), rows)

    def block_at(st, c, at):
        return held[st][c].at[pl.ds(pl.multiple_of(at * n_aux, n_aux), n_aux)]

    def hop_copy(st, c, hop, way, at):
        block = block_at(st, c, at)
        return pltpu.make_async_remote_copy(
            src_ref=block,
            dst_ref=block,
            send_sem=zs.at[st, c, way, hop - 1],
            recv_sem=zr.at[st, c, way, hop - 1],
            device_id=(aux + 2 if way == 0 else aux - 2, row),
            device_id_type=MESH,
        )

    def hop_sends(hop, way):
        if way == 0:
            return (line >= hop - 1) & (line < last_line)
        return (line + hop - 1 <= last_line) & (line > 0)

    def hop_gets(hop, way):
        return line >= hop if way == 0 else line + hop <= last_line

    def hop_send(st, c, hop):
        for way in range(2):

            @pl.when(hop_sends(hop, way))
            def _(way=way):
                at = line - (hop - 1) if way == 0 else line + (hop - 1)
                hop_copy(st, c, hop, way, at).start()

    def hop_get(st, c, hop):
        for way in range(2):

            @pl.when(hop_gets(hop, way))
            def _(way=way):
                at = line - hop if way == 0 else line + hop
                hop_copy(st, c, hop, way, at).wait_recv()

    def hop_relay(st, c, hop):
        hop_get(st, c, hop)
        if hop < lines - 1:
            hop_send(st, c, hop + 1)

    def share(st, c):
        block = block_at(st, c, line)
        hop_send(st, c, 1)
        row_copies[st, c] = [
            send(
                block,
                full[st].at[:, :, own_rows(c), :],
                rs.at[st, c, k],
                rr.at[st, c, k],
                (aux, p),
            )
            for k, p in enumerate(row_peers)
        ]

    def place(st, c, a, part, x):
        b = x.astype(jnp.bfloat16)
        held[st][c][line * n_aux + a, part] = b
        full[st][a, part, own_rows(c), :] = b

    link_copies = [
        send(link_ref, links[k], ls.at[k - 1], lr.at[k - 1], (p, row))
        for k, p in enumerate(line_peers, 1)
    ]
    for f in fetched:
        f.wait()
    for c in range(CHUNKS):

        @pl.loop(0, n_aux)
        def _(a, c=c):
            for part, ref in enumerate((real_ref, imag_ref)):
                place(0, c, a, part, ref[a, c * rows : (c + 1) * rows, :])

        share(0, c)

    ham = ham_ref[...]
    energy_ref[...] = 0.5 * (ham + ham.T)
    energy = energy_ref[...]
    e_hi = energy.astype(jnp.bfloat16)
    e_right[:, :width] = e_hi
    e_right[:, width:] = (energy - e_hi.astype(jnp.float32)).astype(jnp.bfloat16)
    mine = energy_ref[pl.ds(pl.multiple_of(row * rows_dev, rows_dev), rows_dev), :]
    m_hi = mine.astype(jnp.bfloat16)
    e_left[:rows_dev] = m_hi
    e_left[rows_dev:] = (mine - m_hi.astype(jnp.float32)).astype(jnp.bfloat16)
    run[0] = jnp.zeros(run.shape[1:], jnp.float32)

    turned[...] = mode_ref[...].T
    links[0][...] = link_ref[...]
    for d in link_copies:
        d.wait_recv()
    lanes = link_ref.shape[1]
    i32 = jnp.int32
    lane = lax.broadcasted_iota(i32, (1, lanes), 1)
    diagonal = lax.broadcasted_iota(i32, (lanes, lanes), 0) == lax.broadcasted_iota(
        i32, (lanes, lanes), 1
    )
    far = 1 << 20
    keys_row, modes_row, weights_row, source_row, keys_col = [], [], [], [], []
    for k in range(lines):
        from_line = lax.rem(line - k + lines, lines)
        target = links[k][0:1, :]
        dest = target // n_aux
        chosen = (dest // 2 == line) & (lane < count)
        group = jnp.where(lax.rem(dest, 2) == side, 1, 0)
        key = group * n_aux + lax.rem(target, n_aux)
        place_in = from_line * lanes + lane
        key = jnp.where(chosen, key * (lines * lanes) + place_in, far)
        keys_row.append(key)
        modes_row.append(links[k][1:2, :])
        weights_row.append(links[k][2:3, :])
        source_row.append(from_line * n_aux + lane // links_per)
        keys_col.append(jnp.sum(jnp.where(diagonal, key, 0), axis=1, keepdims=True))
    span = lines * lanes
    key = jnp.concatenate(keys_row, axis=1)
    column = jnp.concatenate(keys_col, axis=0)
    chosen = key < far
    before = column < key
    rank = jnp.sum(jnp.where(before, 1, 0), axis=0, keepdims=True)
    again = jnp.sum(jnp.where(before & (column // span == key // span), 1, 0), axis=0, keepdims=True)
    second = n_aux * span
    first_count = jnp.sum(jnp.where(key < second, 1, 0), axis=1, keepdims=True)
    ranked = jnp.where(key < second, rank, rank - first_count)
    slot = jnp.where(key < second, ranked, ranked + half)
    slot = jnp.where(chosen & (ranked < half), slot, -1)
    pick = lax.broadcasted_iota(i32, (2 * half, span), 0) == slot

    def picked(values):
        return jnp.sum(jnp.where(pick, values, 0), axis=1, keepdims=True)

    at = lax.broadcasted_iota(i32, (2 * half, 128), 1)
    table = jnp.where(at == 0, picked(jnp.concatenate(source_row, axis=1)), 0)
    table = jnp.where(at == 1, picked(jnp.concatenate(modes_row, axis=1)), table)
    table = jnp.where(at == 2, picked(jnp.concatenate(weights_row, axis=1)), table)
    table = jnp.where(at == 3, picked(jnp.where(again > 0, 1, 0)), table)
    table = jnp.where(at == 4, picked(jnp.ones_like(key)), table)
    lists[: 2 * half] = table
    wanted = lax.broadcasted_iota(i32, (2 * n_aux, span), 0)
    upto = jnp.sum(jnp.where(key < (wanted + 1) * span, 1, 0), axis=1, keepdims=True)
    here = jnp.sum(jnp.where(key // span == wanted, 1, 0), axis=1, keepdims=True)
    tall = lax.broadcasted_iota(i32, (2 * n_aux, 1), 0)
    upto = jnp.minimum(jnp.where(tall < n_aux, upto, upto - first_count), half)
    lists[2 * half :] = jnp.broadcast_to(jnp.where(here > 0, upto, 0), (2 * n_aux, 128))
    planned = pltpu.make_async_copy(lists, plan, ins.at[2])
    planned.start()
    planned.wait()

    mode_lane = lax.broadcasted_iota(i32, (rows_dev, mode_ref.shape[0]), 1)

    @pl.loop(0, 2 * half)
    def _(e):
        m = plan[e, 1]
        w = plan[e, 2]
        scaled = w.astype(jnp.float32)
        plus = scaled * coef_ref[1, m]
        minus = jnp.where(w == 0, plan[e, 4].astype(jnp.float32), scaled * coef_ref[0, m])
        across = mode_ref[pl.ds(m, 1), :]
        mine = turned[pl.ds(pl.multiple_of(row * rows_dev, rows_dev), rows_dev), :]
        down = jnp.sum(jnp.where(mode_lane == m, mine, 0.0), axis=1, keepdims=True)
        facr_ref[e] = plus * (down + across)
        faci_ref[e] = -minus * (down - across)

    def gather_sum(st, c, group):
        cut = slice(c * rows, (c + 1) * rows)

        def body(e, acc):
            ar, ai = acc
            i = group * half + e
            s = plan[i, 0]
            keep = plan[i, 3].astype(jnp.float32)
            xr = held[st][c][s, 0].astype(jnp.float32)
            xi = held[st][c][s, 1].astype(jnp.float32)
            fr = facr_ref[i, cut, :]
            fi = faci_ref[i, cut, :]
            ar = keep * ar + (fr * xr - fi * xi)
            ai = keep * ai + (fr * xi + fi * xr)
            run[e + 1, 0] = ar
            run[e + 1, 1] = ai
            return ar, ai

        zero = jnp.zeros((rows, width), jnp.float32)
        lax.fori_loop(0, half, body, (zero, zero), unroll=4)

    steps = [(st, c) for st in range(STAGES) for c in range(CHUNKS)]
    hop_relay(0, 0, 1)
    for n, (st, c) in enumerate(steps):
        cut = slice(c * rows, (c + 1) * rows)
        if lines > 2:
            hop_relay(st, c, 2)
        own = pl.ds(pl.multiple_of(line * n_aux, n_aux), n_aux)
        flat = held[st][c][own].reshape(n_aux * 2 * rows, width)
        both = jnp.dot(flat, e_right[...], preferred_element_type=jnp.float32)
        right[...] = (both[:, :width] + both[:, width:]).reshape(n_aux, 2, rows, width)
        for hop in range(3, lines):
            hop_relay(st, c, hop)

        gather_sum(st, c, 0)

        @pl.loop(0, n_aux)
        def _(a, st=st, c=c):
            give[st][c][a] = run[plan[2 * half + a, 0]].astype(jnp.bfloat16)

        across = send(give[st][c], take[st][c], ys.at[st, c], yr.at[st, c], (beside, row))
        gather_sum(st, c, 1)
        if n + 1 < len(steps):
            hop_relay(*steps[n + 1], 1)
        if c == 0:
            for cc in range(CHUNKS):
                for d in row_copies[st, cc]:
                    d.wait_recv()

            @pl.loop(0, n_aux)
            def _(a, st=st):
                for part in range(2):
                    both = jnp.dot(
                        e_left[...], full[st][a, part], preferred_element_type=jnp.float32
                    )
                    left[a, part] = both[:rows_dev] + both[rows_dev:]

        across.wait_recv()

        weight = step_size / 6.0 * (1.0 if st in (0, STAGES - 1) else 2.0)
        ahead = step_size if st == STAGES - 2 else 0.5 * step_size

        @pl.loop(0, n_aux)
        def _(a, st=st, c=c, cut=cut, weight=weight, ahead=ahead):
            came = run[plan[2 * half + n_aux + a, 0]] + take[st][c][a].astype(jnp.float32)
            prod_r = left[a, 0, cut, :] - right[a, 0]
            prod_i = left[a, 1, cut, :] - right[a, 1]
            rate = rate_ref[a]
            base_r = real_ref[a, cut, :]
            base_i = imag_ref[a, cut, :]
            now_r = base_r if st == 0 else now[a, 0, cut, :]
            now_i = base_i if st == 0 else now[a, 1, cut, :]
            k_r = prod_i - rate * now_r + came[0]
            k_i = came[1] - prod_r - rate * now_i
            tot_r = (base_r if st == 0 else total[a, 0, cut, :]) + weight * k_r
            tot_i = (base_i if st == 0 else total[a, 1, cut, :]) + weight * k_i
            if st == STAGES - 1:
                outr_ref[a, cut, :] = tot_r
                outi_ref[a, cut, :] = tot_i
            else:
                total[a, 0, cut, :] = tot_r
                total[a, 1, cut, :] = tot_i
                next_r = base_r + ahead * k_r
                next_i = base_i + ahead * k_i
                now[a, 0, cut, :] = next_r
                now[a, 1, cut, :] = next_i
                place(st + 1, c, a, 0, next_r)
                place(st + 1, c, a, 1, next_i)

        if st < STAGES - 1:
            share(st + 1, c)

    for d in copies:
        d.wait_send()
    for st, c in steps:
        for hop in range(1, lines):
            for way in range(2):

                @pl.when(hop_sends(hop, way))
                def _(st=st, c=c, hop=hop, way=way):
                    at = line - (hop - 1) if way == 0 else line + (hop - 1)
                    hop_copy(st, c, hop, way, at).wait_send()


def by_states(rho_real, rho_imag, hamiltonian, damping, couplings, mode_vector, mode_coef):
    n_aux, rows_dev, width = rho_real.shape
    per_aux = couplings.shape[2]
    devices = lax.axis_size("aux")
    row_devs = lax.axis_size("row")
    lines = devices // 2
    slots = max(1, -(-n_aux * per_aux // devices))
    half = lines * slots
    smem = pl.BlockSpec(memory_space=pltpu.SMEM)
    vmem = pl.BlockSpec(memory_space=pltpu.VMEM)
    anywhere = pl.BlockSpec(memory_space=pl.ANY)
    dma = pltpu.SemaphoreType.DMA
    count = n_aux * per_aux
    lanes = -(-count // 128) * 128
    packed = couplings.transpose(1, 0, 2).reshape(3, count)
    packed = jnp.pad(packed, ((0, 5), (0, lanes - count)))

    rows = rows_dev // CHUNKS
    bf16, f32 = jnp.bfloat16, jnp.float32
    piece = pltpu.VMEM((n_aux, 2, rows, width), bf16)
    grid = (STAGES, CHUNKS)
    scratch = (
        [pltpu.VMEM((lines * n_aux, 2, rows, width), bf16)] * (STAGES * CHUNKS)
        + [pltpu.VMEM((n_aux, 2, row_devs * rows_dev, width), bf16)] * STAGES
        + [piece] * (2 * STAGES * CHUNKS)
        + [
            pltpu.VMEM((n_aux, rows_dev, width), f32),
            pltpu.VMEM((n_aux, rows_dev, width), f32),
            pltpu.VMEM((width, width), f32),
            pltpu.VMEM((2 * half, rows_dev, width), f32),
            pltpu.VMEM((2 * half, rows_dev, width), f32),
            pltpu.VMEM((width, mode_vector.shape[0]), f32),
            pltpu.VMEM((2 * half + 2 * n_aux, 128), jnp.int32),
            pltpu.SMEM((2 * half + 2 * n_aux, 128), jnp.int32),
        ]
        + [pltpu.VMEM((8, lanes), jnp.int32)] * lines
        + [
            pltpu.VMEM((half + 1, 2, rows, width), f32),
            pltpu.VMEM((n_aux, 2, rows_dev, width), f32),
            pltpu.VMEM((n_aux, 2, rows_dev, width), f32),
            pltpu.VMEM((n_aux, 2, rows_dev, width), f32),
            pltpu.VMEM((n_aux, 2, rows, width), f32),
            pltpu.VMEM((2 * rows_dev, width), bf16),
            pltpu.VMEM((width, 2 * width), bf16),
            dma(grid + (2, lines - 1)),
            dma(grid + (2, lines - 1)),
            dma(grid + (row_devs - 1,)),
            dma(grid + (row_devs - 1,)),
            dma(grid),
            dma(grid),
            dma((lines - 1,)),
            dma((lines - 1,)),
            dma((3,)),
        ]
    )
    shape = jax.ShapeDtypeStruct((n_aux, rows_dev, width), f32)
    return pl.pallas_call(
        functools.partial(kernel, lines, row_devs, half, count, per_aux),
        out_shape=(shape, shape),
        in_specs=[smem] * 2 + [anywhere] * 2 + [vmem] * 3,
        out_specs=(vmem, vmem),
        scratch_shapes=scratch,
        compiler_params=pltpu.CompilerParams(
            collective_id=0, has_side_effects=True, vmem_limit_bytes=40 * 1024 * 1024
        ),
    )(damping, mode_coef, rho_real, rho_imag, hamiltonian, mode_vector, packed)


def solution(mesh):
    placed = (
        P("aux", "row", None),
        P("aux", "row", None),
        P(),
        P("aux"),
        P("aux", None, None),
        P(),
        P(),
    )

    def shards(rho_real, rho_imag, hamiltonian, damping, couplings, mode_vector, mode_coef):
        args = (rho_real, rho_imag, hamiltonian, damping, couplings, mode_vector, mode_coef)
        devices = mesh.shape["aux"]
        n_aux, rows_dev, _ = rho_real.shape
        slots = max(1, -(-n_aux * couplings.shape[2] // devices))
        terms_sent = (devices - 1) * slots
        states_sent = devices // 2 * n_aux
        even = devices % 2 == 0 and devices > 2 and mesh.shape["row"] > 1
        if even and states_sent < terms_sent and rows_dev % (16 * CHUNKS) == 0:
            return by_states(*args)
        return by_terms(*args)

    return jax.shard_map(
        shards,
        mesh=mesh,
        in_specs=placed,
        out_specs=(P("aux", "row", None), P("aux", "row", None)),
        check_vma=False,
    )
```

```python
import functools

import jax
import jax.numpy as jnp
from jax import lax
from jax.experimental import pallas as pl
from jax.experimental.pallas import tpu as pltpu
from jax.sharding import PartitionSpec as P

step_size = 0.1
high = lax.Precision.HIGHEST
MESH = pl.DeviceIdType.MESH
CHUNKS = 2
STAGES = 4


def as_sent(x):
    return jax.tree.map(lambda a: a.astype(jnp.bfloat16) if a.dtype == jnp.float32 else a, x)


def by_terms(rho_real, rho_imag, hamiltonian, damping, couplings, mode_vector, mode_coef):
    energy = 0.5 * (hamiltonian + hamiltonian.T)
    width = energy.shape[0]
    local_aux, rows_dev, _ = rho_real.shape
    per_aux = couplings.shape[2]
    row_index = lax.axis_index("row")
    energy_rows = lax.dynamic_slice_in_dim(energy, row_index * rows_dev, rows_dev, 0)
    devices = lax.axis_size("aux")
    count = local_aux * per_aux
    slots = max(1, -(-count // devices))
    targets = couplings[:, 0, :].reshape(count)
    modes = couplings[:, 1, :].reshape(count)
    weights = couplings[:, 2, :].reshape(count)
    dest = targets // local_aux
    local_target = targets % local_aux
    order = jnp.arange(count)
    same_dest = (dest[:, None] == dest[None, :]) & (order[None, :] < order[:, None])
    ranked = jnp.sum(same_dest.astype(jnp.int32), axis=1)
    slot_of = dest * slots + ranked
    picker = (modes[:, None] == jnp.arange(mode_vector.shape[0])[None, :]).astype(jnp.float32)
    vectors = jnp.dot(picker, mode_vector, precision=high, preferred_element_type=jnp.float32)
    coefs = jnp.dot(picker, mode_coef.T, precision=high, preferred_element_type=jnp.float32)
    scaled = weights.astype(jnp.float32)
    plus = scaled * coefs[:, 1]
    minus = jnp.where(weights == 0, 1.0, scaled * coefs[:, 0])
    row_vec = lax.dynamic_slice_in_dim(vectors, row_index * rows_dev, rows_dev, 1)
    summed = row_vec[:, :, None] + vectors[:, None, :]
    differ = row_vec[:, :, None] - vectors[:, None, :]
    fac_real = (plus[:, None, None] * summed).reshape(local_aux, per_aux, rows_dev, width)
    fac_imag = (-(minus[:, None, None] * differ)).reshape(local_aux, per_aux, rows_dev, width)
    marks = jnp.zeros((devices * slots, local_aux), jnp.bfloat16).at[slot_of, local_target].set(1.0)
    rate = damping[:, None, None]

    def derivative(real_part, imag_part):
        zeros_block = jnp.zeros_like(real_part)
        left_real = zeros_block + jnp.einsum(
            "ij,ajk->aik",
            energy_rows,
            lax.all_gather(as_sent(real_part), "row", axis=1, tiled=True),
            precision=high,
        )
        left_imag = zeros_block + jnp.einsum(
            "ij,ajk->aik",
            energy_rows,
            lax.all_gather(as_sent(imag_part), "row", axis=1, tiled=True),
            precision=high,
        )
        prod_real = left_real - jnp.einsum("aij,jk->aik", real_part, energy, precision=high)
        prod_imag = left_imag - jnp.einsum("aij,jk->aik", imag_part, energy, precision=high)
        source_real = real_part[:, None]
        source_imag = imag_part[:, None]
        term_real = (
            (fac_real * source_real - fac_imag * source_imag)
            .astype(jnp.bfloat16)
            .reshape(count, rows_dev, width)
        )
        term_imag = (
            (fac_real * source_imag + fac_imag * source_real)
            .astype(jnp.bfloat16)
            .reshape(count, rows_dev, width)
        )
        send_real = (
            jnp.zeros((devices * slots, rows_dev, width), jnp.bfloat16).at[slot_of].set(term_real)
        )
        send_imag = (
            jnp.zeros((devices * slots, rows_dev, width), jnp.bfloat16).at[slot_of].set(term_imag)
        )
        got_real, got_imag, got_marks = (
            lax.all_to_all(send_real, "aux", split_axis=0, concat_axis=0, tiled=True),
            lax.all_to_all(send_imag, "aux", split_axis=0, concat_axis=0, tiled=True),
            lax.all_to_all(marks, "aux", split_axis=0, concat_axis=0, tiled=True),
        )
        incoming_real = jnp.einsum(
            "sa,srp->arp", got_marks, got_real, preferred_element_type=jnp.float32
        )
        incoming_imag = jnp.einsum(
            "sa,srp->arp", got_marks, got_imag, preferred_element_type=jnp.float32
        )
        out_real = prod_imag - rate * real_part + incoming_real
        out_imag = -prod_real - rate * imag_part + incoming_imag
        return (out_real, out_imag)

    state_real, state_imag = (rho_real, rho_imag)
    one_real, one_imag = derivative(state_real, state_imag)
    two_real, two_imag = derivative(
        state_real + 0.5 * step_size * one_real, state_imag + 0.5 * step_size * one_imag
    )
    three_real, three_imag = derivative(
        state_real + 0.5 * step_size * two_real, state_imag + 0.5 * step_size * two_imag
    )
    four_real, four_imag = derivative(
        state_real + step_size * three_real, state_imag + step_size * three_imag
    )
    state_real = state_real + step_size / 6.0 * (
        one_real + 2.0 * two_real + 2.0 * three_real + four_real
    )
    state_imag = state_imag + step_size / 6.0 * (
        one_imag + 2.0 * two_imag + 2.0 * three_imag + four_imag
    )
    return (state_real, state_imag)


def kernel(
    lines,
    row_devs,
    half,
    count,
    links_per,
    rate_ref,
    coef_ref,
    real_in,
    imag_in,
    ham_ref,
    mode_ref,
    link_ref,
    outr_ref,
    outi_ref,
    *scratch,
):
    n_aux, rows_dev, width = outr_ref.shape
    rows = rows_dev // CHUNKS
    scratch = list(scratch)
    held = [[scratch.pop(0) for _ in range(CHUNKS)] for _ in range(STAGES)]
    full = [scratch.pop(0) for _ in range(STAGES)]
    give = [[scratch.pop(0) for _ in range(CHUNKS)] for _ in range(STAGES)]
    take = [[scratch.pop(0) for _ in range(CHUNKS)] for _ in range(STAGES)]
    real_ref, imag_ref, energy_ref, facr_ref, faci_ref, turned, lists, plan = scratch[:8]
    links = scratch[8 : 8 + lines]
    run, now, total, left, right, e_left, e_right = scratch[8 + lines : 15 + lines]
    zs, zr, rs, rr, ys, yr, ls, lr, ins = scratch[15 + lines :]

    fetched = [
        pltpu.make_async_copy(real_in, real_ref, ins.at[0]),
        pltpu.make_async_copy(imag_in, imag_ref, ins.at[1]),
    ]
    for f in fetched:
        f.start()

    aux = lax.axis_index("aux")
    row = lax.axis_index("row")
    line = aux // 2
    side = lax.rem(aux, 2)
    beside = aux + 1 - 2 * side
    row_peers = [lax.rem(row + k, row_devs) for k in range(1, row_devs)]
    last_line = lines - 1

    barrier = pltpu.get_barrier_semaphore()

    line_peers = [lax.rem(aux + 2 * k, 2 * lines) for k in range(1, lines)]
    peers = [(p, row) for p in line_peers + [beside]] + [(aux, p) for p in row_peers]
    for p in peers:
        pl.semaphore_signal(barrier, inc=1, device_id=p, device_id_type=MESH)
    pl.semaphore_wait(barrier, len(peers))

    copies = []

    def send(src, dst, s_sem, r_sem, device):
        c = pltpu.make_async_remote_copy(
            src_ref=src,
            dst_ref=dst,
            send_sem=s_sem,
            recv_sem=r_sem,
            device_id=device,
            device_id_type=MESH,
        )
        c.start()
        copies.append(c)
        return c

    row_copies = {}

    def own_rows(c):
        return pl.ds(pl.multiple_of(row * rows_dev + c * rows, rows), rows)

    def block_at(st, c, at):
        return held[st][c].at[pl.ds(pl.multiple_of(at * n_aux, n_aux), n_aux)]

    def hop_copy(st, c, hop, way, at):
        block = block_at(st, c, at)
        return pltpu.make_async_remote_copy(
            src_ref=block,
            dst_ref=block,
            send_sem=zs.at[st, c, way, hop - 1],
            recv_sem=zr.at[st, c, way, hop - 1],
            device_id=(aux + 2 if way == 0 else aux - 2, row),
            device_id_type=MESH,
        )

    def hop_sends(hop, way):
        if way == 0:
            return (line >= hop - 1) & (line < last_line)
        return (line + hop - 1 <= last_line) & (line > 0)

    def hop_gets(hop, way):
        return line >= hop if way == 0 else line + hop <= last_line

    def hop_send(st, c, hop):
        for way in range(2):

            @pl.when(hop_sends(hop, way))
            def _(way=way):
                at = line - (hop - 1) if way == 0 else line + (hop - 1)
                hop_copy(st, c, hop, way, at).start()

    def hop_get(st, c, hop):
        for way in range(2):

            @pl.when(hop_gets(hop, way))
            def _(way=way):
                at = line - hop if way == 0 else line + hop
                hop_copy(st, c, hop, way, at).wait_recv()

    def hop_relay(st, c, hop):
        hop_get(st, c, hop)
        if hop < lines - 1:
            hop_send(st, c, hop + 1)

    def share(st, c):
        block = block_at(st, c, line)
        hop_send(st, c, 1)
        row_copies[st, c] = [
            send(
                block,
                full[st].at[:, :, own_rows(c), :],
                rs.at[st, c, k],
                rr.at[st, c, k],
                (aux, p),
            )
            for k, p in enumerate(row_peers)
        ]

    def place(st, c, a, part, x):
        b = x.astype(jnp.bfloat16)
        held[st][c][line * n_aux + a, part] = b
        full[st][a, part, own_rows(c), :] = b

    link_copies = [
        send(link_ref, links[k], ls.at[k - 1], lr.at[k - 1], (p, row))
        for k, p in enumerate(line_peers, 1)
    ]
    for f in fetched:
        f.wait()
    for c in range(CHUNKS):

        @pl.loop(0, n_aux, unroll=8)
        def _(a, c=c):
            for part, ref in enumerate((real_ref, imag_ref)):
                place(0, c, a, part, ref[a, c * rows : (c + 1) * rows, :])

        share(0, c)

    ham = ham_ref[...]
    energy_ref[...] = 0.5 * (ham + ham.T)
    energy = energy_ref[...]
    e_hi = energy.astype(jnp.bfloat16)
    e_right[:, :width] = e_hi
    e_right[:, width:] = (energy - e_hi.astype(jnp.float32)).astype(jnp.bfloat16)
    mine = energy_ref[pl.ds(pl.multiple_of(row * rows_dev, rows_dev), rows_dev), :]
    m_hi = mine.astype(jnp.bfloat16)
    e_left[:rows_dev] = m_hi
    e_left[rows_dev:] = (mine - m_hi.astype(jnp.float32)).astype(jnp.bfloat16)
    run[0] = jnp.zeros(run.shape[1:], jnp.float32)

    turned[...] = mode_ref[...].T
    links[0][...] = link_ref[...]
    for d in link_copies:
        d.wait_recv()
    lanes = link_ref.shape[1]
    i32 = jnp.int32
    lane = lax.broadcasted_iota(i32, (1, lanes), 1)
    diagonal = lax.broadcasted_iota(i32, (lanes, lanes), 0) == lax.broadcasted_iota(
        i32, (lanes, lanes), 1
    )
    far = 1 << 20
    keys_row, modes_row, weights_row, source_row, keys_col = [], [], [], [], []
    for k in range(lines):
        from_line = lax.rem(line - k + lines, lines)
        target = links[k][0:1, :]
        dest = target // n_aux
        chosen = (dest // 2 == line) & (lane < count)
        group = jnp.where(lax.rem(dest, 2) == side, 1, 0)
        key = group * n_aux + lax.rem(target, n_aux)
        place_in = from_line * lanes + lane
        key = jnp.where(chosen, key * (lines * lanes) + place_in, far)
        keys_row.append(key)
        modes_row.append(links[k][1:2, :])
        weights_row.append(links[k][2:3, :])
        source_row.append(from_line * n_aux + lane // links_per)
        keys_col.append(jnp.sum(jnp.where(diagonal, key, 0), axis=1, keepdims=True))
    span = lines * lanes
    key = jnp.concatenate(keys_row, axis=1)
    column = jnp.concatenate(keys_col, axis=0)
    chosen = key < far
    before = column < key
    rank = jnp.sum(jnp.where(before, 1, 0), axis=0, keepdims=True)
    again = jnp.sum(jnp.where(before & (column // span == key // span), 1, 0), axis=0, keepdims=True)
    second = n_aux * span
    first_count = jnp.sum(jnp.where(key < second, 1, 0), axis=1, keepdims=True)
    ranked = jnp.where(key < second, rank, rank - first_count)
    slot = jnp.where(key < second, ranked, ranked + half)
    slot = jnp.where(chosen & (ranked < half), slot, -1)
    pick = lax.broadcasted_iota(i32, (2 * half, span), 0) == slot

    def picked(values):
        return jnp.sum(jnp.where(pick, values, 0), axis=1, keepdims=True)

    at = lax.broadcasted_iota(i32, (2 * half, 128), 1)
    table = jnp.where(at == 0, picked(jnp.concatenate(source_row, axis=1)), 0)
    table = jnp.where(at == 1, picked(jnp.concatenate(modes_row, axis=1)), table)
    table = jnp.where(at == 2, picked(jnp.concatenate(weights_row, axis=1)), table)
    table = jnp.where(at == 3, picked(jnp.where(again > 0, 1, 0)), table)
    table = jnp.where(at == 4, picked(jnp.ones_like(key)), table)
    lists[: 2 * half] = table
    wanted = lax.broadcasted_iota(i32, (2 * n_aux, span), 0)
    upto = jnp.sum(jnp.where(key < (wanted + 1) * span, 1, 0), axis=1, keepdims=True)
    here = jnp.sum(jnp.where(key // span == wanted, 1, 0), axis=1, keepdims=True)
    tall = lax.broadcasted_iota(i32, (2 * n_aux, 1), 0)
    upto = jnp.minimum(jnp.where(tall < n_aux, upto, upto - first_count), half)
    lists[2 * half :] = jnp.broadcast_to(jnp.where(here > 0, upto, 0), (2 * n_aux, 128))
    planned = pltpu.make_async_copy(lists, plan, ins.at[2])
    planned.start()
    hop_relay(0, 0, 1)
    planned.wait()

    mode_lane = lax.broadcasted_iota(i32, (rows_dev, mode_ref.shape[0]), 1)

    @pl.loop(0, 2 * half, unroll=8)
    def _(e):
        m = plan[e, 1]
        w = plan[e, 2]
        scaled = w.astype(jnp.float32)
        plus = scaled * coef_ref[1, m]
        minus = jnp.where(w == 0, plan[e, 4].astype(jnp.float32), scaled * coef_ref[0, m])
        across = mode_ref[pl.ds(m, 1), :]
        mine = turned[pl.ds(pl.multiple_of(row * rows_dev, rows_dev), rows_dev), :]
        down = jnp.sum(jnp.where(mode_lane == m, mine, 0.0), axis=1, keepdims=True)
        facr_ref[e] = plus * (down + across)
        faci_ref[e] = -minus * (down - across)

    def gather_sum(st, c, group):
        cut = slice(c * rows, (c + 1) * rows)

        def body(e, acc):
            ar, ai = acc
            i = group * half + e
            s = plan[i, 0]
            keep = plan[i, 3].astype(jnp.float32)
            xr = held[st][c][s, 0].astype(jnp.float32)
            xi = held[st][c][s, 1].astype(jnp.float32)
            fr = facr_ref[i, cut, :]
            fi = faci_ref[i, cut, :]
            ar = keep * ar + (fr * xr - fi * xi)
            ai = keep * ai + (fr * xi + fi * xr)
            run[e + 1, 0] = ar
            run[e + 1, 1] = ai
            return ar, ai

        zero = jnp.zeros((rows, width), jnp.float32)
        lax.fori_loop(0, half, body, (zero, zero), unroll=12)

    steps = [(st, c) for st in range(STAGES) for c in range(CHUNKS)]
    for n, (st, c) in enumerate(steps):
        cut = slice(c * rows, (c + 1) * rows)
        if lines > 2:
            hop_relay(st, c, 2)
        own = pl.ds(pl.multiple_of(line * n_aux, n_aux), n_aux)
        flat = held[st][c][own].reshape(n_aux * 2 * rows, width)
        both = jnp.dot(flat, e_right[...], preferred_element_type=jnp.float32)
        right[...] = (both[:, :width] + both[:, width:]).reshape(n_aux, 2, rows, width)
        for hop in range(3, lines):
            hop_relay(st, c, hop)

        gather_sum(st, c, 0)

        @pl.loop(0, n_aux, unroll=8)
        def _(a, st=st, c=c):
            give[st][c][a] = run[plan[2 * half + a, 0]].astype(jnp.bfloat16)

        across = send(give[st][c], take[st][c], ys.at[st, c], yr.at[st, c], (beside, row))
        gather_sum(st, c, 1)
        if n + 1 < len(steps):
            hop_relay(*steps[n + 1], 1)
        if c == 0:
            for cc in range(CHUNKS):
                for d in row_copies[st, cc]:
                    d.wait_recv()

            @pl.loop(0, n_aux, unroll=8)
            def _(a, st=st):
                for part in range(2):
                    both = jnp.dot(
                        e_left[...], full[st][a, part], preferred_element_type=jnp.float32
                    )
                    left[a, part] = both[:rows_dev] + both[rows_dev:]

        across.wait_recv()

        weight = step_size / 6.0 * (1.0 if st in (0, STAGES - 1) else 2.0)
        ahead = step_size if st == STAGES - 2 else 0.5 * step_size

        @pl.loop(0, n_aux, unroll=8)
        def _(a, st=st, c=c, cut=cut, weight=weight, ahead=ahead):
            came = run[plan[2 * half + n_aux + a, 0]] + take[st][c][a].astype(jnp.float32)
            prod_r = left[a, 0, cut, :] - right[a, 0]
            prod_i = left[a, 1, cut, :] - right[a, 1]
            rate = rate_ref[a]
            base_r = real_ref[a, cut, :]
            base_i = imag_ref[a, cut, :]
            now_r = base_r if st == 0 else now[a, 0, cut, :]
            now_i = base_i if st == 0 else now[a, 1, cut, :]
            k_r = prod_i - rate * now_r + came[0]
            k_i = came[1] - prod_r - rate * now_i
            tot_r = (base_r if st == 0 else total[a, 0, cut, :]) + weight * k_r
            tot_i = (base_i if st == 0 else total[a, 1, cut, :]) + weight * k_i
            if st == STAGES - 1:
                outr_ref[a, cut, :] = tot_r
                outi_ref[a, cut, :] = tot_i
            else:
                total[a, 0, cut, :] = tot_r
                total[a, 1, cut, :] = tot_i
                next_r = base_r + ahead * k_r
                next_i = base_i + ahead * k_i
                now[a, 0, cut, :] = next_r
                now[a, 1, cut, :] = next_i
                place(st + 1, c, a, 0, next_r)
                place(st + 1, c, a, 1, next_i)

        if st < STAGES - 1:
            share(st + 1, c)

    for d in copies:
        d.wait_send()
    for st, c in steps:
        for hop in range(1, lines):
            for way in range(2):

                @pl.when(hop_sends(hop, way))
                def _(st=st, c=c, hop=hop, way=way):
                    at = line - (hop - 1) if way == 0 else line + (hop - 1)
                    hop_copy(st, c, hop, way, at).wait_send()


def by_states(rho_real, rho_imag, hamiltonian, damping, couplings, mode_vector, mode_coef):
    n_aux, rows_dev, width = rho_real.shape
    per_aux = couplings.shape[2]
    devices = lax.axis_size("aux")
    row_devs = lax.axis_size("row")
    lines = devices // 2
    slots = max(1, -(-n_aux * per_aux // devices))
    half = lines * slots
    smem = pl.BlockSpec(memory_space=pltpu.SMEM)
    vmem = pl.BlockSpec(memory_space=pltpu.VMEM)
    anywhere = pl.BlockSpec(memory_space=pl.ANY)
    dma = pltpu.SemaphoreType.DMA
    count = n_aux * per_aux
    lanes = -(-count // 128) * 128
    packed = couplings.transpose(1, 0, 2).reshape(3, count)
    packed = jnp.pad(packed, ((0, 5), (0, lanes - count)))

    rows = rows_dev // CHUNKS
    bf16, f32 = jnp.bfloat16, jnp.float32
    piece = pltpu.VMEM((n_aux, 2, rows, width), bf16)
    grid = (STAGES, CHUNKS)
    scratch = (
        [pltpu.VMEM((lines * n_aux, 2, rows, width), bf16)] * (STAGES * CHUNKS)
        + [pltpu.VMEM((n_aux, 2, row_devs * rows_dev, width), bf16)] * STAGES
        + [piece] * (2 * STAGES * CHUNKS)
        + [
            pltpu.VMEM((n_aux, rows_dev, width), f32),
            pltpu.VMEM((n_aux, rows_dev, width), f32),
            pltpu.VMEM((width, width), f32),
            pltpu.VMEM((2 * half, rows_dev, width), f32),
            pltpu.VMEM((2 * half, rows_dev, width), f32),
            pltpu.VMEM((width, mode_vector.shape[0]), f32),
            pltpu.VMEM((2 * half + 2 * n_aux, 128), jnp.int32),
            pltpu.SMEM((2 * half + 2 * n_aux, 128), jnp.int32),
        ]
        + [pltpu.VMEM((8, lanes), jnp.int32)] * lines
        + [
            pltpu.VMEM((half + 1, 2, rows, width), f32),
            pltpu.VMEM((n_aux, 2, rows_dev, width), f32),
            pltpu.VMEM((n_aux, 2, rows_dev, width), f32),
            pltpu.VMEM((n_aux, 2, rows_dev, width), f32),
            pltpu.VMEM((n_aux, 2, rows, width), f32),
            pltpu.VMEM((2 * rows_dev, width), bf16),
            pltpu.VMEM((width, 2 * width), bf16),
            dma(grid + (2, lines - 1)),
            dma(grid + (2, lines - 1)),
            dma(grid + (row_devs - 1,)),
            dma(grid + (row_devs - 1,)),
            dma(grid),
            dma(grid),
            dma((lines - 1,)),
            dma((lines - 1,)),
            dma((3,)),
        ]
    )
    shape = jax.ShapeDtypeStruct((n_aux, rows_dev, width), f32)
    return pl.pallas_call(
        functools.partial(kernel, lines, row_devs, half, count, per_aux),
        out_shape=(shape, shape),
        in_specs=[smem] * 2 + [anywhere] * 2 + [vmem] * 3,
        out_specs=(vmem, vmem),
        scratch_shapes=scratch,
        compiler_params=pltpu.CompilerParams(
            collective_id=0, has_side_effects=True, vmem_limit_bytes=60 * 1024 * 1024
        ),
    )(damping, mode_coef, rho_real, rho_imag, hamiltonian, mode_vector, packed)


def solution(mesh):
    placed = (
        P("aux", "row", None),
        P("aux", "row", None),
        P(),
        P("aux"),
        P("aux", None, None),
        P(),
        P(),
    )

    def shards(rho_real, rho_imag, hamiltonian, damping, couplings, mode_vector, mode_coef):
        args = (rho_real, rho_imag, hamiltonian, damping, couplings, mode_vector, mode_coef)
        devices = mesh.shape["aux"]
        n_aux, rows_dev, _ = rho_real.shape
        slots = max(1, -(-n_aux * couplings.shape[2] // devices))
        terms_sent = (devices - 1) * slots
        states_sent = devices // 2 * n_aux
        even = devices % 2 == 0 and devices > 2 and mesh.shape["row"] > 1
        if even and states_sent < terms_sent and rows_dev % (16 * CHUNKS) == 0:
            return by_states(*args)
        return by_terms(*args)

    return jax.shard_map(
        shards,
        mesh=mesh,
        in_specs=placed,
        out_specs=(P("aux", "row", None), P("aux", "row", None)),
        check_vma=False,
    )
```

```python
import functools

import jax
import jax.numpy as jnp
from jax import lax
from jax.experimental import pallas as pl
from jax.experimental.pallas import tpu as pltpu
from jax.sharding import PartitionSpec as P

step_size = 0.1
high = lax.Precision.HIGHEST
MESH = pl.DeviceIdType.MESH
CHUNKS = 4
STAGES = 4


def as_sent(x):
    return jax.tree.map(lambda a: a.astype(jnp.bfloat16) if a.dtype == jnp.float32 else a, x)


def by_terms(rho_real, rho_imag, hamiltonian, damping, couplings, mode_vector, mode_coef):
    energy = 0.5 * (hamiltonian + hamiltonian.T)
    width = energy.shape[0]
    local_aux, rows_dev, _ = rho_real.shape
    per_aux = couplings.shape[2]
    row_index = lax.axis_index("row")
    energy_rows = lax.dynamic_slice_in_dim(energy, row_index * rows_dev, rows_dev, 0)
    devices = lax.axis_size("aux")
    count = local_aux * per_aux
    slots = max(1, -(-count // devices))
    targets = couplings[:, 0, :].reshape(count)
    modes = couplings[:, 1, :].reshape(count)
    weights = couplings[:, 2, :].reshape(count)
    dest = targets // local_aux
    local_target = targets % local_aux
    order = jnp.arange(count)
    same_dest = (dest[:, None] == dest[None, :]) & (order[None, :] < order[:, None])
    ranked = jnp.sum(same_dest.astype(jnp.int32), axis=1)
    slot_of = dest * slots + ranked
    picker = (modes[:, None] == jnp.arange(mode_vector.shape[0])[None, :]).astype(jnp.float32)
    vectors = jnp.dot(picker, mode_vector, precision=high, preferred_element_type=jnp.float32)
    coefs = jnp.dot(picker, mode_coef.T, precision=high, preferred_element_type=jnp.float32)
    scaled = weights.astype(jnp.float32)
    plus = scaled * coefs[:, 1]
    minus = jnp.where(weights == 0, 1.0, scaled * coefs[:, 0])
    row_vec = lax.dynamic_slice_in_dim(vectors, row_index * rows_dev, rows_dev, 1)
    summed = row_vec[:, :, None] + vectors[:, None, :]
    differ = row_vec[:, :, None] - vectors[:, None, :]
    fac_real = (plus[:, None, None] * summed).reshape(local_aux, per_aux, rows_dev, width)
    fac_imag = (-(minus[:, None, None] * differ)).reshape(local_aux, per_aux, rows_dev, width)
    marks = jnp.zeros((devices * slots, local_aux), jnp.bfloat16).at[slot_of, local_target].set(1.0)
    rate = damping[:, None, None]

    def derivative(real_part, imag_part):
        zeros_block = jnp.zeros_like(real_part)
        left_real = zeros_block + jnp.einsum(
            "ij,ajk->aik",
            energy_rows,
            lax.all_gather(as_sent(real_part), "row", axis=1, tiled=True),
            precision=high,
        )
        left_imag = zeros_block + jnp.einsum(
            "ij,ajk->aik",
            energy_rows,
            lax.all_gather(as_sent(imag_part), "row", axis=1, tiled=True),
            precision=high,
        )
        prod_real = left_real - jnp.einsum("aij,jk->aik", real_part, energy, precision=high)
        prod_imag = left_imag - jnp.einsum("aij,jk->aik", imag_part, energy, precision=high)
        source_real = real_part[:, None]
        source_imag = imag_part[:, None]
        term_real = (
            (fac_real * source_real - fac_imag * source_imag)
            .astype(jnp.bfloat16)
            .reshape(count, rows_dev, width)
        )
        term_imag = (
            (fac_real * source_imag + fac_imag * source_real)
            .astype(jnp.bfloat16)
            .reshape(count, rows_dev, width)
        )
        send_real = (
            jnp.zeros((devices * slots, rows_dev, width), jnp.bfloat16).at[slot_of].set(term_real)
        )
        send_imag = (
            jnp.zeros((devices * slots, rows_dev, width), jnp.bfloat16).at[slot_of].set(term_imag)
        )
        got_real, got_imag, got_marks = (
            lax.all_to_all(send_real, "aux", split_axis=0, concat_axis=0, tiled=True),
            lax.all_to_all(send_imag, "aux", split_axis=0, concat_axis=0, tiled=True),
            lax.all_to_all(marks, "aux", split_axis=0, concat_axis=0, tiled=True),
        )
        incoming_real = jnp.einsum(
            "sa,srp->arp", got_marks, got_real, preferred_element_type=jnp.float32
        )
        incoming_imag = jnp.einsum(
            "sa,srp->arp", got_marks, got_imag, preferred_element_type=jnp.float32
        )
        out_real = prod_imag - rate * real_part + incoming_real
        out_imag = -prod_real - rate * imag_part + incoming_imag
        return (out_real, out_imag)

    state_real, state_imag = (rho_real, rho_imag)
    one_real, one_imag = derivative(state_real, state_imag)
    two_real, two_imag = derivative(
        state_real + 0.5 * step_size * one_real, state_imag + 0.5 * step_size * one_imag
    )
    three_real, three_imag = derivative(
        state_real + 0.5 * step_size * two_real, state_imag + 0.5 * step_size * two_imag
    )
    four_real, four_imag = derivative(
        state_real + step_size * three_real, state_imag + step_size * three_imag
    )
    state_real = state_real + step_size / 6.0 * (
        one_real + 2.0 * two_real + 2.0 * three_real + four_real
    )
    state_imag = state_imag + step_size / 6.0 * (
        one_imag + 2.0 * two_imag + 2.0 * three_imag + four_imag
    )
    return (state_real, state_imag)


def kernel(
    lines,
    row_devs,
    half,
    count,
    links_per,
    rate_ref,
    coef_ref,
    real_in,
    imag_in,
    ham_ref,
    mode_ref,
    link_ref,
    outr_ref,
    outi_ref,
    *scratch,
):
    n_aux, rows_dev, width = outr_ref.shape
    rows = rows_dev // CHUNKS
    pair = 2 * rows
    scratch = list(scratch)
    held = [[scratch.pop(0) for _ in range(CHUNKS)] for _ in range(STAGES)]
    full = [scratch.pop(0) for _ in range(STAGES)]
    give = [[scratch.pop(0) for _ in range(CHUNKS)] for _ in range(STAGES)]
    take = [[scratch.pop(0) for _ in range(CHUNKS)] for _ in range(STAGES)]
    real_ref, imag_ref, energy_ref, facr_ref, faci_ref, turned, lists, plan = scratch[:8]
    links = scratch[8 : 8 + lines]
    run, now, total, left, right, e_left, e_right = scratch[8 + lines : 15 + lines]
    zs, zr, rs, rr, ys, yr, ls, lr, ins = scratch[15 + lines :]

    fetched = [
        pltpu.make_async_copy(real_in, real_ref, ins.at[0]),
        pltpu.make_async_copy(imag_in, imag_ref, ins.at[1]),
    ]
    for f in fetched:
        f.start()

    aux = lax.axis_index("aux")
    row = lax.axis_index("row")
    line = aux // 2
    side = lax.rem(aux, 2)
    beside = aux + 1 - 2 * side
    row_peers = [lax.rem(row + k, row_devs) for k in range(1, row_devs)]
    last_line = lines - 1

    barrier = pltpu.get_barrier_semaphore()

    line_peers = [lax.rem(aux + 2 * k, 2 * lines) for k in range(1, lines)]
    peers = [(p, row) for p in line_peers + [beside]] + [(aux, p) for p in row_peers]
    for p in peers:
        pl.semaphore_signal(barrier, inc=1, device_id=p, device_id_type=MESH)
    pl.semaphore_wait(barrier, len(peers))

    copies = []

    def send(src, dst, s_sem, r_sem, device):
        c = pltpu.make_async_remote_copy(
            src_ref=src,
            dst_ref=dst,
            send_sem=s_sem,
            recv_sem=r_sem,
            device_id=device,
            device_id_type=MESH,
        )
        c.start()
        copies.append(c)
        return c

    row_copies = {}

    def own_rows(c):
        return pl.ds(pl.multiple_of((row * CHUNKS + c) * pair, pair), pair)

    def block_at(st, c, at):
        return held[st][c].at[pl.ds(pl.multiple_of(at * n_aux, n_aux), n_aux)]

    def hop_copy(st, c, hop, way, at):
        block = block_at(st, c, at)
        return pltpu.make_async_remote_copy(
            src_ref=block,
            dst_ref=block,
            send_sem=zs.at[st, c, way, hop - 1],
            recv_sem=zr.at[st, c, way, hop - 1],
            device_id=(aux + 2 if way == 0 else aux - 2, row),
            device_id_type=MESH,
        )

    def hop_sends(hop, way):
        if way == 0:
            return (line >= hop - 1) & (line < last_line)
        return (line + hop - 1 <= last_line) & (line > 0)

    def hop_gets(hop, way):
        return line >= hop if way == 0 else line + hop <= last_line

    def hop_send(st, c, hop):
        for way in range(2):

            @pl.when(hop_sends(hop, way))
            def _(way=way):
                at = line - (hop - 1) if way == 0 else line + (hop - 1)
                hop_copy(st, c, hop, way, at).start()

    def hop_get(st, c, hop):
        for way in range(2):

            @pl.when(hop_gets(hop, way))
            def _(way=way):
                at = line - hop if way == 0 else line + hop
                hop_copy(st, c, hop, way, at).wait_recv()

    def hop_relay(st, c, hop):
        hop_get(st, c, hop)
        if hop < lines - 1:
            hop_send(st, c, hop + 1)

    def share(st, c):
        block = block_at(st, c, line)
        hop_send(st, c, 1)
        row_copies[st, c] = [
            send(
                block,
                full[st].at[:, own_rows(c), :],
                rs.at[st, c, k],
                rr.at[st, c, k],
                (aux, p),
            )
            for k, p in enumerate(row_peers)
        ]

    def place(st, c, a, x):
        b = x.astype(jnp.bfloat16)
        held[st][c][line * n_aux + a] = b
        full[st][a, own_rows(c), :] = b

    def base_of(a, cut):
        return jnp.concatenate([real_ref[a, cut, :], imag_ref[a, cut, :]], axis=0)

    link_copies = [
        send(link_ref, links[k], ls.at[k - 1], lr.at[k - 1], (p, row))
        for k, p in enumerate(line_peers, 1)
    ]
    for f in fetched:
        f.wait()
    for c in range(CHUNKS):

        @pl.loop(0, n_aux, unroll=8)
        def _(a, c=c):
            place(0, c, a, base_of(a, slice(c * rows, (c + 1) * rows)))

        share(0, c)

    ham = ham_ref[...]
    energy_ref[...] = 0.5 * (ham + ham.T)
    energy = energy_ref[...]
    e_hi = energy.astype(jnp.bfloat16)
    e_right[:, :width] = e_hi
    e_right[:, width:] = (energy - e_hi.astype(jnp.float32)).astype(jnp.bfloat16)
    i32 = jnp.int32

    def spot(i):
        return i // pair * rows + lax.rem(i, rows)

    def part_of(i):
        return lax.rem(i // rows, 2)

    tall = 2 * rows_dev
    wide = 2 * width
    take_rows = lax.broadcasted_iota(i32, (tall, width), 1) == row * rows_dev + spot(
        lax.broadcasted_iota(i32, (tall, width), 0)
    )
    put_columns = lax.broadcasted_iota(i32, (width, wide), 0) == spot(
        lax.broadcasted_iota(i32, (width, wide), 1)
    )
    same_part = part_of(lax.broadcasted_iota(i32, (tall, wide), 0)) == part_of(
        lax.broadcasted_iota(i32, (tall, wide), 1)
    )
    ones_rows = jnp.where(take_rows, 1.0, 0.0).astype(jnp.bfloat16)
    ones_columns = jnp.where(put_columns, 1.0, 0.0).astype(jnp.bfloat16)
    for k in range(2):
        piece = e_right[:, k * width : (k + 1) * width]
        mine = jnp.dot(ones_rows, piece, preferred_element_type=jnp.float32)
        spread = jnp.dot(
            mine.astype(jnp.bfloat16), ones_columns, preferred_element_type=jnp.float32
        )
        e_left[k * tall : (k + 1) * tall] = jnp.where(same_part, spread, 0.0).astype(jnp.bfloat16)
    run[0] = jnp.zeros(run.shape[1:], jnp.float32)

    turned[...] = mode_ref[...].T
    links[0][...] = link_ref[...]
    for d in link_copies:
        d.wait_recv()
    lanes = link_ref.shape[1]
    lane = lax.broadcasted_iota(i32, (1, lanes), 1)
    diagonal = lax.broadcasted_iota(i32, (lanes, lanes), 0) == lax.broadcasted_iota(
        i32, (lanes, lanes), 1
    )
    far = 1 << 20
    keys_row, modes_row, weights_row, source_row, keys_col = [], [], [], [], []
    for k in range(lines):
        from_line = lax.rem(line - k + lines, lines)
        target = links[k][0:1, :]
        dest = target // n_aux
        chosen = (dest // 2 == line) & (lane < count)
        group = jnp.where(lax.rem(dest, 2) == side, 1, 0)
        key = group * n_aux + lax.rem(target, n_aux)
        place_in = from_line * lanes + lane
        key = jnp.where(chosen, key * (lines * lanes) + place_in, far)
        keys_row.append(key)
        modes_row.append(links[k][1:2, :])
        weights_row.append(links[k][2:3, :])
        source_row.append(from_line * n_aux + lane // links_per)
        keys_col.append(jnp.sum(jnp.where(diagonal, key, 0), axis=1, keepdims=True))
    span = lines * lanes
    key = jnp.concatenate(keys_row, axis=1)
    column = jnp.concatenate(keys_col, axis=0)
    chosen = key < far
    before = column < key
    rank = jnp.sum(jnp.where(before, 1, 0), axis=0, keepdims=True)
    again = jnp.sum(jnp.where(before & (column // span == key // span), 1, 0), axis=0, keepdims=True)
    second = n_aux * span
    first_count = jnp.sum(jnp.where(key < second, 1, 0), axis=1, keepdims=True)
    ranked = jnp.where(key < second, rank, rank - first_count)
    slot = jnp.where(key < second, ranked, ranked + half)
    slot = jnp.where(chosen & (ranked < half), slot, -1)
    pick = lax.broadcasted_iota(i32, (2 * half, span), 0) == slot

    def picked(values):
        return jnp.sum(jnp.where(pick, values, 0), axis=1, keepdims=True)

    at = lax.broadcasted_iota(i32, (2 * half, 128), 1)
    table = jnp.where(at == 0, picked(jnp.concatenate(source_row, axis=1)), 0)
    table = jnp.where(at == 1, picked(jnp.concatenate(modes_row, axis=1)), table)
    table = jnp.where(at == 2, picked(jnp.concatenate(weights_row, axis=1)), table)
    table = jnp.where(at == 3, picked(jnp.where(again > 0, 1, 0)), table)
    table = jnp.where(at == 4, picked(jnp.ones_like(key)), table)
    lists[: 2 * half] = table
    wanted = lax.broadcasted_iota(i32, (2 * n_aux, span), 0)
    upto = jnp.sum(jnp.where(key < (wanted + 1) * span, 1, 0), axis=1, keepdims=True)
    here = jnp.sum(jnp.where(key // span == wanted, 1, 0), axis=1, keepdims=True)
    which = lax.broadcasted_iota(i32, (2 * n_aux, 1), 0)
    upto = jnp.minimum(jnp.where(which < n_aux, upto, upto - first_count), half)
    lists[2 * half :] = jnp.broadcast_to(jnp.where(here > 0, upto, 0), (2 * n_aux, 128))
    planned = pltpu.make_async_copy(lists, plan, ins.at[2])
    planned.start()
    steps = [(st, c) for st in range(STAGES) for c in range(CHUNKS)]
    hop_relay(*steps[0], 1)
    hop_relay(*steps[1], 1)
    planned.wait()

    mode_lane = lax.broadcasted_iota(i32, (rows_dev, mode_ref.shape[0]), 1)

    @pl.loop(0, 2 * half, unroll=8)
    def _(e):
        m = plan[e, 1]
        w = plan[e, 2]
        scaled = w.astype(jnp.float32)
        plus = scaled * coef_ref[1, m]
        minus = jnp.where(w == 0, plan[e, 4].astype(jnp.float32), scaled * coef_ref[0, m])
        across = mode_ref[pl.ds(m, 1), :]
        mine = turned[pl.ds(pl.multiple_of(row * rows_dev, rows_dev), rows_dev), :]
        down = jnp.sum(jnp.where(mode_lane == m, mine, 0.0), axis=1, keepdims=True)
        facr_ref[e] = plus * (down + across)
        faci_ref[e] = -minus * (down - across)

    def gather_sum(st, c, group):
        cut = slice(c * rows, (c + 1) * rows)

        def body(e, acc):
            ar, ai = acc
            i = group * half + e
            s = plan[i, 0]
            keep = plan[i, 3].astype(jnp.float32)
            x = held[st][c][s].astype(jnp.float32)
            xr, xi = x[:rows], x[rows:]
            fr = facr_ref[i, cut, :]
            fi = faci_ref[i, cut, :]
            ar = keep * ar + (fr * xr - fi * xi)
            ai = keep * ai + (fr * xi + fi * xr)
            run[e + 1, :rows] = ar
            run[e + 1, rows:] = ai
            return ar, ai

        zero = jnp.zeros((rows, width), jnp.float32)
        lax.fori_loop(0, half, body, (zero, zero), unroll=12)

    hop_relay(*steps[0], 2)
    for n, (st, c) in enumerate(steps):
        cut = slice(c * rows, (c + 1) * rows)
        both_cut = slice(c * pair, (c + 1) * pair)
        for hop in range(3, lines):
            hop_relay(st, c, hop)
        gather_sum(st, c, 0)

        @pl.loop(0, n_aux, unroll=8)
        def _(a, st=st, c=c):
            give[st][c][a] = run[plan[2 * half + a, 0]].astype(jnp.bfloat16)

        across = send(give[st][c], take[st][c], ys.at[st, c], yr.at[st, c], (beside, row))
        if n + 1 < len(steps):
            hop_relay(*steps[n + 1], 2)
        if n + 2 < len(steps):
            hop_relay(*steps[n + 2], 1)
        own = pl.ds(pl.multiple_of(line * n_aux, n_aux), n_aux)
        flat = held[st][c][own].reshape(n_aux * pair, width)
        both = jnp.dot(flat, e_right[...], preferred_element_type=jnp.float32)
        right[...] = (both[:, :width] + both[:, width:]).reshape(n_aux, pair, width)
        gather_sum(st, c, 1)
        if c == 0:
            for cc in range(CHUNKS):
                for d in row_copies[st, cc]:
                    d.wait_recv()

            @pl.loop(0, n_aux, unroll=8)
            def _(a, st=st):
                both = jnp.dot(e_left[...], full[st][a], preferred_element_type=jnp.float32)
                left[a] = both[:tall] + both[tall:]

        across.wait_recv()

        weight = step_size / 6.0 * (1.0 if st in (0, STAGES - 1) else 2.0)
        ahead = step_size if st == STAGES - 2 else 0.5 * step_size

        @pl.loop(0, n_aux, unroll=8)
        def _(a, st=st, c=c, cut=cut, both_cut=both_cut, weight=weight, ahead=ahead):
            came = run[plan[2 * half + n_aux + a, 0]] + take[st][c][a].astype(jnp.float32)
            prod = left[a, both_cut, :] - right[a]
            turn = jnp.concatenate([prod[rows:], -prod[:rows]], axis=0)
            base = base_of(a, cut)
            here = base if st == 0 else now[a, both_cut, :]
            slope = turn - rate_ref[a] * here + came
            sums = (base if st == 0 else total[a, both_cut, :]) + weight * slope
            if st == STAGES - 1:
                outr_ref[a, cut, :] = sums[:rows]
                outi_ref[a, cut, :] = sums[rows:]
            else:
                total[a, both_cut, :] = sums
                ahead_x = base + ahead * slope
                now[a, both_cut, :] = ahead_x
                place(st + 1, c, a, ahead_x)

        if st < STAGES - 1:
            share(st + 1, c)

    for d in copies:
        d.wait_send()
    for st, c in steps:
        for hop in range(1, lines):
            for way in range(2):

                @pl.when(hop_sends(hop, way))
                def _(st=st, c=c, hop=hop, way=way):
                    at = line - (hop - 1) if way == 0 else line + (hop - 1)
                    hop_copy(st, c, hop, way, at).wait_send()


def by_states(rho_real, rho_imag, hamiltonian, damping, couplings, mode_vector, mode_coef):
    n_aux, rows_dev, width = rho_real.shape
    per_aux = couplings.shape[2]
    devices = lax.axis_size("aux")
    row_devs = lax.axis_size("row")
    lines = devices // 2
    slots = max(1, -(-n_aux * per_aux // devices))
    half = lines * slots
    smem = pl.BlockSpec(memory_space=pltpu.SMEM)
    vmem = pl.BlockSpec(memory_space=pltpu.VMEM)
    anywhere = pl.BlockSpec(memory_space=pl.ANY)
    dma = pltpu.SemaphoreType.DMA
    count = n_aux * per_aux
    lanes = -(-count // 128) * 128
    packed = couplings.transpose(1, 0, 2).reshape(3, count)
    packed = jnp.pad(packed, ((0, 5), (0, lanes - count)))

    rows = rows_dev // CHUNKS
    bf16, f32 = jnp.bfloat16, jnp.float32
    piece = pltpu.VMEM((n_aux, 2 * rows, width), bf16)
    grid = (STAGES, CHUNKS)
    scratch = (
        [pltpu.VMEM((lines * n_aux, 2 * rows, width), bf16)] * (STAGES * CHUNKS)
        + [pltpu.VMEM((n_aux, 2 * row_devs * rows_dev, width), bf16)] * STAGES
        + [piece] * (2 * STAGES * CHUNKS)
        + [
            pltpu.VMEM((n_aux, rows_dev, width), f32),
            pltpu.VMEM((n_aux, rows_dev, width), f32),
            pltpu.VMEM((width, width), f32),
            pltpu.VMEM((2 * half, rows_dev, width), f32),
            pltpu.VMEM((2 * half, rows_dev, width), f32),
            pltpu.VMEM((width, mode_vector.shape[0]), f32),
            pltpu.VMEM((2 * half + 2 * n_aux, 128), jnp.int32),
            pltpu.SMEM((2 * half + 2 * n_aux, 128), jnp.int32),
        ]
        + [pltpu.VMEM((8, lanes), jnp.int32)] * lines
        + [
            pltpu.VMEM((half + 1, 2 * rows, width), f32),
            pltpu.VMEM((n_aux, 2 * rows_dev, width), f32),
            pltpu.VMEM((n_aux, 2 * rows_dev, width), f32),
            pltpu.VMEM((n_aux, 2 * rows_dev, width), f32),
            pltpu.VMEM((n_aux, 2 * rows, width), f32),
            pltpu.VMEM((4 * rows_dev, 2 * width), bf16),
            pltpu.VMEM((width, 2 * width), bf16),
            dma(grid + (2, lines - 1)),
            dma(grid + (2, lines - 1)),
            dma(grid + (row_devs - 1,)),
            dma(grid + (row_devs - 1,)),
            dma(grid),
            dma(grid),
            dma((lines - 1,)),
            dma((lines - 1,)),
            dma((3,)),
        ]
    )
    shape = jax.ShapeDtypeStruct((n_aux, rows_dev, width), f32)
    return pl.pallas_call(
        functools.partial(kernel, lines, row_devs, half, count, per_aux),
        out_shape=(shape, shape),
        in_specs=[smem] * 2 + [anywhere] * 2 + [vmem] * 3,
        out_specs=(vmem, vmem),
        scratch_shapes=scratch,
        compiler_params=pltpu.CompilerParams(
            collective_id=0, has_side_effects=True, vmem_limit_bytes=60 * 1024 * 1024
        ),
    )(damping, mode_coef, rho_real, rho_imag, hamiltonian, mode_vector, packed)


def solution(mesh):
    placed = (
        P("aux", "row", None),
        P("aux", "row", None),
        P(),
        P("aux"),
        P("aux", None, None),
        P(),
        P(),
    )

    def shards(rho_real, rho_imag, hamiltonian, damping, couplings, mode_vector, mode_coef):
        args = (rho_real, rho_imag, hamiltonian, damping, couplings, mode_vector, mode_coef)
        devices = mesh.shape["aux"]
        n_aux, rows_dev, _ = rho_real.shape
        slots = max(1, -(-n_aux * couplings.shape[2] // devices))
        terms_sent = (devices - 1) * slots
        states_sent = devices // 2 * n_aux
        even = devices % 2 == 0 and devices > 4 and mesh.shape["row"] > 1
        if even and states_sent < terms_sent and rows_dev % (8 * CHUNKS) == 0:
            return by_states(*args)
        return by_terms(*args)

    return jax.shard_map(
        shards,
        mesh=mesh,
        in_specs=placed,
        out_specs=(P("aux", "row", None), P("aux", "row", None)),
        check_vma=False,
    )
```

```python
import functools

import jax
import jax.numpy as jnp
from jax import lax
from jax.experimental import pallas as pl
from jax.experimental.pallas import tpu as pltpu
from jax.sharding import PartitionSpec as P

step_size = 0.1
high = lax.Precision.HIGHEST
MESH = pl.DeviceIdType.MESH
CHUNKS = 4
STAGES = 4
GROUPS = 4
LINES = 4


def as_sent(x):
    return jax.tree.map(lambda a: a.astype(jnp.bfloat16) if a.dtype == jnp.float32 else a, x)


def by_terms(rho_real, rho_imag, hamiltonian, damping, couplings, mode_vector, mode_coef):
    energy = 0.5 * (hamiltonian + hamiltonian.T)
    width = energy.shape[0]
    local_aux, rows_dev, _ = rho_real.shape
    per_aux = couplings.shape[2]
    row_index = lax.axis_index("row")
    energy_rows = lax.dynamic_slice_in_dim(energy, row_index * rows_dev, rows_dev, 0)
    devices = lax.axis_size("aux")
    count = local_aux * per_aux
    slots = max(1, -(-count // devices))
    targets = couplings[:, 0, :].reshape(count)
    modes = couplings[:, 1, :].reshape(count)
    weights = couplings[:, 2, :].reshape(count)
    dest = targets // local_aux
    local_target = targets % local_aux
    order = jnp.arange(count)
    same_dest = (dest[:, None] == dest[None, :]) & (order[None, :] < order[:, None])
    ranked = jnp.sum(same_dest.astype(jnp.int32), axis=1)
    slot_of = dest * slots + ranked
    picker = (modes[:, None] == jnp.arange(mode_vector.shape[0])[None, :]).astype(jnp.float32)
    vectors = jnp.dot(picker, mode_vector, precision=high, preferred_element_type=jnp.float32)
    coefs = jnp.dot(picker, mode_coef.T, precision=high, preferred_element_type=jnp.float32)
    scaled = weights.astype(jnp.float32)
    plus = scaled * coefs[:, 1]
    minus = jnp.where(weights == 0, 1.0, scaled * coefs[:, 0])
    row_vec = lax.dynamic_slice_in_dim(vectors, row_index * rows_dev, rows_dev, 1)
    summed = row_vec[:, :, None] + vectors[:, None, :]
    differ = row_vec[:, :, None] - vectors[:, None, :]
    fac_real = (plus[:, None, None] * summed).reshape(local_aux, per_aux, rows_dev, width)
    fac_imag = (-(minus[:, None, None] * differ)).reshape(local_aux, per_aux, rows_dev, width)
    marks = jnp.zeros((devices * slots, local_aux), jnp.bfloat16).at[slot_of, local_target].set(1.0)
    rate = damping[:, None, None]

    def derivative(real_part, imag_part):
        zeros_block = jnp.zeros_like(real_part)
        left_real = zeros_block + jnp.einsum(
            "ij,ajk->aik",
            energy_rows,
            lax.all_gather(as_sent(real_part), "row", axis=1, tiled=True),
            precision=high,
        )
        left_imag = zeros_block + jnp.einsum(
            "ij,ajk->aik",
            energy_rows,
            lax.all_gather(as_sent(imag_part), "row", axis=1, tiled=True),
            precision=high,
        )
        prod_real = left_real - jnp.einsum("aij,jk->aik", real_part, energy, precision=high)
        prod_imag = left_imag - jnp.einsum("aij,jk->aik", imag_part, energy, precision=high)
        source_real = real_part[:, None]
        source_imag = imag_part[:, None]
        term_real = (
            (fac_real * source_real - fac_imag * source_imag)
            .astype(jnp.bfloat16)
            .reshape(count, rows_dev, width)
        )
        term_imag = (
            (fac_real * source_imag + fac_imag * source_real)
            .astype(jnp.bfloat16)
            .reshape(count, rows_dev, width)
        )
        send_real = (
            jnp.zeros((devices * slots, rows_dev, width), jnp.bfloat16).at[slot_of].set(term_real)
        )
        send_imag = (
            jnp.zeros((devices * slots, rows_dev, width), jnp.bfloat16).at[slot_of].set(term_imag)
        )
        got_real, got_imag, got_marks = (
            lax.all_to_all(send_real, "aux", split_axis=0, concat_axis=0, tiled=True),
            lax.all_to_all(send_imag, "aux", split_axis=0, concat_axis=0, tiled=True),
            lax.all_to_all(marks, "aux", split_axis=0, concat_axis=0, tiled=True),
        )
        incoming_real = jnp.einsum(
            "sa,srp->arp", got_marks, got_real, preferred_element_type=jnp.float32
        )
        incoming_imag = jnp.einsum(
            "sa,srp->arp", got_marks, got_imag, preferred_element_type=jnp.float32
        )
        out_real = prod_imag - rate * real_part + incoming_real
        out_imag = -prod_real - rate * imag_part + incoming_imag
        return (out_real, out_imag)

    state_real, state_imag = (rho_real, rho_imag)
    one_real, one_imag = derivative(state_real, state_imag)
    two_real, two_imag = derivative(
        state_real + 0.5 * step_size * one_real, state_imag + 0.5 * step_size * one_imag
    )
    three_real, three_imag = derivative(
        state_real + 0.5 * step_size * two_real, state_imag + 0.5 * step_size * two_imag
    )
    four_real, four_imag = derivative(
        state_real + step_size * three_real, state_imag + step_size * three_imag
    )
    state_real = state_real + step_size / 6.0 * (
        one_real + 2.0 * two_real + 2.0 * three_real + four_real
    )
    state_imag = state_imag + step_size / 6.0 * (
        one_imag + 2.0 * two_imag + 2.0 * three_imag + four_imag
    )
    return (state_real, state_imag)


def kernel(
    lines,
    row_devs,
    half,
    count,
    links_per,
    rate_ref,
    coef_ref,
    real_in,
    imag_in,
    ham_ref,
    mode_ref,
    link_ref,
    outr_ref,
    outi_ref,
    *scratch,
):
    n_aux, rows_dev, width = outr_ref.shape
    rows = rows_dev // CHUNKS
    pair = 2 * rows
    scratch = list(scratch)
    held = [[scratch.pop(0) for _ in range(CHUNKS)] for _ in range(STAGES)]
    full = [scratch.pop(0) for _ in range(STAGES)]
    give = [[scratch.pop(0) for _ in range(CHUNKS)] for _ in range(STAGES)]
    take = [[scratch.pop(0) for _ in range(CHUNKS)] for _ in range(STAGES)]
    fold = [[scratch.pop(0) for _ in range(CHUNKS)] for _ in range(STAGES)]
    land = [[scratch.pop(0) for _ in range(CHUNKS)] for _ in range(STAGES)]
    real_ref, imag_ref, energy_ref, facr_ref, faci_ref, turned, lists, plan = scratch[:8]
    links = scratch[8 : 8 + lines]
    run, run_own, came, now, total, left, right, e_left, e_right = scratch[8 + lines : 17 + lines]
    zs, zr, rs, rr, ys, yr, fs, fr, ls, lr, ins = scratch[17 + lines :]

    fetched = [
        pltpu.make_async_copy(real_in, real_ref, ins.at[0]),
        pltpu.make_async_copy(imag_in, imag_ref, ins.at[1]),
    ]
    for f in fetched:
        f.start()

    aux = lax.axis_index("aux")
    row = lax.axis_index("row")
    line = aux // 2
    side = lax.rem(aux, 2)
    beside = aux + 1 - 2 * side
    row_peers = [lax.rem(row + k, row_devs) for k in range(1, row_devs)]
    last_line = lines - 1
    inner = (line > 0) & (line < last_line)
    at_end = (line == 0) | (line == last_line)
    end_line = jnp.where(line < lines // 2, 0, last_line)
    outward = aux + 2 * (end_line - line)

    barrier = pltpu.get_barrier_semaphore()

    line_peers = [lax.rem(aux + 2 * k, 2 * lines) for k in range(1, lines)]
    peers = [(p, row) for p in line_peers + [beside]] + [(aux, p) for p in row_peers]
    for p in peers:
        pl.semaphore_signal(barrier, inc=1, device_id=p, device_id_type=MESH)
    pl.semaphore_wait(barrier, len(peers))

    copies = []

    def send(src, dst, s_sem, r_sem, device):
        c = pltpu.make_async_remote_copy(
            src_ref=src,
            dst_ref=dst,
            send_sem=s_sem,
            recv_sem=r_sem,
            device_id=device,
            device_id_type=MESH,
        )
        c.start()
        copies.append(c)
        return c

    row_copies = {}

    def across_copy(st, c):
        return pltpu.make_async_remote_copy(
            src_ref=give[st][c],
            dst_ref=take[st][c],
            send_sem=ys.at[st, c],
            recv_sem=yr.at[st, c],
            device_id=(beside, row),
            device_id_type=MESH,
        )

    def fold_copy(st, c):
        return pltpu.make_async_remote_copy(
            src_ref=fold[st][c],
            dst_ref=land[st][c],
            send_sem=fs.at[st, c],
            recv_sem=fr.at[st, c],
            device_id=(outward, row),
            device_id_type=MESH,
        )

    def own_rows(c):
        return pl.ds(pl.multiple_of((row * CHUNKS + c) * pair, pair), pair)

    def block_at(st, c, at):
        return held[st][c].at[pl.ds(pl.multiple_of(at * n_aux, n_aux), n_aux)]

    def hop_copy(st, c, hop, way, at):
        block = block_at(st, c, at)
        return pltpu.make_async_remote_copy(
            src_ref=block,
            dst_ref=block,
            send_sem=zs.at[st, c, way, hop - 1],
            recv_sem=zr.at[st, c, way, hop - 1],
            device_id=(aux + 2 if way == 0 else aux - 2, row),
            device_id_type=MESH,
        )

    def hop_sends(hop, way):
        if way == 0:
            return (line >= hop - 1) & (line < last_line - 1)
        return (line + hop - 1 <= last_line) & (line > 1)

    def hop_gets(hop, way):
        if way == 0:
            return (line >= hop) & (line < last_line)
        return (line + hop <= last_line) & (line > 0)

    def hop_send(st, c, hop):
        for way in range(2):

            @pl.when(hop_sends(hop, way))
            def _(way=way):
                at = line - (hop - 1) if way == 0 else line + (hop - 1)
                hop_copy(st, c, hop, way, at).start()

    def hop_get(st, c, hop):
        for way in range(2):

            @pl.when(hop_gets(hop, way))
            def _(way=way):
                at = line - hop if way == 0 else line + hop
                hop_copy(st, c, hop, way, at).wait_recv()

    def hop_relay(st, c, hop):
        hop_get(st, c, hop)
        if hop < lines - 2:
            hop_send(st, c, hop + 1)

    def share(st, c):
        block = block_at(st, c, line)
        hop_send(st, c, 1)
        row_copies[st, c] = [
            send(
                block,
                full[st].at[:, own_rows(c), :],
                rs.at[st, c, k],
                rr.at[st, c, k],
                (aux, p),
            )
            for k, p in enumerate(row_peers)
        ]

    def place(st, c, a, x):
        b = x.astype(jnp.bfloat16)
        held[st][c][line * n_aux + a] = b
        full[st][a, own_rows(c), :] = b

    def base_of(a, cut):
        return jnp.concatenate([real_ref[a, cut, :], imag_ref[a, cut, :]], axis=0)

    link_copies = [
        send(link_ref, links[k], ls.at[k - 1], lr.at[k - 1], (p, row))
        for k, p in enumerate(line_peers, 1)
    ]
    for f in fetched:
        f.wait()
    for c in range(CHUNKS):

        @pl.loop(0, n_aux, unroll=8)
        def _(a, c=c):
            place(0, c, a, base_of(a, slice(c * rows, (c + 1) * rows)))

        share(0, c)

    ham = ham_ref[...]
    energy_ref[...] = 0.5 * (ham + ham.T)
    energy = energy_ref[...]
    e_hi = energy.astype(jnp.bfloat16)
    e_right[:, :width] = e_hi
    e_right[:, width:] = (energy - e_hi.astype(jnp.float32)).astype(jnp.bfloat16)
    i32 = jnp.int32

    def spot(i):
        return i // pair * rows + lax.rem(i, rows)

    def part_of(i):
        return lax.rem(i // rows, 2)

    tall = 2 * rows_dev
    wide = 2 * width
    take_rows = lax.broadcasted_iota(i32, (tall, width), 1) == row * rows_dev + spot(
        lax.broadcasted_iota(i32, (tall, width), 0)
    )
    put_columns = lax.broadcasted_iota(i32, (width, wide), 0) == spot(
        lax.broadcasted_iota(i32, (width, wide), 1)
    )
    same_part = part_of(lax.broadcasted_iota(i32, (tall, wide), 0)) == part_of(
        lax.broadcasted_iota(i32, (tall, wide), 1)
    )
    ones_rows = jnp.where(take_rows, 1.0, 0.0).astype(jnp.bfloat16)
    ones_columns = jnp.where(put_columns, 1.0, 0.0).astype(jnp.bfloat16)
    for k in range(2):
        piece = e_right[:, k * width : (k + 1) * width]
        mine = jnp.dot(ones_rows, piece, preferred_element_type=jnp.float32)
        spread = jnp.dot(
            mine.astype(jnp.bfloat16), ones_columns, preferred_element_type=jnp.float32
        )
        e_left[k * tall : (k + 1) * tall] = jnp.where(same_part, spread, 0.0).astype(jnp.bfloat16)
    run[0] = jnp.zeros(run.shape[1:], jnp.float32)
    run_own[0] = jnp.zeros(run.shape[1:], jnp.float32)

    turned[...] = mode_ref[...].T
    links[0][...] = link_ref[...]
    for d in link_copies:
        d.wait_recv()
    lanes = link_ref.shape[1]
    lane = lax.broadcasted_iota(i32, (1, lanes), 1)
    diagonal = lax.broadcasted_iota(i32, (lanes, lanes), 0) == lax.broadcasted_iota(
        i32, (lanes, lanes), 1
    )
    far = 1 << 20
    keys_row, modes_row, weights_row, source_row, keys_col = [], [], [], [], []
    for k in range(lines):
        from_line = lax.rem(line - k + lines, lines)
        target = links[k][0:1, :]
        dest = target // n_aux
        goes_to = dest // 2
        own_line = jnp.where(inner | (from_line == line), line, -1)
        fold_line = jnp.where(inner & (from_line != end_line), end_line, -1)
        chosen = ((goes_to == own_line) | (goes_to == fold_line)) & (lane < count)
        group = jnp.where(lax.rem(dest, 2) == side, 1, 0) + jnp.where(goes_to == line, 0, 2)
        key = group * n_aux + lax.rem(target, n_aux)
        place_in = from_line * lanes + lane
        key = jnp.where(chosen, key * (lines * lanes) + place_in, far)
        keys_row.append(key)
        modes_row.append(links[k][1:2, :])
        weights_row.append(links[k][2:3, :])
        source_row.append(from_line * n_aux + lane // links_per)
        keys_col.append(jnp.sum(jnp.where(diagonal, key, 0), axis=1, keepdims=True))
    span = lines * lanes
    key = jnp.concatenate(keys_row, axis=1)
    column = jnp.concatenate(keys_col, axis=0)
    chosen = key < far
    before = column < key
    rank = jnp.sum(jnp.where(before, 1, 0), axis=0, keepdims=True)
    again = jnp.sum(jnp.where(before & (column // span == key // span), 1, 0), axis=0, keepdims=True)
    second = n_aux * span
    which = lax.broadcasted_iota(i32, (GROUPS * n_aux, 1), 0)
    ranked, skipped = rank, jnp.zeros_like(which)
    for g in range(GROUPS - 1):
        inside = (key >= g * second) & (key < (g + 1) * second)
        size = jnp.sum(jnp.where(inside, 1, 0), axis=1, keepdims=True)
        ranked = ranked - jnp.where(key >= (g + 1) * second, size, 0)
        skipped = skipped + jnp.where(which >= (g + 1) * n_aux, size, 0)
    slot = key // second * half + ranked
    slot = jnp.where(chosen & (ranked < half), slot, -1)
    pick = lax.broadcasted_iota(i32, (GROUPS * half, span), 0) == slot

    def picked(values):
        return jnp.sum(jnp.where(pick, values, 0), axis=1, keepdims=True)

    at = lax.broadcasted_iota(i32, (GROUPS * half, 128), 1)
    filled = picked(jnp.ones_like(key))
    source = picked(jnp.concatenate(source_row, axis=1)) + (1 - filled) * line * n_aux
    table = jnp.where(at == 0, source, 0)
    table = jnp.where(at == 1, picked(jnp.concatenate(modes_row, axis=1)), table)
    table = jnp.where(at == 2, picked(jnp.concatenate(weights_row, axis=1)), table)
    table = jnp.where(at == 3, picked(jnp.where(again > 0, 1, 0)), table)
    table = jnp.where(at == 4, filled, table)
    lists[: GROUPS * half] = table
    wanted = lax.broadcasted_iota(i32, (GROUPS * n_aux, span), 0)
    upto = jnp.sum(jnp.where(key < (wanted + 1) * span, 1, 0), axis=1, keepdims=True)
    here = jnp.sum(jnp.where(key // span == wanted, 1, 0), axis=1, keepdims=True)
    upto = jnp.minimum(upto - skipped, half)
    lists[GROUPS * half :] = jnp.broadcast_to(
        jnp.where(here > 0, upto, 0), (GROUPS * n_aux, 128)
    )
    planned = pltpu.make_async_copy(lists, plan, ins.at[2])
    planned.start()
    steps = [(st, c) for st in range(STAGES) for c in range(CHUNKS)]
    hop_relay(*steps[0], 1)
    hop_relay(*steps[1], 1)
    planned.wait()

    mode_lane = lax.broadcasted_iota(i32, (rows_dev, mode_ref.shape[0]), 1)

    @pl.loop(0, GROUPS * half, unroll=8)
    def _(e):
        m = plan[e, 1]
        w = plan[e, 2]
        scaled = w.astype(jnp.float32)
        plus = scaled * coef_ref[1, m]
        minus = jnp.where(w == 0, plan[e, 4].astype(jnp.float32), scaled * coef_ref[0, m])
        across = mode_ref[pl.ds(m, 1), :]
        mine = turned[pl.ds(pl.multiple_of(row * rows_dev, rows_dev), rows_dev), :]
        down = jnp.sum(jnp.where(mode_lane == m, mine, 0.0), axis=1, keepdims=True)
        facr_ref[e] = plus * (down + across)
        faci_ref[e] = -minus * (down - across)

    def gather_sum(st, c, group, run):
        cut = slice(c * rows, (c + 1) * rows)

        def body(e, acc):
            ar, ai = acc
            i = group * half + e
            s = plan[i, 0]
            keep = plan[i, 3].astype(jnp.float32)
            x = held[st][c][s].astype(jnp.float32)
            xr, xi = x[:rows], x[rows:]
            fr = facr_ref[i, cut, :]
            fi = faci_ref[i, cut, :]
            ar = keep * ar + (fr * xr - fi * xi)
            ai = keep * ai + (fr * xi + fi * xr)
            run[e + 1, :rows] = ar
            run[e + 1, rows:] = ai
            return ar, ai

        zero = jnp.zeros((rows, width), jnp.float32)
        lax.fori_loop(0, half, body, (zero, zero), unroll=12)

    def last_of(group, a):
        return plan[GROUPS * half + group * n_aux + a, 0]

    def fold_out(st, c):
        hop_get(st, c, 2)

        @pl.when(inner)
        def _():
            for g in range(2):
                gather_sum(st, c, 2 + g, run)

                @pl.loop(0, n_aux, unroll=8)
                def _(a):
                    fold[st][c][g * n_aux + a] = run[last_of(2 + g, a)].astype(jnp.bfloat16)

            fold_copy(st, c).start()

    fold_out(*steps[0])
    for n, (st, c) in enumerate(steps):
        cut = slice(c * rows, (c + 1) * rows)
        both_cut = slice(c * pair, (c + 1) * pair)
        gather_sum(st, c, 0, run)

        @pl.when(inner)
        def _(st=st, c=c):
            @pl.loop(0, n_aux, unroll=8)
            def _(a):
                give[st][c][a] = run[last_of(0, a)].astype(jnp.bfloat16)

            across_copy(st, c).start()

        @pl.when(at_end)
        def _():
            @pl.loop(0, n_aux, unroll=8)
            def _(a):
                came[a] = run[last_of(0, a)]

        if n + 2 < len(steps):
            hop_relay(*steps[n + 2], 1)
        gather_sum(st, c, 1, run_own)
        if n + 1 < len(steps):
            fold_out(*steps[n + 1])

        @pl.when(at_end)
        def _(st=st, c=c):
            fold_copy(st, c).wait_recv()

            @pl.loop(0, n_aux, unroll=8)
            def _(a):
                both_sums = came[a] + land[st][c][a].astype(jnp.float32)
                give[st][c][a] = both_sums.astype(jnp.bfloat16)

            across_copy(st, c).start()

            @pl.loop(0, n_aux, unroll=8)
            def _(a):
                came[a] = run_own[last_of(1, a)] + land[st][c][n_aux + a].astype(jnp.float32)

        @pl.when(inner)
        def _():
            @pl.loop(0, n_aux, unroll=8)
            def _(a):
                came[a] = run_own[last_of(1, a)]

        own = pl.ds(pl.multiple_of(line * n_aux, n_aux), n_aux)
        flat = held[st][c][own].reshape(n_aux * pair, width)
        both = jnp.dot(flat, e_right[...], preferred_element_type=jnp.float32)
        right[...] = (both[:, :width] + both[:, width:]).reshape(n_aux, pair, width)
        if c == 0:
            for cc in range(CHUNKS):
                for d in row_copies[st, cc]:
                    d.wait_recv()

            @pl.loop(0, n_aux, unroll=8)
            def _(a, st=st):
                both = jnp.dot(e_left[...], full[st][a], preferred_element_type=jnp.float32)
                left[a] = both[:tall] + both[tall:]

        across_copy(st, c).wait_recv()

        weight = step_size / 6.0 * (1.0 if st in (0, STAGES - 1) else 2.0)
        ahead = step_size if st == STAGES - 2 else 0.5 * step_size

        @pl.loop(0, n_aux, unroll=8)
        def _(a, st=st, c=c, cut=cut, both_cut=both_cut, weight=weight, ahead=ahead):
            arrived = came[a] + take[st][c][a].astype(jnp.float32)
            prod = left[a, both_cut, :] - right[a]
            turn = jnp.concatenate([prod[rows:], -prod[:rows]], axis=0)
            base = base_of(a, cut)
            here = base if st == 0 else now[a, both_cut, :]
            slope = turn - rate_ref[a] * here + arrived
            sums = (base if st == 0 else total[a, both_cut, :]) + weight * slope
            if st == STAGES - 1:
                outr_ref[a, cut, :] = sums[:rows]
                outi_ref[a, cut, :] = sums[rows:]
            else:
                total[a, both_cut, :] = sums
                ahead_x = base + ahead * slope
                now[a, both_cut, :] = ahead_x
                place(st + 1, c, a, ahead_x)

        if st < STAGES - 1:
            share(st + 1, c)

    for d in copies:
        d.wait_send()
    for st, c in steps:
        across_copy(st, c).wait_send()

        @pl.when(inner)
        def _(st=st, c=c):
            fold_copy(st, c).wait_send()

        for hop in range(1, lines - 1):
            for way in range(2):

                @pl.when(hop_sends(hop, way))
                def _(st=st, c=c, hop=hop, way=way):
                    at = line - (hop - 1) if way == 0 else line + (hop - 1)
                    hop_copy(st, c, hop, way, at).wait_send()


def by_states(rho_real, rho_imag, hamiltonian, damping, couplings, mode_vector, mode_coef):
    n_aux, rows_dev, width = rho_real.shape
    per_aux = couplings.shape[2]
    devices = lax.axis_size("aux")
    row_devs = lax.axis_size("row")
    lines = devices // 2
    slots = max(1, -(-n_aux * per_aux // devices))
    half = lines * slots
    smem = pl.BlockSpec(memory_space=pltpu.SMEM)
    vmem = pl.BlockSpec(memory_space=pltpu.VMEM)
    anywhere = pl.BlockSpec(memory_space=pl.ANY)
    dma = pltpu.SemaphoreType.DMA
    count = n_aux * per_aux
    lanes = -(-count // 128) * 128
    packed = couplings.transpose(1, 0, 2).reshape(3, count)
    packed = jnp.pad(packed, ((0, 5), (0, lanes - count)))

    rows = rows_dev // CHUNKS
    bf16, f32 = jnp.bfloat16, jnp.float32
    piece = pltpu.VMEM((n_aux, 2 * rows, width), bf16)
    grid = (STAGES, CHUNKS)
    scratch = (
        [pltpu.VMEM((lines * n_aux, 2 * rows, width), bf16)] * (STAGES * CHUNKS)
        + [pltpu.VMEM((n_aux, 2 * row_devs * rows_dev, width), bf16)] * STAGES
        + [piece] * (2 * STAGES * CHUNKS)
        + [pltpu.VMEM((2 * n_aux, 2 * rows, width), bf16)] * (2 * STAGES * CHUNKS)
        + [
            pltpu.VMEM((n_aux, rows_dev, width), f32),
            pltpu.VMEM((n_aux, rows_dev, width), f32),
            pltpu.VMEM((width, width), f32),
            pltpu.VMEM((GROUPS * half, rows_dev, width), f32),
            pltpu.VMEM((GROUPS * half, rows_dev, width), f32),
            pltpu.VMEM((width, mode_vector.shape[0]), f32),
            pltpu.VMEM((GROUPS * (half + n_aux), 128), jnp.int32),
            pltpu.SMEM((GROUPS * (half + n_aux), 128), jnp.int32),
        ]
        + [pltpu.VMEM((8, lanes), jnp.int32)] * lines
        + [
            pltpu.VMEM((half + 1, 2 * rows, width), f32),
            pltpu.VMEM((half + 1, 2 * rows, width), f32),
            pltpu.VMEM((n_aux, 2 * rows, width), f32),
            pltpu.VMEM((n_aux, 2 * rows_dev, width), f32),
            pltpu.VMEM((n_aux, 2 * rows_dev, width), f32),
            pltpu.VMEM((n_aux, 2 * rows_dev, width), f32),
            pltpu.VMEM((n_aux, 2 * rows, width), f32),
            pltpu.VMEM((4 * rows_dev, 2 * width), bf16),
            pltpu.VMEM((width, 2 * width), bf16),
            dma(grid + (2, lines - 2)),
            dma(grid + (2, lines - 2)),
            dma(grid + (row_devs - 1,)),
            dma(grid + (row_devs - 1,)),
            dma(grid),
            dma(grid),
            dma(grid),
            dma(grid),
            dma((lines - 1,)),
            dma((lines - 1,)),
            dma((3,)),
        ]
    )
    shape = jax.ShapeDtypeStruct((n_aux, rows_dev, width), f32)
    return pl.pallas_call(
        functools.partial(kernel, lines, row_devs, half, count, per_aux),
        out_shape=(shape, shape),
        in_specs=[smem] * 2 + [anywhere] * 2 + [vmem] * 3,
        out_specs=(vmem, vmem),
        scratch_shapes=scratch,
        compiler_params=pltpu.CompilerParams(
            collective_id=0, has_side_effects=True, vmem_limit_bytes=60 * 1024 * 1024
        ),
    )(damping, mode_coef, rho_real, rho_imag, hamiltonian, mode_vector, packed)


def solution(mesh):
    placed = (
        P("aux", "row", None),
        P("aux", "row", None),
        P(),
        P("aux"),
        P("aux", None, None),
        P(),
        P(),
    )

    def shards(rho_real, rho_imag, hamiltonian, damping, couplings, mode_vector, mode_coef):
        args = (rho_real, rho_imag, hamiltonian, damping, couplings, mode_vector, mode_coef)
        devices = mesh.shape["aux"]
        n_aux, rows_dev, _ = rho_real.shape
        slots = max(1, -(-n_aux * couplings.shape[2] // devices))
        terms_sent = (devices - 1) * slots
        states_sent = devices // 2 * n_aux
        even = devices == 2 * LINES and mesh.shape["row"] > 1
        if even and states_sent < terms_sent and rows_dev % (8 * CHUNKS) == 0:
            return by_states(*args)
        return by_terms(*args)

    return jax.shard_map(
        shards,
        mesh=mesh,
        in_specs=placed,
        out_specs=(P("aux", "row", None), P("aux", "row", None)),
        check_vma=False,
    )
```

```python
import functools

import jax
import jax.numpy as jnp
from jax import lax
from jax.experimental import pallas as pl
from jax.experimental.pallas import tpu as pltpu
from jax.sharding import PartitionSpec as P

step_size = 0.1
high = lax.Precision.HIGHEST
MESH = pl.DeviceIdType.MESH
CHUNKS = 4
STAGES = 4
GROUPS = 4
LINES = 4


def as_sent(x):
    return jax.tree.map(lambda a: a.astype(jnp.bfloat16) if a.dtype == jnp.float32 else a, x)


def by_terms(rho_real, rho_imag, hamiltonian, damping, couplings, mode_vector, mode_coef):
    energy = 0.5 * (hamiltonian + hamiltonian.T)
    width = energy.shape[0]
    local_aux, rows_dev, _ = rho_real.shape
    per_aux = couplings.shape[2]
    row_index = lax.axis_index("row")
    energy_rows = lax.dynamic_slice_in_dim(energy, row_index * rows_dev, rows_dev, 0)
    devices = lax.axis_size("aux")
    count = local_aux * per_aux
    slots = max(1, -(-count // devices))
    targets = couplings[:, 0, :].reshape(count)
    modes = couplings[:, 1, :].reshape(count)
    weights = couplings[:, 2, :].reshape(count)
    dest = targets // local_aux
    local_target = targets % local_aux
    order = jnp.arange(count)
    same_dest = (dest[:, None] == dest[None, :]) & (order[None, :] < order[:, None])
    ranked = jnp.sum(same_dest.astype(jnp.int32), axis=1)
    slot_of = dest * slots + ranked
    picker = (modes[:, None] == jnp.arange(mode_vector.shape[0])[None, :]).astype(jnp.float32)
    vectors = jnp.dot(picker, mode_vector, precision=high, preferred_element_type=jnp.float32)
    coefs = jnp.dot(picker, mode_coef.T, precision=high, preferred_element_type=jnp.float32)
    scaled = weights.astype(jnp.float32)
    plus = scaled * coefs[:, 1]
    minus = jnp.where(weights == 0, 1.0, scaled * coefs[:, 0])
    row_vec = lax.dynamic_slice_in_dim(vectors, row_index * rows_dev, rows_dev, 1)
    summed = row_vec[:, :, None] + vectors[:, None, :]
    differ = row_vec[:, :, None] - vectors[:, None, :]
    fac_real = (plus[:, None, None] * summed).reshape(local_aux, per_aux, rows_dev, width)
    fac_imag = (-(minus[:, None, None] * differ)).reshape(local_aux, per_aux, rows_dev, width)
    marks = jnp.zeros((devices * slots, local_aux), jnp.bfloat16).at[slot_of, local_target].set(1.0)
    rate = damping[:, None, None]

    def derivative(real_part, imag_part):
        zeros_block = jnp.zeros_like(real_part)
        left_real = zeros_block + jnp.einsum(
            "ij,ajk->aik",
            energy_rows,
            lax.all_gather(as_sent(real_part), "row", axis=1, tiled=True),
            precision=high,
        )
        left_imag = zeros_block + jnp.einsum(
            "ij,ajk->aik",
            energy_rows,
            lax.all_gather(as_sent(imag_part), "row", axis=1, tiled=True),
            precision=high,
        )
        prod_real = left_real - jnp.einsum("aij,jk->aik", real_part, energy, precision=high)
        prod_imag = left_imag - jnp.einsum("aij,jk->aik", imag_part, energy, precision=high)
        source_real = real_part[:, None]
        source_imag = imag_part[:, None]
        term_real = (
            (fac_real * source_real - fac_imag * source_imag)
            .astype(jnp.bfloat16)
            .reshape(count, rows_dev, width)
        )
        term_imag = (
            (fac_real * source_imag + fac_imag * source_real)
            .astype(jnp.bfloat16)
            .reshape(count, rows_dev, width)
        )
        send_real = (
            jnp.zeros((devices * slots, rows_dev, width), jnp.bfloat16).at[slot_of].set(term_real)
        )
        send_imag = (
            jnp.zeros((devices * slots, rows_dev, width), jnp.bfloat16).at[slot_of].set(term_imag)
        )
        got_real, got_imag, got_marks = (
            lax.all_to_all(send_real, "aux", split_axis=0, concat_axis=0, tiled=True),
            lax.all_to_all(send_imag, "aux", split_axis=0, concat_axis=0, tiled=True),
            lax.all_to_all(marks, "aux", split_axis=0, concat_axis=0, tiled=True),
        )
        incoming_real = jnp.einsum(
            "sa,srp->arp", got_marks, got_real, preferred_element_type=jnp.float32
        )
        incoming_imag = jnp.einsum(
            "sa,srp->arp", got_marks, got_imag, preferred_element_type=jnp.float32
        )
        out_real = prod_imag - rate * real_part + incoming_real
        out_imag = -prod_real - rate * imag_part + incoming_imag
        return (out_real, out_imag)

    state_real, state_imag = (rho_real, rho_imag)
    one_real, one_imag = derivative(state_real, state_imag)
    two_real, two_imag = derivative(
        state_real + 0.5 * step_size * one_real, state_imag + 0.5 * step_size * one_imag
    )
    three_real, three_imag = derivative(
        state_real + 0.5 * step_size * two_real, state_imag + 0.5 * step_size * two_imag
    )
    four_real, four_imag = derivative(
        state_real + step_size * three_real, state_imag + step_size * three_imag
    )
    state_real = state_real + step_size / 6.0 * (
        one_real + 2.0 * two_real + 2.0 * three_real + four_real
    )
    state_imag = state_imag + step_size / 6.0 * (
        one_imag + 2.0 * two_imag + 2.0 * three_imag + four_imag
    )
    return (state_real, state_imag)


def kernel(
    lines,
    row_devs,
    half,
    count,
    links_per,
    rate_ref,
    coef_ref,
    real_in,
    imag_in,
    ham_ref,
    mode_ref,
    link_ref,
    outr_ref,
    outi_ref,
    *scratch,
):
    n_aux, rows_dev, width = outr_ref.shape
    rows = rows_dev // CHUNKS
    pair = 2 * rows
    scratch = list(scratch)
    held = [[scratch.pop(0) for _ in range(CHUNKS)] for _ in range(STAGES)]
    full = [scratch.pop(0) for _ in range(STAGES)]
    give = [[scratch.pop(0) for _ in range(CHUNKS)] for _ in range(STAGES)]
    take = [[scratch.pop(0) for _ in range(CHUNKS)] for _ in range(STAGES)]
    fold = [[scratch.pop(0) for _ in range(CHUNKS)] for _ in range(STAGES)]
    land = [[scratch.pop(0) for _ in range(CHUNKS)] for _ in range(STAGES)]
    real_ref, imag_ref, energy_ref, facr_ref, faci_ref, turned, lists, plan = scratch[:8]
    links = scratch[8 : 8 + lines]
    run, run_own, came, now, total, left, right, e_left, e_right = scratch[8 + lines : 17 + lines]
    zs, zr, rs, rr, ys, yr, fs, fr, ls, lr, ins = scratch[17 + lines :]

    fetched = [
        pltpu.make_async_copy(real_in, real_ref, ins.at[0]),
        pltpu.make_async_copy(imag_in, imag_ref, ins.at[1]),
    ]
    for f in fetched:
        f.start()

    aux = lax.axis_index("aux")
    row = lax.axis_index("row")
    line = aux // 2
    side = lax.rem(aux, 2)
    beside = aux + 1 - 2 * side
    row_peers = [lax.rem(row + k, row_devs) for k in range(1, row_devs)]
    last_line = lines - 1
    inner = (line > 0) & (line < last_line)
    at_end = (line == 0) | (line == last_line)
    end_line = jnp.where(line < lines // 2, 0, last_line)
    outward = aux + 2 * (end_line - line)

    barrier = pltpu.get_barrier_semaphore()

    line_peers = [lax.rem(aux + 2 * k, 2 * lines) for k in range(1, lines)]
    peers = [(p, row) for p in line_peers + [beside]] + [(aux, p) for p in row_peers]
    for p in peers:
        pl.semaphore_signal(barrier, inc=1, device_id=p, device_id_type=MESH)
    pl.semaphore_wait(barrier, len(peers))

    copies = []

    def send(src, dst, s_sem, r_sem, device):
        c = pltpu.make_async_remote_copy(
            src_ref=src,
            dst_ref=dst,
            send_sem=s_sem,
            recv_sem=r_sem,
            device_id=device,
            device_id_type=MESH,
        )
        c.start()
        copies.append(c)
        return c

    row_copies = {}

    def across_copy(st, c):
        return pltpu.make_async_remote_copy(
            src_ref=give[st][c],
            dst_ref=take[st][c],
            send_sem=ys.at[st, c],
            recv_sem=yr.at[st, c],
            device_id=(beside, row),
            device_id_type=MESH,
        )

    def fold_copy(st, c):
        return pltpu.make_async_remote_copy(
            src_ref=fold[st][c],
            dst_ref=land[st][c],
            send_sem=fs.at[st, c],
            recv_sem=fr.at[st, c],
            device_id=(outward, row),
            device_id_type=MESH,
        )

    def own_rows(c):
        return pl.ds(pl.multiple_of((row * CHUNKS + c) * pair, pair), pair)

    def block_at(st, c, at):
        return held[st][c].at[pl.ds(pl.multiple_of(at * n_aux, n_aux), n_aux)]

    def hop_copy(st, c, hop, way, at):
        block = block_at(st, c, at)
        return pltpu.make_async_remote_copy(
            src_ref=block,
            dst_ref=block,
            send_sem=zs.at[st, c, way, hop - 1],
            recv_sem=zr.at[st, c, way, hop - 1],
            device_id=(aux + 2 if way == 0 else aux - 2, row),
            device_id_type=MESH,
        )

    def hop_sends(hop, way):
        if way == 0:
            return (line >= hop - 1) & (line < last_line - 1)
        return (line + hop - 1 <= last_line) & (line > 1)

    def hop_gets(hop, way):
        if way == 0:
            return (line >= hop) & (line < last_line)
        return (line + hop <= last_line) & (line > 0)

    def hop_send(st, c, hop):
        for way in range(2):

            @pl.when(hop_sends(hop, way))
            def _(way=way):
                at = line - (hop - 1) if way == 0 else line + (hop - 1)
                hop_copy(st, c, hop, way, at).start()

    def hop_get(st, c, hop):
        for way in range(2):

            @pl.when(hop_gets(hop, way))
            def _(way=way):
                at = line - hop if way == 0 else line + hop
                hop_copy(st, c, hop, way, at).wait_recv()

    def hop_relay(st, c, hop):
        hop_get(st, c, hop)
        if hop < lines - 2:
            hop_send(st, c, hop + 1)

    def share(st, c):
        block = block_at(st, c, line)
        hop_send(st, c, 1)
        row_copies[st, c] = [
            send(
                block,
                full[st].at[:, own_rows(c), :],
                rs.at[st, c, k],
                rr.at[st, c, k],
                (aux, p),
            )
            for k, p in enumerate(row_peers)
        ]

    def place(st, c, a, x):
        b = x.astype(jnp.bfloat16)
        held[st][c][line * n_aux + a] = b
        full[st][a, own_rows(c), :] = b

    def base_of(a, cut):
        return jnp.concatenate([real_ref[a, cut, :], imag_ref[a, cut, :]], axis=0)

    link_copies = [
        send(link_ref, links[k], ls.at[k - 1], lr.at[k - 1], (p, row))
        for k, p in enumerate(line_peers, 1)
    ]
    for f in fetched:
        f.wait()
    for c in range(CHUNKS):

        @pl.loop(0, n_aux, unroll=8)
        def _(a, c=c):
            place(0, c, a, base_of(a, slice(c * rows, (c + 1) * rows)))

        share(0, c)

    ham = ham_ref[...]
    energy_ref[...] = 0.5 * (ham + ham.T)
    energy = energy_ref[...]
    e_hi = energy.astype(jnp.bfloat16)
    e_right[:, :width] = e_hi
    e_right[:, width:] = (energy - e_hi.astype(jnp.float32)).astype(jnp.bfloat16)
    i32 = jnp.int32

    def spot(i):
        return i // pair * rows + lax.rem(i, rows)

    def part_of(i):
        return lax.rem(i // rows, 2)

    tall = 2 * rows_dev
    wide = 2 * width
    take_rows = lax.broadcasted_iota(i32, (tall, width), 1) == row * rows_dev + spot(
        lax.broadcasted_iota(i32, (tall, width), 0)
    )
    put_columns = lax.broadcasted_iota(i32, (width, wide), 0) == spot(
        lax.broadcasted_iota(i32, (width, wide), 1)
    )
    same_part = part_of(lax.broadcasted_iota(i32, (tall, wide), 0)) == part_of(
        lax.broadcasted_iota(i32, (tall, wide), 1)
    )
    ones_rows = jnp.where(take_rows, 1.0, 0.0).astype(jnp.bfloat16)
    ones_columns = jnp.where(put_columns, 1.0, 0.0).astype(jnp.bfloat16)
    for k in range(2):
        piece = e_right[:, k * width : (k + 1) * width]
        mine = jnp.dot(ones_rows, piece, preferred_element_type=jnp.float32)
        spread = jnp.dot(
            mine.astype(jnp.bfloat16), ones_columns, preferred_element_type=jnp.float32
        )
        e_left[k * tall : (k + 1) * tall] = jnp.where(same_part, spread, 0.0).astype(jnp.bfloat16)
    run[0] = jnp.zeros(run.shape[1:], jnp.float32)
    run_own[0] = jnp.zeros(run.shape[1:], jnp.float32)

    turned[...] = mode_ref[...].T
    links[0][...] = link_ref[...]
    for d in link_copies:
        d.wait_recv()
    lanes = link_ref.shape[1]
    lane = lax.broadcasted_iota(i32, (1, lanes), 1)
    diagonal = lax.broadcasted_iota(i32, (lanes, lanes), 0) == lax.broadcasted_iota(
        i32, (lanes, lanes), 1
    )
    far = 1 << 20
    keys_row, modes_row, weights_row, source_row, keys_col = [], [], [], [], []
    for k in range(lines):
        from_line = lax.rem(line - k + lines, lines)
        target = links[k][0:1, :]
        dest = target // n_aux
        goes_to = dest // 2
        own_line = jnp.where(inner | (from_line == line), line, -1)
        fold_line = jnp.where(inner & (from_line != end_line), end_line, -1)
        chosen = ((goes_to == own_line) | (goes_to == fold_line)) & (lane < count)
        group = jnp.where(lax.rem(dest, 2) == side, 1, 0) + jnp.where(goes_to == line, 0, 2)
        key = group * n_aux + lax.rem(target, n_aux)
        place_in = from_line * lanes + lane
        key = jnp.where(chosen, key * (lines * lanes) + place_in, far)
        keys_row.append(key)
        modes_row.append(links[k][1:2, :])
        weights_row.append(links[k][2:3, :])
        source_row.append(from_line * n_aux + lane // links_per)
        keys_col.append(jnp.sum(jnp.where(diagonal, key, 0), axis=1, keepdims=True))
    span = lines * lanes
    key = jnp.concatenate(keys_row, axis=1)
    column = jnp.concatenate(keys_col, axis=0)
    chosen = key < far
    before = column < key
    rank = jnp.sum(jnp.where(before, 1, 0), axis=0, keepdims=True)
    again = jnp.sum(jnp.where(before & (column // span == key // span), 1, 0), axis=0, keepdims=True)
    second = n_aux * span
    which = lax.broadcasted_iota(i32, (GROUPS * n_aux, 1), 0)
    ranked, skipped = rank, jnp.zeros_like(which)
    for g in range(GROUPS - 1):
        inside = (key >= g * second) & (key < (g + 1) * second)
        size = jnp.sum(jnp.where(inside, 1, 0), axis=1, keepdims=True)
        ranked = ranked - jnp.where(key >= (g + 1) * second, size, 0)
        skipped = skipped + jnp.where(which >= (g + 1) * n_aux, size, 0)
    slot = key // second * half + ranked
    slot = jnp.where(chosen & (ranked < half), slot, -1)
    pick = lax.broadcasted_iota(i32, (GROUPS * half, span), 0) == slot

    def picked(values):
        return jnp.sum(jnp.where(pick, values, 0), axis=1, keepdims=True)

    at = lax.broadcasted_iota(i32, (GROUPS * half, 128), 1)
    filled = picked(jnp.ones_like(key))
    source = picked(jnp.concatenate(source_row, axis=1)) + (1 - filled) * line * n_aux
    table = jnp.where(at == 0, source, 0)
    table = jnp.where(at == 1, picked(jnp.concatenate(modes_row, axis=1)), table)
    table = jnp.where(at == 2, picked(jnp.concatenate(weights_row, axis=1)), table)
    table = jnp.where(at == 3, picked(jnp.where(again > 0, 1, 0)), table)
    table = jnp.where(at == 4, filled, table)
    lists[: GROUPS * half] = table
    wanted = lax.broadcasted_iota(i32, (GROUPS * n_aux, span), 0)
    upto = jnp.sum(jnp.where(key < (wanted + 1) * span, 1, 0), axis=1, keepdims=True)
    here = jnp.sum(jnp.where(key // span == wanted, 1, 0), axis=1, keepdims=True)
    upto = jnp.minimum(upto - skipped, half)
    lists[GROUPS * half :] = jnp.broadcast_to(
        jnp.where(here > 0, upto, 0), (GROUPS * n_aux, 128)
    )
    planned = pltpu.make_async_copy(lists, plan, ins.at[2])
    planned.start()
    steps = [(st, c) for st in range(STAGES) for c in range(CHUNKS)]
    hop_relay(*steps[0], 1)
    hop_relay(*steps[1], 1)
    planned.wait()

    mode_lane = lax.broadcasted_iota(i32, (rows_dev, mode_ref.shape[0]), 1)

    @pl.loop(0, GROUPS * half, unroll=8)
    def _(e):
        m = plan[e, 1]
        w = plan[e, 2]
        scaled = w.astype(jnp.float32)
        plus = scaled * coef_ref[1, m]
        minus = jnp.where(w == 0, plan[e, 4].astype(jnp.float32), scaled * coef_ref[0, m])
        across = mode_ref[pl.ds(m, 1), :]
        mine = turned[pl.ds(pl.multiple_of(row * rows_dev, rows_dev), rows_dev), :]
        down = jnp.sum(jnp.where(mode_lane == m, mine, 0.0), axis=1, keepdims=True)
        facr_ref[e] = plus * (down + across)
        faci_ref[e] = -minus * (down - across)

    def gather_sum(st, c, group, run, entries):
        cut = slice(c * rows, (c + 1) * rows)

        def body(e, acc):
            ar, ai = acc
            i = group * half + e
            s = plan[i, 0]
            keep = plan[i, 3].astype(jnp.float32)
            x = held[st][c][s].astype(jnp.float32)
            xr, xi = x[:rows], x[rows:]
            fr = facr_ref[i, cut, :]
            fi = faci_ref[i, cut, :]
            ar = keep * ar + (fr * xr - fi * xi)
            ai = keep * ai + (fr * xi + fi * xr)
            run[e + 1, :rows] = ar
            run[e + 1, rows:] = ai
            return ar, ai

        zero = jnp.zeros((rows, width), jnp.float32)
        lax.fori_loop(0, entries, body, (zero, zero), unroll=12)

    def last_of(group, a):
        return plan[GROUPS * half + group * n_aux + a, 0]

    def fold_out(st, c):
        hop_get(st, c, 2)

        @pl.when(inner)
        def _():
            for g in range(2):
                gather_sum(st, c, 2 + g, run, half - half // lines)

                @pl.loop(0, n_aux, unroll=8)
                def _(a):
                    fold[st][c][g * n_aux + a] = run[last_of(2 + g, a)].astype(jnp.bfloat16)

            fold_copy(st, c).start()

    def sums_out(n):
        st, c = steps[n]
        turn = n % 2
        fold_out(st, c)
        gather_sum(st, c, 0, run, half)

        @pl.when(inner)
        def _():
            @pl.loop(0, n_aux, unroll=8)
            def _(a):
                give[st][c][a] = run[last_of(0, a)].astype(jnp.bfloat16)

            across_copy(st, c).start()

        @pl.when(at_end)
        def _():
            @pl.loop(0, n_aux, unroll=8)
            def _(a):
                came[2 + turn, a] = run[last_of(0, a)]

        gather_sum(st, c, 1, run_own, half)

        @pl.loop(0, n_aux, unroll=8)
        def _(a):
            came[turn, a] = run_own[last_of(1, a)]

        own = pl.ds(pl.multiple_of(line * n_aux, n_aux), n_aux)
        flat = held[st][c][own].reshape(n_aux * pair, width)
        both = jnp.dot(flat, e_right[...], preferred_element_type=jnp.float32)
        right[turn] = (both[:, :width] + both[:, width:]).reshape(n_aux, pair, width)

    def end_out(n):
        st, c = steps[n]
        turn = n % 2

        @pl.when(at_end)
        def _():
            fold_copy(st, c).wait_recv()

            @pl.loop(0, n_aux, unroll=8)
            def _(a):
                both_sums = came[2 + turn, a] + land[st][c][a].astype(jnp.float32)
                give[st][c][a] = both_sums.astype(jnp.bfloat16)

            across_copy(st, c).start()

            @pl.loop(0, n_aux, unroll=8)
            def _(a):
                came[turn, a] += land[st][c][n_aux + a].astype(jnp.float32)

    def finish(n):
        st, c = steps[n]
        order = n % 2
        cut = slice(c * rows, (c + 1) * rows)
        both_cut = slice(c * pair, (c + 1) * pair)
        if c == 0:
            for cc in range(CHUNKS):
                for d in row_copies[st, cc]:
                    d.wait_recv()

            @pl.loop(0, n_aux, unroll=8)
            def _(a, st=st):
                both = jnp.dot(e_left[...], full[st][a], preferred_element_type=jnp.float32)
                left[a] = both[:tall] + both[tall:]

        across_copy(st, c).wait_recv()

        weight = step_size / 6.0 * (1.0 if st in (0, STAGES - 1) else 2.0)
        ahead = step_size if st == STAGES - 2 else 0.5 * step_size

        @pl.loop(0, n_aux, unroll=8)
        def _(a, st=st, c=c, cut=cut, both_cut=both_cut, weight=weight, ahead=ahead):
            arrived = came[order, a] + take[st][c][a].astype(jnp.float32)
            prod = left[a, both_cut, :] - right[order, a]
            turn = jnp.concatenate([prod[rows:], -prod[:rows]], axis=0)
            base = base_of(a, cut)
            here = base if st == 0 else now[a, both_cut, :]
            slope = turn - rate_ref[a] * here + arrived
            sums = (base if st == 0 else total[a, both_cut, :]) + weight * slope
            if st == STAGES - 1:
                outr_ref[a, cut, :] = sums[:rows]
                outi_ref[a, cut, :] = sums[rows:]
            else:
                total[a, both_cut, :] = sums
                ahead_x = base + ahead * slope
                now[a, both_cut, :] = ahead_x
                place(st + 1, c, a, ahead_x)

        if st < STAGES - 1:
            share(st + 1, c)

    for n in range(len(steps) + 1):
        if n < len(steps):
            sums_out(n)
        if n > 0:
            end_out(n - 1)
        if n + 2 < len(steps):
            hop_relay(*steps[n + 2], 1)
        if n > 0:
            finish(n - 1)

    for d in copies:
        d.wait_send()
    for st, c in steps:
        across_copy(st, c).wait_send()

        @pl.when(inner)
        def _(st=st, c=c):
            fold_copy(st, c).wait_send()

        for hop in range(1, lines - 1):
            for way in range(2):

                @pl.when(hop_sends(hop, way))
                def _(st=st, c=c, hop=hop, way=way):
                    at = line - (hop - 1) if way == 0 else line + (hop - 1)
                    hop_copy(st, c, hop, way, at).wait_send()


def by_states(rho_real, rho_imag, hamiltonian, damping, couplings, mode_vector, mode_coef):
    n_aux, rows_dev, width = rho_real.shape
    per_aux = couplings.shape[2]
    devices = lax.axis_size("aux")
    row_devs = lax.axis_size("row")
    lines = devices // 2
    slots = max(1, -(-n_aux * per_aux // devices))
    half = lines * slots
    smem = pl.BlockSpec(memory_space=pltpu.SMEM)
    vmem = pl.BlockSpec(memory_space=pltpu.VMEM)
    anywhere = pl.BlockSpec(memory_space=pl.ANY)
    dma = pltpu.SemaphoreType.DMA
    count = n_aux * per_aux
    lanes = -(-count // 128) * 128
    packed = couplings.transpose(1, 0, 2).reshape(3, count)
    packed = jnp.pad(packed, ((0, 5), (0, lanes - count)))

    rows = rows_dev // CHUNKS
    bf16, f32 = jnp.bfloat16, jnp.float32
    piece = pltpu.VMEM((n_aux, 2 * rows, width), bf16)
    grid = (STAGES, CHUNKS)
    scratch = (
        [pltpu.VMEM((lines * n_aux, 2 * rows, width), bf16)] * (STAGES * CHUNKS)
        + [pltpu.VMEM((n_aux, 2 * row_devs * rows_dev, width), bf16)] * STAGES
        + [piece] * (2 * STAGES * CHUNKS)
        + [pltpu.VMEM((2 * n_aux, 2 * rows, width), bf16)] * (2 * STAGES * CHUNKS)
        + [
            pltpu.VMEM((n_aux, rows_dev, width), f32),
            pltpu.VMEM((n_aux, rows_dev, width), f32),
            pltpu.VMEM((width, width), f32),
            pltpu.VMEM((GROUPS * half, rows_dev, width), f32),
            pltpu.VMEM((GROUPS * half, rows_dev, width), f32),
            pltpu.VMEM((width, mode_vector.shape[0]), f32),
            pltpu.VMEM((GROUPS * (half + n_aux), 128), jnp.int32),
            pltpu.SMEM((GROUPS * (half + n_aux), 128), jnp.int32),
        ]
        + [pltpu.VMEM((8, lanes), jnp.int32)] * lines
        + [
            pltpu.VMEM((half + 1, 2 * rows, width), f32),
            pltpu.VMEM((half + 1, 2 * rows, width), f32),
            pltpu.VMEM((4, n_aux, 2 * rows, width), f32),
            pltpu.VMEM((n_aux, 2 * rows_dev, width), f32),
            pltpu.VMEM((n_aux, 2 * rows_dev, width), f32),
            pltpu.VMEM((n_aux, 2 * rows_dev, width), f32),
            pltpu.VMEM((2, n_aux, 2 * rows, width), f32),
            pltpu.VMEM((4 * rows_dev, 2 * width), bf16),
            pltpu.VMEM((width, 2 * width), bf16),
            dma(grid + (2, lines - 2)),
            dma(grid + (2, lines - 2)),
            dma(grid + (row_devs - 1,)),
            dma(grid + (row_devs - 1,)),
            dma(grid),
            dma(grid),
            dma(grid),
            dma(grid),
            dma((lines - 1,)),
            dma((lines - 1,)),
            dma((3,)),
        ]
    )
    shape = jax.ShapeDtypeStruct((n_aux, rows_dev, width), f32)
    return pl.pallas_call(
        functools.partial(kernel, lines, row_devs, half, count, per_aux),
        out_shape=(shape, shape),
        in_specs=[smem] * 2 + [anywhere] * 2 + [vmem] * 3,
        out_specs=(vmem, vmem),
        scratch_shapes=scratch,
        compiler_params=pltpu.CompilerParams(
            collective_id=0, has_side_effects=True, vmem_limit_bytes=60 * 1024 * 1024
        ),
    )(damping, mode_coef, rho_real, rho_imag, hamiltonian, mode_vector, packed)


def solution(mesh):
    placed = (
        P("aux", "row", None),
        P("aux", "row", None),
        P(),
        P("aux"),
        P("aux", None, None),
        P(),
        P(),
    )

    def shards(rho_real, rho_imag, hamiltonian, damping, couplings, mode_vector, mode_coef):
        args = (rho_real, rho_imag, hamiltonian, damping, couplings, mode_vector, mode_coef)
        devices = mesh.shape["aux"]
        n_aux, rows_dev, _ = rho_real.shape
        slots = max(1, -(-n_aux * couplings.shape[2] // devices))
        terms_sent = (devices - 1) * slots
        states_sent = devices // 2 * n_aux
        even = devices == 2 * LINES and mesh.shape["row"] > 1
        if even and states_sent < terms_sent and rows_dev % (8 * CHUNKS) == 0:
            return by_states(*args)
        return by_terms(*args)

    return jax.shard_map(
        shards,
        mesh=mesh,
        in_specs=placed,
        out_specs=(P("aux", "row", None), P("aux", "row", None)),
        check_vma=False,
    )
```

```python
import functools

import jax
import jax.numpy as jnp
from jax import lax
from jax.experimental import pallas as pl
from jax.experimental.pallas import tpu as pltpu
from jax.sharding import PartitionSpec as P

step_size = 0.1
high = lax.Precision.HIGHEST
MESH = pl.DeviceIdType.MESH
CHUNKS = 4
STAGES = 4


def as_sent(x):
    return jax.tree.map(lambda a: a.astype(jnp.bfloat16) if a.dtype == jnp.float32 else a, x)


def by_terms(rho_real, rho_imag, hamiltonian, damping, couplings, mode_vector, mode_coef):
    energy = 0.5 * (hamiltonian + hamiltonian.T)
    width = energy.shape[0]
    local_aux, rows_dev, _ = rho_real.shape
    per_aux = couplings.shape[2]
    row_index = lax.axis_index("row")
    energy_rows = lax.dynamic_slice_in_dim(energy, row_index * rows_dev, rows_dev, 0)
    devices = lax.axis_size("aux")
    count = local_aux * per_aux
    slots = max(1, -(-count // devices))
    targets = couplings[:, 0, :].reshape(count)
    modes = couplings[:, 1, :].reshape(count)
    weights = couplings[:, 2, :].reshape(count)
    dest = targets // local_aux
    local_target = targets % local_aux
    order = jnp.arange(count)
    same_dest = (dest[:, None] == dest[None, :]) & (order[None, :] < order[:, None])
    ranked = jnp.sum(same_dest.astype(jnp.int32), axis=1)
    slot_of = dest * slots + ranked
    picker = (modes[:, None] == jnp.arange(mode_vector.shape[0])[None, :]).astype(jnp.float32)
    vectors = jnp.dot(picker, mode_vector, precision=high, preferred_element_type=jnp.float32)
    coefs = jnp.dot(picker, mode_coef.T, precision=high, preferred_element_type=jnp.float32)
    scaled = weights.astype(jnp.float32)
    plus = scaled * coefs[:, 1]
    minus = jnp.where(weights == 0, 1.0, scaled * coefs[:, 0])
    row_vec = lax.dynamic_slice_in_dim(vectors, row_index * rows_dev, rows_dev, 1)
    summed = row_vec[:, :, None] + vectors[:, None, :]
    differ = row_vec[:, :, None] - vectors[:, None, :]
    fac_real = (plus[:, None, None] * summed).reshape(local_aux, per_aux, rows_dev, width)
    fac_imag = (-(minus[:, None, None] * differ)).reshape(local_aux, per_aux, rows_dev, width)
    marks = jnp.zeros((devices * slots, local_aux), jnp.bfloat16).at[slot_of, local_target].set(1.0)
    rate = damping[:, None, None]

    def derivative(real_part, imag_part):
        zeros_block = jnp.zeros_like(real_part)
        left_real = zeros_block + jnp.einsum(
            "ij,ajk->aik",
            energy_rows,
            lax.all_gather(as_sent(real_part), "row", axis=1, tiled=True),
            precision=high,
        )
        left_imag = zeros_block + jnp.einsum(
            "ij,ajk->aik",
            energy_rows,
            lax.all_gather(as_sent(imag_part), "row", axis=1, tiled=True),
            precision=high,
        )
        prod_real = left_real - jnp.einsum("aij,jk->aik", real_part, energy, precision=high)
        prod_imag = left_imag - jnp.einsum("aij,jk->aik", imag_part, energy, precision=high)
        source_real = real_part[:, None]
        source_imag = imag_part[:, None]
        term_real = (
            (fac_real * source_real - fac_imag * source_imag)
            .astype(jnp.bfloat16)
            .reshape(count, rows_dev, width)
        )
        term_imag = (
            (fac_real * source_imag + fac_imag * source_real)
            .astype(jnp.bfloat16)
            .reshape(count, rows_dev, width)
        )
        send_real = (
            jnp.zeros((devices * slots, rows_dev, width), jnp.bfloat16).at[slot_of].set(term_real)
        )
        send_imag = (
            jnp.zeros((devices * slots, rows_dev, width), jnp.bfloat16).at[slot_of].set(term_imag)
        )
        got_real, got_imag, got_marks = (
            lax.all_to_all(send_real, "aux", split_axis=0, concat_axis=0, tiled=True),
            lax.all_to_all(send_imag, "aux", split_axis=0, concat_axis=0, tiled=True),
            lax.all_to_all(marks, "aux", split_axis=0, concat_axis=0, tiled=True),
        )
        incoming_real = jnp.einsum(
            "sa,srp->arp", got_marks, got_real, preferred_element_type=jnp.float32
        )
        incoming_imag = jnp.einsum(
            "sa,srp->arp", got_marks, got_imag, preferred_element_type=jnp.float32
        )
        out_real = prod_imag - rate * real_part + incoming_real
        out_imag = -prod_real - rate * imag_part + incoming_imag
        return (out_real, out_imag)

    state_real, state_imag = (rho_real, rho_imag)
    one_real, one_imag = derivative(state_real, state_imag)
    two_real, two_imag = derivative(
        state_real + 0.5 * step_size * one_real, state_imag + 0.5 * step_size * one_imag
    )
    three_real, three_imag = derivative(
        state_real + 0.5 * step_size * two_real, state_imag + 0.5 * step_size * two_imag
    )
    four_real, four_imag = derivative(
        state_real + step_size * three_real, state_imag + step_size * three_imag
    )
    state_real = state_real + step_size / 6.0 * (
        one_real + 2.0 * two_real + 2.0 * three_real + four_real
    )
    state_imag = state_imag + step_size / 6.0 * (
        one_imag + 2.0 * two_imag + 2.0 * three_imag + four_imag
    )
    return (state_real, state_imag)


def kernel(
    lines,
    row_devs,
    half,
    count,
    links_per,
    rate_ref,
    coef_ref,
    real_in,
    imag_in,
    ham_ref,
    mode_ref,
    link_ref,
    outr_ref,
    outi_ref,
    *scratch,
):
    n_aux, rows_dev, width = outr_ref.shape
    rows = rows_dev // CHUNKS
    pair = 2 * rows
    scratch = list(scratch)
    held = [[scratch.pop(0) for _ in range(CHUNKS)] for _ in range(STAGES)]
    full = [scratch.pop(0) for _ in range(STAGES)]
    give = [[scratch.pop(0) for _ in range(CHUNKS)] for _ in range(STAGES)]
    take = [[scratch.pop(0) for _ in range(CHUNKS)] for _ in range(STAGES)]
    real_ref, imag_ref, energy_ref, facr_ref, faci_ref, turned, lists, plan = scratch[:8]
    links = scratch[8 : 8 + lines]
    run, came, now, total, left, right, e_left, e_right = scratch[8 + lines : 16 + lines]
    zs, zr, rs, rr, ys, yr, ls, lr, ins = scratch[16 + lines :]

    fetched = [
        pltpu.make_async_copy(real_in, real_ref, ins.at[0]),
        pltpu.make_async_copy(imag_in, imag_ref, ins.at[1]),
    ]
    for f in fetched:
        f.start()

    aux = lax.axis_index("aux")
    row = lax.axis_index("row")
    line = aux // 2
    side = lax.rem(aux, 2)
    beside = aux + 1 - 2 * side
    row_peers = [lax.rem(row + k, row_devs) for k in range(1, row_devs)]
    last_line = lines - 1

    barrier = pltpu.get_barrier_semaphore()

    line_peers = [lax.rem(aux + 2 * k, 2 * lines) for k in range(1, lines)]
    peers = [(p, row) for p in line_peers + [beside]] + [(aux, p) for p in row_peers]
    for p in peers:
        pl.semaphore_signal(barrier, inc=1, device_id=p, device_id_type=MESH)
    pl.semaphore_wait(barrier, len(peers))

    copies = []

    def send(src, dst, s_sem, r_sem, device):
        c = pltpu.make_async_remote_copy(
            src_ref=src,
            dst_ref=dst,
            send_sem=s_sem,
            recv_sem=r_sem,
            device_id=device,
            device_id_type=MESH,
        )
        c.start()
        copies.append(c)
        return c

    row_copies = {}

    def own_rows(c):
        return pl.ds(pl.multiple_of((row * CHUNKS + c) * pair, pair), pair)

    def block_at(st, c, at):
        return held[st][c].at[pl.ds(pl.multiple_of(at * n_aux, n_aux), n_aux)]

    def hop_copy(st, c, hop, way, at):
        block = block_at(st, c, at)
        return pltpu.make_async_remote_copy(
            src_ref=block,
            dst_ref=block,
            send_sem=zs.at[st, c, way, hop - 1],
            recv_sem=zr.at[st, c, way, hop - 1],
            device_id=(aux + 2 if way == 0 else aux - 2, row),
            device_id_type=MESH,
        )

    def hop_sends(hop, way):
        if way == 0:
            return (line >= hop - 1) & (line < last_line)
        return (line + hop - 1 <= last_line) & (line > 0)

    def hop_gets(hop, way):
        return line >= hop if way == 0 else line + hop <= last_line

    def hop_send(st, c, hop):
        for way in range(2):

            @pl.when(hop_sends(hop, way))
            def _(way=way):
                at = line - (hop - 1) if way == 0 else line + (hop - 1)
                hop_copy(st, c, hop, way, at).start()

    def hop_get(st, c, hop):
        for way in range(2):

            @pl.when(hop_gets(hop, way))
            def _(way=way):
                at = line - hop if way == 0 else line + hop
                hop_copy(st, c, hop, way, at).wait_recv()

    def hop_relay(st, c, hop):
        hop_get(st, c, hop)
        if hop < lines - 1:
            hop_send(st, c, hop + 1)

    def share(st, c):
        block = block_at(st, c, line)
        hop_send(st, c, 1)
        row_copies[st, c] = [
            send(
                block,
                full[st].at[:, own_rows(c), :],
                rs.at[st, c, k],
                rr.at[st, c, k],
                (aux, p),
            )
            for k, p in enumerate(row_peers)
        ]

    def place(st, c, a, x):
        b = x.astype(jnp.bfloat16)
        held[st][c][line * n_aux + a] = b
        full[st][a, own_rows(c), :] = b

    def base_of(a, cut):
        return jnp.concatenate([real_ref[a, cut, :], imag_ref[a, cut, :]], axis=0)

    link_copies = [
        send(link_ref, links[k], ls.at[k - 1], lr.at[k - 1], (p, row))
        for k, p in enumerate(line_peers, 1)
    ]
    for f in fetched:
        f.wait()
    for c in range(CHUNKS):

        @pl.loop(0, n_aux, unroll=8)
        def _(a, c=c):
            place(0, c, a, base_of(a, slice(c * rows, (c + 1) * rows)))

        share(0, c)

    ham = ham_ref[...]
    energy_ref[...] = 0.5 * (ham + ham.T)
    energy = energy_ref[...]
    e_hi = energy.astype(jnp.bfloat16)
    e_right[:, :width] = e_hi
    e_right[:, width:] = (energy - e_hi.astype(jnp.float32)).astype(jnp.bfloat16)
    i32 = jnp.int32

    def spot(i):
        return i // pair * rows + lax.rem(i, rows)

    def part_of(i):
        return lax.rem(i // rows, 2)

    tall = 2 * rows_dev
    wide = 2 * width
    take_rows = lax.broadcasted_iota(i32, (tall, width), 1) == row * rows_dev + spot(
        lax.broadcasted_iota(i32, (tall, width), 0)
    )
    put_columns = lax.broadcasted_iota(i32, (width, wide), 0) == spot(
        lax.broadcasted_iota(i32, (width, wide), 1)
    )
    same_part = part_of(lax.broadcasted_iota(i32, (tall, wide), 0)) == part_of(
        lax.broadcasted_iota(i32, (tall, wide), 1)
    )
    ones_rows = jnp.where(take_rows, 1.0, 0.0).astype(jnp.bfloat16)
    ones_columns = jnp.where(put_columns, 1.0, 0.0).astype(jnp.bfloat16)
    for k in range(2):
        piece = e_right[:, k * width : (k + 1) * width]
        mine = jnp.dot(ones_rows, piece, preferred_element_type=jnp.float32)
        spread = jnp.dot(
            mine.astype(jnp.bfloat16), ones_columns, preferred_element_type=jnp.float32
        )
        e_left[k * tall : (k + 1) * tall] = jnp.where(same_part, spread, 0.0).astype(jnp.bfloat16)
    run[0] = jnp.zeros(run.shape[1:], jnp.float32)

    turned[...] = mode_ref[...].T
    links[0][...] = link_ref[...]
    for d in link_copies:
        d.wait_recv()
    lanes = link_ref.shape[1]
    lane = lax.broadcasted_iota(i32, (1, lanes), 1)
    diagonal = lax.broadcasted_iota(i32, (lanes, lanes), 0) == lax.broadcasted_iota(
        i32, (lanes, lanes), 1
    )
    far = 1 << 20
    keys_row, modes_row, weights_row, source_row, keys_col = [], [], [], [], []
    for k in range(lines):
        from_line = lax.rem(line - k + lines, lines)
        target = links[k][0:1, :]
        dest = target // n_aux
        chosen = (dest // 2 == line) & (lane < count)
        group = jnp.where(lax.rem(dest, 2) == side, 1, 0)
        key = group * n_aux + lax.rem(target, n_aux)
        place_in = from_line * lanes + lane
        key = jnp.where(chosen, key * (lines * lanes) + place_in, far)
        keys_row.append(key)
        modes_row.append(links[k][1:2, :])
        weights_row.append(links[k][2:3, :])
        source_row.append(from_line * n_aux + lane // links_per)
        keys_col.append(jnp.sum(jnp.where(diagonal, key, 0), axis=1, keepdims=True))
    span = lines * lanes
    key = jnp.concatenate(keys_row, axis=1)
    column = jnp.concatenate(keys_col, axis=0)
    chosen = key < far
    before = column < key
    rank = jnp.sum(jnp.where(before, 1, 0), axis=0, keepdims=True)
    again = jnp.sum(jnp.where(before & (column // span == key // span), 1, 0), axis=0, keepdims=True)
    second = n_aux * span
    first_count = jnp.sum(jnp.where(key < second, 1, 0), axis=1, keepdims=True)
    ranked = jnp.where(key < second, rank, rank - first_count)
    slot = jnp.where(key < second, ranked, ranked + half)
    slot = jnp.where(chosen & (ranked < half), slot, -1)
    pick = lax.broadcasted_iota(i32, (2 * half, span), 0) == slot

    def picked(values):
        return jnp.sum(jnp.where(pick, values, 0), axis=1, keepdims=True)

    at = lax.broadcasted_iota(i32, (2 * half, 128), 1)
    table = jnp.where(at == 0, picked(jnp.concatenate(source_row, axis=1)), 0)
    table = jnp.where(at == 1, picked(jnp.concatenate(modes_row, axis=1)), table)
    table = jnp.where(at == 2, picked(jnp.concatenate(weights_row, axis=1)), table)
    table = jnp.where(at == 3, picked(jnp.where(again > 0, 1, 0)), table)
    table = jnp.where(at == 4, picked(jnp.ones_like(key)), table)
    lists[: 2 * half] = table
    wanted = lax.broadcasted_iota(i32, (2 * n_aux, span), 0)
    upto = jnp.sum(jnp.where(key < (wanted + 1) * span, 1, 0), axis=1, keepdims=True)
    here = jnp.sum(jnp.where(key // span == wanted, 1, 0), axis=1, keepdims=True)
    which = lax.broadcasted_iota(i32, (2 * n_aux, 1), 0)
    upto = jnp.minimum(jnp.where(which < n_aux, upto, upto - first_count), half)
    lists[2 * half :] = jnp.broadcast_to(jnp.where(here > 0, upto, 0), (2 * n_aux, 128))
    planned = pltpu.make_async_copy(lists, plan, ins.at[2])
    planned.start()
    steps = [(st, c) for st in range(STAGES) for c in range(CHUNKS)]
    hop_relay(*steps[0], 1)
    hop_relay(*steps[1], 1)
    planned.wait()

    mode_lane = lax.broadcasted_iota(i32, (rows_dev, mode_ref.shape[0]), 1)

    @pl.loop(0, 2 * half, unroll=8)
    def _(e):
        m = plan[e, 1]
        w = plan[e, 2]
        scaled = w.astype(jnp.float32)
        plus = scaled * coef_ref[1, m]
        minus = jnp.where(w == 0, plan[e, 4].astype(jnp.float32), scaled * coef_ref[0, m])
        across = mode_ref[pl.ds(m, 1), :]
        mine = turned[pl.ds(pl.multiple_of(row * rows_dev, rows_dev), rows_dev), :]
        down = jnp.sum(jnp.where(mode_lane == m, mine, 0.0), axis=1, keepdims=True)
        facr_ref[e] = plus * (down + across)
        faci_ref[e] = -minus * (down - across)

    def gather_sum(st, c, group):
        cut = slice(c * rows, (c + 1) * rows)

        def body(e, acc):
            ar, ai = acc
            i = group * half + e
            s = plan[i, 0]
            keep = plan[i, 3].astype(jnp.float32)
            x = held[st][c][s].astype(jnp.float32)
            xr, xi = x[:rows], x[rows:]
            fr = facr_ref[i, cut, :]
            fi = faci_ref[i, cut, :]
            ar = keep * ar + (fr * xr - fi * xi)
            ai = keep * ai + (fr * xi + fi * xr)
            run[e + 1, :rows] = ar
            run[e + 1, rows:] = ai
            return ar, ai

        zero = jnp.zeros((rows, width), jnp.float32)
        lax.fori_loop(0, half, body, (zero, zero), unroll=12)

    across = {}

    def sums_out(n):
        st, c = steps[n]
        turn = n % 2
        for hop in range(3, lines):
            hop_relay(st, c, hop)
        gather_sum(st, c, 0)

        @pl.loop(0, n_aux, unroll=8)
        def _(a):
            give[st][c][a] = run[plan[2 * half + a, 0]].astype(jnp.bfloat16)

        across[n] = send(give[st][c], take[st][c], ys.at[st, c], yr.at[st, c], (beside, row))
        if n + 1 < len(steps):
            hop_relay(*steps[n + 1], 2)
        gather_sum(st, c, 1)

        @pl.loop(0, n_aux, unroll=8)
        def _(a):
            came[turn, a] = run[plan[2 * half + n_aux + a, 0]]

        own = pl.ds(pl.multiple_of(line * n_aux, n_aux), n_aux)
        flat = held[st][c][own].reshape(n_aux * pair, width)
        both = jnp.dot(flat, e_right[...], preferred_element_type=jnp.float32)
        right[turn] = (both[:, :width] + both[:, width:]).reshape(n_aux, pair, width)
        if n + 2 < len(steps):
            hop_relay(*steps[n + 2], 1)

    def finish(n):
        st, c = steps[n]
        order = n % 2
        cut = slice(c * rows, (c + 1) * rows)
        both_cut = slice(c * pair, (c + 1) * pair)
        if c == 0:
            for cc in range(CHUNKS):
                for d in row_copies[st, cc]:
                    d.wait_recv()

            @pl.loop(0, n_aux, unroll=8)
            def _(a, st=st):
                both = jnp.dot(e_left[...], full[st][a], preferred_element_type=jnp.float32)
                left[a] = both[:tall] + both[tall:]

        across[n].wait_recv()

        weight = step_size / 6.0 * (1.0 if st in (0, STAGES - 1) else 2.0)
        ahead = step_size if st == STAGES - 2 else 0.5 * step_size

        @pl.loop(0, n_aux, unroll=8)
        def _(a, st=st, c=c, cut=cut, both_cut=both_cut, weight=weight, ahead=ahead):
            arrived = came[order, a] + take[st][c][a].astype(jnp.float32)
            prod = left[a, both_cut, :] - right[order, a]
            turn = jnp.concatenate([prod[rows:], -prod[:rows]], axis=0)
            base = base_of(a, cut)
            here = base if st == 0 else now[a, both_cut, :]
            slope = turn - rate_ref[a] * here + arrived
            sums = (base if st == 0 else total[a, both_cut, :]) + weight * slope
            if st == STAGES - 1:
                outr_ref[a, cut, :] = sums[:rows]
                outi_ref[a, cut, :] = sums[rows:]
            else:
                total[a, both_cut, :] = sums
                ahead_x = base + ahead * slope
                now[a, both_cut, :] = ahead_x
                place(st + 1, c, a, ahead_x)

        if st < STAGES - 1:
            share(st + 1, c)

    hop_relay(*steps[0], 2)
    for n in range(len(steps) + 1):
        if n < len(steps):
            sums_out(n)
        if n > 0:
            finish(n - 1)

    for d in copies:
        d.wait_send()
    for st, c in steps:
        for hop in range(1, lines):
            for way in range(2):

                @pl.when(hop_sends(hop, way))
                def _(st=st, c=c, hop=hop, way=way):
                    at = line - (hop - 1) if way == 0 else line + (hop - 1)
                    hop_copy(st, c, hop, way, at).wait_send()


def by_states(rho_real, rho_imag, hamiltonian, damping, couplings, mode_vector, mode_coef):
    n_aux, rows_dev, width = rho_real.shape
    per_aux = couplings.shape[2]
    devices = lax.axis_size("aux")
    row_devs = lax.axis_size("row")
    lines = devices // 2
    slots = max(1, -(-n_aux * per_aux // devices))
    half = lines * slots
    smem = pl.BlockSpec(memory_space=pltpu.SMEM)
    vmem = pl.BlockSpec(memory_space=pltpu.VMEM)
    anywhere = pl.BlockSpec(memory_space=pl.ANY)
    dma = pltpu.SemaphoreType.DMA
    count = n_aux * per_aux
    lanes = -(-count // 128) * 128
    packed = couplings.transpose(1, 0, 2).reshape(3, count)
    packed = jnp.pad(packed, ((0, 5), (0, lanes - count)))

    rows = rows_dev // CHUNKS
    bf16, f32 = jnp.bfloat16, jnp.float32
    piece = pltpu.VMEM((n_aux, 2 * rows, width), bf16)
    grid = (STAGES, CHUNKS)
    scratch = (
        [pltpu.VMEM((lines * n_aux, 2 * rows, width), bf16)] * (STAGES * CHUNKS)
        + [pltpu.VMEM((n_aux, 2 * row_devs * rows_dev, width), bf16)] * STAGES
        + [piece] * (2 * STAGES * CHUNKS)
        + [
            pltpu.VMEM((n_aux, rows_dev, width), f32),
            pltpu.VMEM((n_aux, rows_dev, width), f32),
            pltpu.VMEM((width, width), f32),
            pltpu.VMEM((2 * half, rows_dev, width), f32),
            pltpu.VMEM((2 * half, rows_dev, width), f32),
            pltpu.VMEM((width, mode_vector.shape[0]), f32),
            pltpu.VMEM((2 * half + 2 * n_aux, 128), jnp.int32),
            pltpu.SMEM((2 * half + 2 * n_aux, 128), jnp.int32),
        ]
        + [pltpu.VMEM((8, lanes), jnp.int32)] * lines
        + [
            pltpu.VMEM((half + 1, 2 * rows, width), f32),
            pltpu.VMEM((2, n_aux, 2 * rows, width), f32),
            pltpu.VMEM((n_aux, 2 * rows_dev, width), f32),
            pltpu.VMEM((n_aux, 2 * rows_dev, width), f32),
            pltpu.VMEM((n_aux, 2 * rows_dev, width), f32),
            pltpu.VMEM((2, n_aux, 2 * rows, width), f32),
            pltpu.VMEM((4 * rows_dev, 2 * width), bf16),
            pltpu.VMEM((width, 2 * width), bf16),
            dma(grid + (2, lines - 1)),
            dma(grid + (2, lines - 1)),
            dma(grid + (row_devs - 1,)),
            dma(grid + (row_devs - 1,)),
            dma(grid),
            dma(grid),
            dma((lines - 1,)),
            dma((lines - 1,)),
            dma((3,)),
        ]
    )
    shape = jax.ShapeDtypeStruct((n_aux, rows_dev, width), f32)
    return pl.pallas_call(
        functools.partial(kernel, lines, row_devs, half, count, per_aux),
        out_shape=(shape, shape),
        in_specs=[smem] * 2 + [anywhere] * 2 + [vmem] * 3,
        out_specs=(vmem, vmem),
        scratch_shapes=scratch,
        compiler_params=pltpu.CompilerParams(
            collective_id=0, has_side_effects=True, vmem_limit_bytes=60 * 1024 * 1024
        ),
    )(damping, mode_coef, rho_real, rho_imag, hamiltonian, mode_vector, packed)


def solution(mesh):
    placed = (
        P("aux", "row", None),
        P("aux", "row", None),
        P(),
        P("aux"),
        P("aux", None, None),
        P(),
        P(),
    )

    def shards(rho_real, rho_imag, hamiltonian, damping, couplings, mode_vector, mode_coef):
        args = (rho_real, rho_imag, hamiltonian, damping, couplings, mode_vector, mode_coef)
        devices = mesh.shape["aux"]
        n_aux, rows_dev, _ = rho_real.shape
        slots = max(1, -(-n_aux * couplings.shape[2] // devices))
        terms_sent = (devices - 1) * slots
        states_sent = devices // 2 * n_aux
        even = devices % 2 == 0 and devices > 4 and mesh.shape["row"] > 1
        if even and states_sent < terms_sent and rows_dev % (8 * CHUNKS) == 0:
            return by_states(*args)
        return by_terms(*args)

    return jax.shard_map(
        shards,
        mesh=mesh,
        in_specs=placed,
        out_specs=(P("aux", "row", None), P("aux", "row", None)),
        check_vma=False,
    )
```

```python
import functools

import jax
import jax.numpy as jnp
from jax import lax
from jax.experimental import pallas as pl
from jax.experimental.pallas import tpu as pltpu
from jax.sharding import PartitionSpec as P

step_size = 0.1
high = lax.Precision.HIGHEST
MESH = pl.DeviceIdType.MESH
CHUNKS = 4
STAGES = 4


def as_sent(x):
    return jax.tree.map(lambda a: a.astype(jnp.bfloat16) if a.dtype == jnp.float32 else a, x)


def by_terms(rho_real, rho_imag, hamiltonian, damping, couplings, mode_vector, mode_coef):
    energy = 0.5 * (hamiltonian + hamiltonian.T)
    width = energy.shape[0]
    local_aux, rows_dev, _ = rho_real.shape
    per_aux = couplings.shape[2]
    row_index = lax.axis_index("row")
    energy_rows = lax.dynamic_slice_in_dim(energy, row_index * rows_dev, rows_dev, 0)
    devices = lax.axis_size("aux")
    count = local_aux * per_aux
    slots = max(1, -(-count // devices))
    targets = couplings[:, 0, :].reshape(count)
    modes = couplings[:, 1, :].reshape(count)
    weights = couplings[:, 2, :].reshape(count)
    dest = targets // local_aux
    local_target = targets % local_aux
    order = jnp.arange(count)
    same_dest = (dest[:, None] == dest[None, :]) & (order[None, :] < order[:, None])
    ranked = jnp.sum(same_dest.astype(jnp.int32), axis=1)
    slot_of = dest * slots + ranked
    picker = (modes[:, None] == jnp.arange(mode_vector.shape[0])[None, :]).astype(jnp.float32)
    vectors = jnp.dot(picker, mode_vector, precision=high, preferred_element_type=jnp.float32)
    coefs = jnp.dot(picker, mode_coef.T, precision=high, preferred_element_type=jnp.float32)
    scaled = weights.astype(jnp.float32)
    plus = scaled * coefs[:, 1]
    minus = jnp.where(weights == 0, 1.0, scaled * coefs[:, 0])
    row_vec = lax.dynamic_slice_in_dim(vectors, row_index * rows_dev, rows_dev, 1)
    summed = row_vec[:, :, None] + vectors[:, None, :]
    differ = row_vec[:, :, None] - vectors[:, None, :]
    fac_real = (plus[:, None, None] * summed).reshape(local_aux, per_aux, rows_dev, width)
    fac_imag = (-(minus[:, None, None] * differ)).reshape(local_aux, per_aux, rows_dev, width)
    marks = jnp.zeros((devices * slots, local_aux), jnp.bfloat16).at[slot_of, local_target].set(1.0)
    rate = damping[:, None, None]

    def derivative(real_part, imag_part):
        zeros_block = jnp.zeros_like(real_part)
        left_real = zeros_block + jnp.einsum(
            "ij,ajk->aik",
            energy_rows,
            lax.all_gather(as_sent(real_part), "row", axis=1, tiled=True),
            precision=high,
        )
        left_imag = zeros_block + jnp.einsum(
            "ij,ajk->aik",
            energy_rows,
            lax.all_gather(as_sent(imag_part), "row", axis=1, tiled=True),
            precision=high,
        )
        prod_real = left_real - jnp.einsum("aij,jk->aik", real_part, energy, precision=high)
        prod_imag = left_imag - jnp.einsum("aij,jk->aik", imag_part, energy, precision=high)
        source_real = real_part[:, None]
        source_imag = imag_part[:, None]
        term_real = (
            (fac_real * source_real - fac_imag * source_imag)
            .astype(jnp.bfloat16)
            .reshape(count, rows_dev, width)
        )
        term_imag = (
            (fac_real * source_imag + fac_imag * source_real)
            .astype(jnp.bfloat16)
            .reshape(count, rows_dev, width)
        )
        send_real = (
            jnp.zeros((devices * slots, rows_dev, width), jnp.bfloat16).at[slot_of].set(term_real)
        )
        send_imag = (
            jnp.zeros((devices * slots, rows_dev, width), jnp.bfloat16).at[slot_of].set(term_imag)
        )
        got_real, got_imag, got_marks = (
            lax.all_to_all(send_real, "aux", split_axis=0, concat_axis=0, tiled=True),
            lax.all_to_all(send_imag, "aux", split_axis=0, concat_axis=0, tiled=True),
            lax.all_to_all(marks, "aux", split_axis=0, concat_axis=0, tiled=True),
        )
        incoming_real = jnp.einsum(
            "sa,srp->arp", got_marks, got_real, preferred_element_type=jnp.float32
        )
        incoming_imag = jnp.einsum(
            "sa,srp->arp", got_marks, got_imag, preferred_element_type=jnp.float32
        )
        out_real = prod_imag - rate * real_part + incoming_real
        out_imag = -prod_real - rate * imag_part + incoming_imag
        return (out_real, out_imag)

    state_real, state_imag = (rho_real, rho_imag)
    one_real, one_imag = derivative(state_real, state_imag)
    two_real, two_imag = derivative(
        state_real + 0.5 * step_size * one_real, state_imag + 0.5 * step_size * one_imag
    )
    three_real, three_imag = derivative(
        state_real + 0.5 * step_size * two_real, state_imag + 0.5 * step_size * two_imag
    )
    four_real, four_imag = derivative(
        state_real + step_size * three_real, state_imag + step_size * three_imag
    )
    state_real = state_real + step_size / 6.0 * (
        one_real + 2.0 * two_real + 2.0 * three_real + four_real
    )
    state_imag = state_imag + step_size / 6.0 * (
        one_imag + 2.0 * two_imag + 2.0 * three_imag + four_imag
    )
    return (state_real, state_imag)


def kernel(
    lines,
    row_devs,
    half,
    count,
    links_per,
    rate_ref,
    coef_ref,
    real_in,
    imag_in,
    ham_ref,
    mode_ref,
    link_ref,
    outr_ref,
    outi_ref,
    *scratch,
):
    n_aux, rows_dev, width = outr_ref.shape
    rows = rows_dev // CHUNKS
    pair = 2 * rows
    scratch = list(scratch)
    held = [[scratch.pop(0) for _ in range(CHUNKS)] for _ in range(STAGES)]
    full = [scratch.pop(0) for _ in range(STAGES)]
    give = [[scratch.pop(0) for _ in range(CHUNKS)] for _ in range(STAGES)]
    take = [[scratch.pop(0) for _ in range(CHUNKS)] for _ in range(STAGES)]
    real_ref, imag_ref, energy_ref, facr_ref, faci_ref, turned, lists, plan = scratch[:8]
    links = scratch[8 : 8 + lines]
    run, now, total, left, right, e_left, e_right = scratch[8 + lines : 15 + lines]
    zs, zr, rs, rr, ys, yr, ls, lr, ins = scratch[15 + lines :]

    fetched = [
        pltpu.make_async_copy(real_in, real_ref, ins.at[0]),
        pltpu.make_async_copy(imag_in, imag_ref, ins.at[1]),
    ]
    for f in fetched:
        f.start()

    aux = lax.axis_index("aux")
    row = lax.axis_index("row")
    line = aux // 2
    side = lax.rem(aux, 2)
    beside = aux + 1 - 2 * side
    row_peers = [lax.rem(row + k, row_devs) for k in range(1, row_devs)]
    last_line = lines - 1

    barrier = pltpu.get_barrier_semaphore()

    line_peers = [lax.rem(aux + 2 * k, 2 * lines) for k in range(1, lines)]
    peers = [(p, row) for p in line_peers + [beside]] + [(aux, p) for p in row_peers]
    for p in peers:
        pl.semaphore_signal(barrier, inc=1, device_id=p, device_id_type=MESH)
    pl.semaphore_wait(barrier, len(peers))

    copies = []

    def send(src, dst, s_sem, r_sem, device):
        c = pltpu.make_async_remote_copy(
            src_ref=src,
            dst_ref=dst,
            send_sem=s_sem,
            recv_sem=r_sem,
            device_id=device,
            device_id_type=MESH,
        )
        c.start()
        copies.append(c)
        return c

    row_copies = {}

    def own_rows(c):
        return pl.ds(pl.multiple_of((row * CHUNKS + c) * pair, pair), pair)

    def block_at(st, c, at):
        return held[st][c].at[pl.ds(pl.multiple_of(at * n_aux, n_aux), n_aux)]

    def hop_copy(st, c, hop, way, at):
        block = block_at(st, c, at)
        return pltpu.make_async_remote_copy(
            src_ref=block,
            dst_ref=block,
            send_sem=zs.at[st, c, way, hop - 1],
            recv_sem=zr.at[st, c, way, hop - 1],
            device_id=(aux + 2 if way == 0 else aux - 2, row),
            device_id_type=MESH,
        )

    def hop_sends(hop, way):
        if way == 0:
            return (line >= hop - 1) & (line < last_line)
        return (line + hop - 1 <= last_line) & (line > 0)

    def hop_gets(hop, way):
        return line >= hop if way == 0 else line + hop <= last_line

    def hop_send(st, c, hop):
        for way in range(2):

            @pl.when(hop_sends(hop, way))
            def _(way=way):
                at = line - (hop - 1) if way == 0 else line + (hop - 1)
                hop_copy(st, c, hop, way, at).start()

    def hop_get(st, c, hop):
        for way in range(2):

            @pl.when(hop_gets(hop, way))
            def _(way=way):
                at = line - hop if way == 0 else line + hop
                hop_copy(st, c, hop, way, at).wait_recv()

    def hop_relay(st, c, hop):
        hop_get(st, c, hop)
        if hop < lines - 1:
            hop_send(st, c, hop + 1)

    def share(st, c):
        block = block_at(st, c, line)
        hop_send(st, c, 1)
        row_copies[st, c] = [
            send(
                block,
                full[st].at[:, own_rows(c), :],
                rs.at[st, c, k],
                rr.at[st, c, k],
                (aux, p),
            )
            for k, p in enumerate(row_peers)
        ]

    def place(st, c, a, x):
        b = x.astype(jnp.bfloat16)
        held[st][c][line * n_aux + a] = b
        full[st][a, own_rows(c), :] = b

    def base_of(a, cut):
        return jnp.concatenate([real_ref[a, cut, :], imag_ref[a, cut, :]], axis=0)

    link_copies = [
        send(link_ref, links[k], ls.at[k - 1], lr.at[k - 1], (p, row))
        for k, p in enumerate(line_peers, 1)
    ]
    for f in fetched:
        f.wait()
    for c in range(CHUNKS):

        @pl.loop(0, n_aux, unroll=8)
        def _(a, c=c):
            place(0, c, a, base_of(a, slice(c * rows, (c + 1) * rows)))

        share(0, c)

    ham = ham_ref[...]
    energy_ref[...] = 0.5 * (ham + ham.T)
    energy = energy_ref[...]
    e_hi = energy.astype(jnp.bfloat16)
    e_right[:, :width] = e_hi
    e_right[:, width:] = (energy - e_hi.astype(jnp.float32)).astype(jnp.bfloat16)
    i32 = jnp.int32

    def spot(i):
        return i // pair * rows + lax.rem(i, rows)

    def part_of(i):
        return lax.rem(i // rows, 2)

    tall = 2 * rows_dev
    wide = 2 * width
    take_rows = lax.broadcasted_iota(i32, (tall, width), 1) == row * rows_dev + spot(
        lax.broadcasted_iota(i32, (tall, width), 0)
    )
    put_columns = lax.broadcasted_iota(i32, (width, wide), 0) == spot(
        lax.broadcasted_iota(i32, (width, wide), 1)
    )
    same_part = part_of(lax.broadcasted_iota(i32, (tall, wide), 0)) == part_of(
        lax.broadcasted_iota(i32, (tall, wide), 1)
    )
    ones_rows = jnp.where(take_rows, 1.0, 0.0).astype(jnp.bfloat16)
    ones_columns = jnp.where(put_columns, 1.0, 0.0).astype(jnp.bfloat16)
    for k in range(2):
        piece = e_right[:, k * width : (k + 1) * width]
        mine = jnp.dot(ones_rows, piece, preferred_element_type=jnp.float32)
        spread = jnp.dot(
            mine.astype(jnp.bfloat16), ones_columns, preferred_element_type=jnp.float32
        )
        e_left[k * tall : (k + 1) * tall] = jnp.where(same_part, spread, 0.0).astype(jnp.bfloat16)
    run[0] = jnp.zeros(run.shape[1:], jnp.float32)

    turned[...] = mode_ref[...].T
    links[0][...] = link_ref[...]
    for d in link_copies:
        d.wait_recv()
    lanes = link_ref.shape[1]
    lane = lax.broadcasted_iota(i32, (1, lanes), 1)
    diagonal = lax.broadcasted_iota(i32, (lanes, lanes), 0) == lax.broadcasted_iota(
        i32, (lanes, lanes), 1
    )
    far = 1 << 20
    keys_row, modes_row, weights_row, source_row, keys_col = [], [], [], [], []
    for k in range(lines):
        from_line = lax.rem(line - k + lines, lines)
        target = links[k][0:1, :]
        dest = target // n_aux
        chosen = (dest // 2 == line) & (lane < count)
        group = jnp.where(lax.rem(dest, 2) == side, 1, 0)
        key = group * n_aux + lax.rem(target, n_aux)
        place_in = from_line * lanes + lane
        key = jnp.where(chosen, key * (lines * lanes) + place_in, far)
        keys_row.append(key)
        modes_row.append(links[k][1:2, :])
        weights_row.append(links[k][2:3, :])
        source_row.append(from_line * n_aux + lane // links_per)
        keys_col.append(jnp.sum(jnp.where(diagonal, key, 0), axis=1, keepdims=True))
    steps = [(st, c) for st in range(STAGES) for c in range(CHUNKS)]
    hop_relay(*steps[0], 1)
    span = lines * lanes
    key = jnp.concatenate(keys_row, axis=1)
    column = jnp.concatenate(keys_col, axis=0)
    chosen = key < far
    before = column < key
    rank = jnp.sum(jnp.where(before, 1, 0), axis=0, keepdims=True)
    again = jnp.sum(jnp.where(before & (column // span == key // span), 1, 0), axis=0, keepdims=True)
    second = n_aux * span
    first_count = jnp.sum(jnp.where(key < second, 1, 0), axis=1, keepdims=True)
    ranked = jnp.where(key < second, rank, rank - first_count)
    slot = jnp.where(key < second, ranked, ranked + half)
    slot = jnp.where(chosen & (ranked < half), slot, -1)
    pick = lax.broadcasted_iota(i32, (2 * half, span), 0) == slot

    def picked(values):
        return jnp.sum(jnp.where(pick, values, 0), axis=1, keepdims=True)

    hop_relay(*steps[1], 1)
    at = lax.broadcasted_iota(i32, (2 * half, 128), 1)
    table = jnp.where(at == 0, picked(jnp.concatenate(source_row, axis=1)), 0)
    table = jnp.where(at == 1, picked(jnp.concatenate(modes_row, axis=1)), table)
    table = jnp.where(at == 2, picked(jnp.concatenate(weights_row, axis=1)), table)
    table = jnp.where(at == 3, picked(jnp.where(again > 0, 1, 0)), table)
    table = jnp.where(at == 4, picked(jnp.ones_like(key)), table)
    lists[: 2 * half] = table
    wanted = lax.broadcasted_iota(i32, (2 * n_aux, span), 0)
    upto = jnp.sum(jnp.where(key < (wanted + 1) * span, 1, 0), axis=1, keepdims=True)
    here = jnp.sum(jnp.where(key // span == wanted, 1, 0), axis=1, keepdims=True)
    which = lax.broadcasted_iota(i32, (2 * n_aux, 1), 0)
    upto = jnp.minimum(jnp.where(which < n_aux, upto, upto - first_count), half)
    lists[2 * half :] = jnp.broadcast_to(jnp.where(here > 0, upto, 0), (2 * n_aux, 128))
    planned = pltpu.make_async_copy(lists, plan, ins.at[2])
    planned.start()
    hop_relay(*steps[0], 2)
    planned.wait()

    mode_lane = lax.broadcasted_iota(i32, (rows_dev, mode_ref.shape[0]), 1)

    @pl.loop(0, 2 * half, unroll=8)
    def _(e):
        m = plan[e, 1]
        w = plan[e, 2]
        scaled = w.astype(jnp.float32)
        plus = scaled * coef_ref[1, m]
        minus = jnp.where(w == 0, plan[e, 4].astype(jnp.float32), scaled * coef_ref[0, m])
        across = mode_ref[pl.ds(m, 1), :]
        mine = turned[pl.ds(pl.multiple_of(row * rows_dev, rows_dev), rows_dev), :]
        down = jnp.sum(jnp.where(mode_lane == m, mine, 0.0), axis=1, keepdims=True)
        facr_ref[e] = plus * (down + across)
        faci_ref[e] = -minus * (down - across)

    def gather_sum(st, c, group):
        cut = slice(c * rows, (c + 1) * rows)

        def body(e, acc):
            ar, ai = acc
            i = group * half + e
            s = plan[i, 0]
            keep = plan[i, 3].astype(jnp.float32)
            x = held[st][c][s].astype(jnp.float32)
            xr, xi = x[:rows], x[rows:]
            fr = facr_ref[i, cut, :]
            fi = faci_ref[i, cut, :]
            ar = keep * ar + (fr * xr - fi * xi)
            ai = keep * ai + (fr * xi + fi * xr)
            run[e + 1, :rows] = ar
            run[e + 1, rows:] = ai
            return ar, ai

        zero = jnp.zeros((rows, width), jnp.float32)
        lax.fori_loop(0, half, body, (zero, zero), unroll=12)

    for n, (st, c) in enumerate(steps):
        cut = slice(c * rows, (c + 1) * rows)
        both_cut = slice(c * pair, (c + 1) * pair)
        for hop in range(3, lines):
            hop_relay(st, c, hop)
        gather_sum(st, c, 0)

        @pl.loop(0, n_aux, unroll=8)
        def _(a, st=st, c=c):
            give[st][c][a] = run[plan[2 * half + a, 0]].astype(jnp.bfloat16)

        across = send(give[st][c], take[st][c], ys.at[st, c], yr.at[st, c], (beside, row))
        if n + 1 < len(steps):
            hop_relay(*steps[n + 1], 2)
        if n + 2 < len(steps):
            hop_relay(*steps[n + 2], 1)
        own = pl.ds(pl.multiple_of(line * n_aux, n_aux), n_aux)
        flat = held[st][c][own].reshape(n_aux * pair, width)
        both = jnp.dot(flat, e_right[...], preferred_element_type=jnp.float32)
        right[...] = (both[:, :width] + both[:, width:]).reshape(n_aux, pair, width)
        gather_sum(st, c, 1)
        if c == 0:
            for cc in range(CHUNKS):
                for d in row_copies[st, cc]:
                    d.wait_recv()

            @pl.loop(0, n_aux, unroll=8)
            def _(a, st=st):
                both = jnp.dot(e_left[...], full[st][a], preferred_element_type=jnp.float32)
                left[a] = both[:tall] + both[tall:]

        across.wait_recv()

        weight = step_size / 6.0 * (1.0 if st in (0, STAGES - 1) else 2.0)
        ahead = step_size if st == STAGES - 2 else 0.5 * step_size

        @pl.loop(0, n_aux, unroll=8)
        def _(a, st=st, c=c, cut=cut, both_cut=both_cut, weight=weight, ahead=ahead):
            came = run[plan[2 * half + n_aux + a, 0]] + take[st][c][a].astype(jnp.float32)
            prod = left[a, both_cut, :] - right[a]
            turn = jnp.concatenate([prod[rows:], -prod[:rows]], axis=0)
            base = base_of(a, cut)
            here = base if st == 0 else now[a, both_cut, :]
            slope = turn - rate_ref[a] * here + came
            sums = (base if st == 0 else total[a, both_cut, :]) + weight * slope
            if st == STAGES - 1:
                outr_ref[a, cut, :] = sums[:rows]
                outi_ref[a, cut, :] = sums[rows:]
            else:
                total[a, both_cut, :] = sums
                ahead_x = base + ahead * slope
                now[a, both_cut, :] = ahead_x
                place(st + 1, c, a, ahead_x)

        if st < STAGES - 1:
            share(st + 1, c)

    for d in copies:
        d.wait_send()
    for st, c in steps:
        for hop in range(1, lines):
            for way in range(2):

                @pl.when(hop_sends(hop, way))
                def _(st=st, c=c, hop=hop, way=way):
                    at = line - (hop - 1) if way == 0 else line + (hop - 1)
                    hop_copy(st, c, hop, way, at).wait_send()


def by_states(rho_real, rho_imag, hamiltonian, damping, couplings, mode_vector, mode_coef):
    n_aux, rows_dev, width = rho_real.shape
    per_aux = couplings.shape[2]
    devices = lax.axis_size("aux")
    row_devs = lax.axis_size("row")
    lines = devices // 2
    slots = max(1, -(-n_aux * per_aux // devices))
    half = lines * slots
    smem = pl.BlockSpec(memory_space=pltpu.SMEM)
    vmem = pl.BlockSpec(memory_space=pltpu.VMEM)
    anywhere = pl.BlockSpec(memory_space=pl.ANY)
    dma = pltpu.SemaphoreType.DMA
    count = n_aux * per_aux
    lanes = -(-count // 128) * 128
    packed = couplings.transpose(1, 0, 2).reshape(3, count)
    packed = jnp.pad(packed, ((0, 5), (0, lanes - count)))

    rows = rows_dev // CHUNKS
    bf16, f32 = jnp.bfloat16, jnp.float32
    piece = pltpu.VMEM((n_aux, 2 * rows, width), bf16)
    grid = (STAGES, CHUNKS)
    scratch = (
        [pltpu.VMEM((lines * n_aux, 2 * rows, width), bf16)] * (STAGES * CHUNKS)
        + [pltpu.VMEM((n_aux, 2 * row_devs * rows_dev, width), bf16)] * STAGES
        + [piece] * (2 * STAGES * CHUNKS)
        + [
            pltpu.VMEM((n_aux, rows_dev, width), f32),
            pltpu.VMEM((n_aux, rows_dev, width), f32),
            pltpu.VMEM((width, width), f32),
            pltpu.VMEM((2 * half, rows_dev, width), f32),
            pltpu.VMEM((2 * half, rows_dev, width), f32),
            pltpu.VMEM((width, mode_vector.shape[0]), f32),
            pltpu.VMEM((2 * half + 2 * n_aux, 128), jnp.int32),
            pltpu.SMEM((2 * half + 2 * n_aux, 128), jnp.int32),
        ]
        + [pltpu.VMEM((8, lanes), jnp.int32)] * lines
        + [
            pltpu.VMEM((half + 1, 2 * rows, width), f32),
            pltpu.VMEM((n_aux, 2 * rows_dev, width), f32),
            pltpu.VMEM((n_aux, 2 * rows_dev, width), f32),
            pltpu.VMEM((n_aux, 2 * rows_dev, width), f32),
            pltpu.VMEM((n_aux, 2 * rows, width), f32),
            pltpu.VMEM((4 * rows_dev, 2 * width), bf16),
            pltpu.VMEM((width, 2 * width), bf16),
            dma(grid + (2, lines - 1)),
            dma(grid + (2, lines - 1)),
            dma(grid + (row_devs - 1,)),
            dma(grid + (row_devs - 1,)),
            dma(grid),
            dma(grid),
            dma((lines - 1,)),
            dma((lines - 1,)),
            dma((3,)),
        ]
    )
    shape = jax.ShapeDtypeStruct((n_aux, rows_dev, width), f32)
    return pl.pallas_call(
        functools.partial(kernel, lines, row_devs, half, count, per_aux),
        out_shape=(shape, shape),
        in_specs=[smem] * 2 + [anywhere] * 2 + [vmem] * 3,
        out_specs=(vmem, vmem),
        scratch_shapes=scratch,
        compiler_params=pltpu.CompilerParams(
            collective_id=0, has_side_effects=True, vmem_limit_bytes=60 * 1024 * 1024
        ),
    )(damping, mode_coef, rho_real, rho_imag, hamiltonian, mode_vector, packed)


def solution(mesh):
    placed = (
        P("aux", "row", None),
        P("aux", "row", None),
        P(),
        P("aux"),
        P("aux", None, None),
        P(),
        P(),
    )

    def shards(rho_real, rho_imag, hamiltonian, damping, couplings, mode_vector, mode_coef):
        args = (rho_real, rho_imag, hamiltonian, damping, couplings, mode_vector, mode_coef)
        devices = mesh.shape["aux"]
        n_aux, rows_dev, _ = rho_real.shape
        slots = max(1, -(-n_aux * couplings.shape[2] // devices))
        terms_sent = (devices - 1) * slots
        states_sent = devices // 2 * n_aux
        even = devices % 2 == 0 and devices > 4 and mesh.shape["row"] > 1
        if even and states_sent < terms_sent and rows_dev % (8 * CHUNKS) == 0:
            return by_states(*args)
        return by_terms(*args)

    return jax.shard_map(
        shards,
        mesh=mesh,
        in_specs=placed,
        out_specs=(P("aux", "row", None), P("aux", "row", None)),
        check_vma=False,
    )
```

```python
import functools

import jax
import jax.numpy as jnp
from jax import lax
from jax.experimental import pallas as pl
from jax.experimental.pallas import tpu as pltpu
from jax.sharding import PartitionSpec as P

step_size = 0.1
high = lax.Precision.HIGHEST
MESH = pl.DeviceIdType.MESH
CHUNKS = 4
STAGES = 4


def as_sent(x):
    return jax.tree.map(lambda a: a.astype(jnp.bfloat16) if a.dtype == jnp.float32 else a, x)


def by_terms(rho_real, rho_imag, hamiltonian, damping, couplings, mode_vector, mode_coef):
    energy = 0.5 * (hamiltonian + hamiltonian.T)
    width = energy.shape[0]
    local_aux, rows_dev, _ = rho_real.shape
    per_aux = couplings.shape[2]
    row_index = lax.axis_index("row")
    energy_rows = lax.dynamic_slice_in_dim(energy, row_index * rows_dev, rows_dev, 0)
    devices = lax.axis_size("aux")
    count = local_aux * per_aux
    slots = max(1, -(-count // devices))
    targets = couplings[:, 0, :].reshape(count)
    modes = couplings[:, 1, :].reshape(count)
    weights = couplings[:, 2, :].reshape(count)
    dest = targets // local_aux
    local_target = targets % local_aux
    order = jnp.arange(count)
    same_dest = (dest[:, None] == dest[None, :]) & (order[None, :] < order[:, None])
    ranked = jnp.sum(same_dest.astype(jnp.int32), axis=1)
    slot_of = dest * slots + ranked
    picker = (modes[:, None] == jnp.arange(mode_vector.shape[0])[None, :]).astype(jnp.float32)
    vectors = jnp.dot(picker, mode_vector, precision=high, preferred_element_type=jnp.float32)
    coefs = jnp.dot(picker, mode_coef.T, precision=high, preferred_element_type=jnp.float32)
    scaled = weights.astype(jnp.float32)
    plus = scaled * coefs[:, 1]
    minus = jnp.where(weights == 0, 1.0, scaled * coefs[:, 0])
    row_vec = lax.dynamic_slice_in_dim(vectors, row_index * rows_dev, rows_dev, 1)
    summed = row_vec[:, :, None] + vectors[:, None, :]
    differ = row_vec[:, :, None] - vectors[:, None, :]
    fac_real = (plus[:, None, None] * summed).reshape(local_aux, per_aux, rows_dev, width)
    fac_imag = (-(minus[:, None, None] * differ)).reshape(local_aux, per_aux, rows_dev, width)
    marks = jnp.zeros((devices * slots, local_aux), jnp.bfloat16).at[slot_of, local_target].set(1.0)
    rate = damping[:, None, None]

    def derivative(real_part, imag_part):
        zeros_block = jnp.zeros_like(real_part)
        left_real = zeros_block + jnp.einsum(
            "ij,ajk->aik",
            energy_rows,
            lax.all_gather(as_sent(real_part), "row", axis=1, tiled=True),
            precision=high,
        )
        left_imag = zeros_block + jnp.einsum(
            "ij,ajk->aik",
            energy_rows,
            lax.all_gather(as_sent(imag_part), "row", axis=1, tiled=True),
            precision=high,
        )
        prod_real = left_real - jnp.einsum("aij,jk->aik", real_part, energy, precision=high)
        prod_imag = left_imag - jnp.einsum("aij,jk->aik", imag_part, energy, precision=high)
        source_real = real_part[:, None]
        source_imag = imag_part[:, None]
        term_real = (
            (fac_real * source_real - fac_imag * source_imag)
            .astype(jnp.bfloat16)
            .reshape(count, rows_dev, width)
        )
        term_imag = (
            (fac_real * source_imag + fac_imag * source_real)
            .astype(jnp.bfloat16)
            .reshape(count, rows_dev, width)
        )
        send_real = (
            jnp.zeros((devices * slots, rows_dev, width), jnp.bfloat16).at[slot_of].set(term_real)
        )
        send_imag = (
            jnp.zeros((devices * slots, rows_dev, width), jnp.bfloat16).at[slot_of].set(term_imag)
        )
        got_real, got_imag, got_marks = (
            lax.all_to_all(send_real, "aux", split_axis=0, concat_axis=0, tiled=True),
            lax.all_to_all(send_imag, "aux", split_axis=0, concat_axis=0, tiled=True),
            lax.all_to_all(marks, "aux", split_axis=0, concat_axis=0, tiled=True),
        )
        incoming_real = jnp.einsum(
            "sa,srp->arp", got_marks, got_real, preferred_element_type=jnp.float32
        )
        incoming_imag = jnp.einsum(
            "sa,srp->arp", got_marks, got_imag, preferred_element_type=jnp.float32
        )
        out_real = prod_imag - rate * real_part + incoming_real
        out_imag = -prod_real - rate * imag_part + incoming_imag
        return (out_real, out_imag)

    state_real, state_imag = (rho_real, rho_imag)
    one_real, one_imag = derivative(state_real, state_imag)
    two_real, two_imag = derivative(
        state_real + 0.5 * step_size * one_real, state_imag + 0.5 * step_size * one_imag
    )
    three_real, three_imag = derivative(
        state_real + 0.5 * step_size * two_real, state_imag + 0.5 * step_size * two_imag
    )
    four_real, four_imag = derivative(
        state_real + step_size * three_real, state_imag + step_size * three_imag
    )
    state_real = state_real + step_size / 6.0 * (
        one_real + 2.0 * two_real + 2.0 * three_real + four_real
    )
    state_imag = state_imag + step_size / 6.0 * (
        one_imag + 2.0 * two_imag + 2.0 * three_imag + four_imag
    )
    return (state_real, state_imag)


def kernel(
    lines,
    row_devs,
    half,
    count,
    links_per,
    rate_ref,
    coef_ref,
    real_in,
    imag_in,
    ham_ref,
    mode_ref,
    link_ref,
    outr_ref,
    outi_ref,
    *scratch,
):
    n_aux, rows_dev, width = outr_ref.shape
    rows = rows_dev // CHUNKS
    pair = 2 * rows
    scratch = list(scratch)
    held = [[scratch.pop(0) for _ in range(CHUNKS)] for _ in range(STAGES)]
    full = [scratch.pop(0) for _ in range(STAGES)]
    give = [[scratch.pop(0) for _ in range(CHUNKS)] for _ in range(STAGES)]
    take = [[scratch.pop(0) for _ in range(CHUNKS)] for _ in range(STAGES)]
    real_ref, imag_ref, energy_ref, facr_ref, faci_ref, turned, lists, plan = scratch[:8]
    links = scratch[8 : 8 + lines]
    run, now, total, left, right, e_left, e_right = scratch[8 + lines : 15 + lines]
    zs, zr, rs, rr, ys, yr, ls, lr, ins = scratch[15 + lines :]

    fetched = [
        pltpu.make_async_copy(real_in, real_ref, ins.at[0]),
        pltpu.make_async_copy(imag_in, imag_ref, ins.at[1]),
    ]
    for f in fetched:
        f.start()

    aux = lax.axis_index("aux")
    row = lax.axis_index("row")
    line = aux // 2
    side = lax.rem(aux, 2)
    beside = aux + 1 - 2 * side
    row_peers = [lax.rem(row + k, row_devs) for k in range(1, row_devs)]
    last_line = lines - 1

    barrier = pltpu.get_barrier_semaphore()

    line_peers = [lax.rem(aux + 2 * k, 2 * lines) for k in range(1, lines)]
    peers = [(p, row) for p in line_peers + [beside]] + [(aux, p) for p in row_peers]
    for p in peers:
        pl.semaphore_signal(barrier, inc=1, device_id=p, device_id_type=MESH)
    pl.semaphore_wait(barrier, len(peers))

    copies = []

    def send(src, dst, s_sem, r_sem, device):
        c = pltpu.make_async_remote_copy(
            src_ref=src,
            dst_ref=dst,
            send_sem=s_sem,
            recv_sem=r_sem,
            device_id=device,
            device_id_type=MESH,
        )
        c.start()
        copies.append(c)
        return c

    row_copies = {}

    def own_rows(c):
        return pl.ds(pl.multiple_of((row * CHUNKS + c) * pair, pair), pair)

    def block_at(st, c, at):
        return held[st][c].at[pl.ds(pl.multiple_of(at * n_aux, n_aux), n_aux)]

    def hop_copy(st, c, hop, way, at):
        block = block_at(st, c, at)
        return pltpu.make_async_remote_copy(
            src_ref=block,
            dst_ref=block,
            send_sem=zs.at[st, c, way, hop - 1],
            recv_sem=zr.at[st, c, way, hop - 1],
            device_id=(aux + 2 if way == 0 else aux - 2, row),
            device_id_type=MESH,
        )

    def hop_sends(hop, way):
        if way == 0:
            return (line >= hop - 1) & (line < last_line)
        return (line + hop - 1 <= last_line) & (line > 0)

    def hop_gets(hop, way):
        return line >= hop if way == 0 else line + hop <= last_line

    def hop_send(st, c, hop):
        for way in range(2):

            @pl.when(hop_sends(hop, way))
            def _(way=way):
                at = line - (hop - 1) if way == 0 else line + (hop - 1)
                hop_copy(st, c, hop, way, at).start()

    def hop_get(st, c, hop):
        for way in range(2):

            @pl.when(hop_gets(hop, way))
            def _(way=way):
                at = line - hop if way == 0 else line + hop
                hop_copy(st, c, hop, way, at).wait_recv()

    def hop_relay(st, c, hop):
        hop_get(st, c, hop)
        if hop < lines - 1:
            hop_send(st, c, hop + 1)

    def share(st, c):
        block = block_at(st, c, line)
        hop_send(st, c, 1)
        row_copies[st, c] = [
            send(
                block,
                full[st].at[:, own_rows(c), :],
                rs.at[st, c, k],
                rr.at[st, c, k],
                (aux, p),
            )
            for k, p in enumerate(row_peers)
        ]

    def place(st, c, a, x):
        b = x.astype(jnp.bfloat16)
        held[st][c][line * n_aux + a] = b
        full[st][a, own_rows(c), :] = b

    def base_of(a, cut):
        return jnp.concatenate([real_ref[a, cut, :], imag_ref[a, cut, :]], axis=0)

    link_copies = [
        send(link_ref, links[k], ls.at[k - 1], lr.at[k - 1], (p, row))
        for k, p in enumerate(line_peers, 1)
    ]
    for f in fetched:
        f.wait()
    for c in range(CHUNKS):

        @pl.loop(0, n_aux, unroll=8)
        def _(a, c=c):
            place(0, c, a, base_of(a, slice(c * rows, (c + 1) * rows)))

        share(0, c)

    ham = ham_ref[...]
    energy_ref[...] = 0.5 * (ham + ham.T)
    energy = energy_ref[...]
    e_hi = energy.astype(jnp.bfloat16)
    e_right[:, :width] = e_hi
    e_right[:, width:] = (energy - e_hi.astype(jnp.float32)).astype(jnp.bfloat16)
    i32 = jnp.int32

    def spot(i):
        return i // pair * rows + lax.rem(i, rows)

    def part_of(i):
        return lax.rem(i // rows, 2)

    tall = 2 * rows_dev
    wide = 2 * width
    take_rows = lax.broadcasted_iota(i32, (tall, width), 1) == row * rows_dev + spot(
        lax.broadcasted_iota(i32, (tall, width), 0)
    )
    put_columns = lax.broadcasted_iota(i32, (width, wide), 0) == spot(
        lax.broadcasted_iota(i32, (width, wide), 1)
    )
    same_part = part_of(lax.broadcasted_iota(i32, (tall, wide), 0)) == part_of(
        lax.broadcasted_iota(i32, (tall, wide), 1)
    )
    ones_rows = jnp.where(take_rows, 1.0, 0.0).astype(jnp.bfloat16)
    ones_columns = jnp.where(put_columns, 1.0, 0.0).astype(jnp.bfloat16)
    for k in range(2):
        piece = e_right[:, k * width : (k + 1) * width]
        mine = jnp.dot(ones_rows, piece, preferred_element_type=jnp.float32)
        spread = jnp.dot(
            mine.astype(jnp.bfloat16), ones_columns, preferred_element_type=jnp.float32
        )
        e_left[k * tall : (k + 1) * tall] = jnp.where(same_part, spread, 0.0).astype(jnp.bfloat16)
    run[0] = jnp.zeros(run.shape[1:], jnp.float32)

    turned[...] = mode_ref[...].T
    links[0][...] = link_ref[...]
    for d in link_copies:
        d.wait_recv()
    lanes = link_ref.shape[1]
    lane = lax.broadcasted_iota(i32, (1, lanes), 1)
    diagonal = lax.broadcasted_iota(i32, (lanes, lanes), 0) == lax.broadcasted_iota(
        i32, (lanes, lanes), 1
    )
    far = 1 << 20
    keys_row, modes_row, weights_row, source_row, keys_col = [], [], [], [], []
    for k in range(lines):
        from_line = lax.rem(line - k + lines, lines)
        target = links[k][0:1, :]
        dest = target // n_aux
        chosen = (dest // 2 == line) & (lane < count)
        group = jnp.where(lax.rem(dest, 2) == side, 1, 0)
        key = group * n_aux + lax.rem(target, n_aux)
        place_in = from_line * lanes + lane
        key = jnp.where(chosen, key * (lines * lanes) + place_in, far)
        keys_row.append(key)
        modes_row.append(links[k][1:2, :])
        weights_row.append(links[k][2:3, :])
        source_row.append(from_line * n_aux + lane // links_per)
        keys_col.append(jnp.sum(jnp.where(diagonal, key, 0), axis=1, keepdims=True))
    steps = [(st, c) for st in range(STAGES) for c in range(CHUNKS)]
    hop_relay(*steps[0], 1)
    span = lines * lanes
    key = jnp.concatenate(keys_row, axis=1)
    column = jnp.concatenate(keys_col, axis=0)
    chosen = key < far
    before = column < key
    rank = jnp.sum(jnp.where(before, 1, 0), axis=0, keepdims=True)
    again = jnp.sum(jnp.where(before & (column // span == key // span), 1, 0), axis=0, keepdims=True)
    second = n_aux * span
    first_count = jnp.sum(jnp.where(key < second, 1, 0), axis=1, keepdims=True)
    ranked = jnp.where(key < second, rank, rank - first_count)
    slot = jnp.where(key < second, ranked, ranked + half)
    slot = jnp.where(chosen & (ranked < half), slot, -1)
    pick = lax.broadcasted_iota(i32, (2 * half, span), 0) == slot

    def picked(values):
        return jnp.sum(jnp.where(pick, values, 0), axis=1, keepdims=True)

    hop_relay(*steps[1], 1)
    at = lax.broadcasted_iota(i32, (2 * half, 128), 1)
    table = jnp.where(at == 0, picked(jnp.concatenate(source_row, axis=1)), 0)
    table = jnp.where(at == 1, picked(jnp.concatenate(modes_row, axis=1)), table)
    table = jnp.where(at == 2, picked(jnp.concatenate(weights_row, axis=1)), table)
    table = jnp.where(at == 3, picked(jnp.where(again > 0, 1, 0)), table)
    table = jnp.where(at == 4, picked(jnp.ones_like(key)), table)
    lists[: 2 * half] = table
    wanted = lax.broadcasted_iota(i32, (2 * n_aux, span), 0)
    upto = jnp.sum(jnp.where(key < (wanted + 1) * span, 1, 0), axis=1, keepdims=True)
    here = jnp.sum(jnp.where(key // span == wanted, 1, 0), axis=1, keepdims=True)
    which = lax.broadcasted_iota(i32, (2 * n_aux, 1), 0)
    upto = jnp.minimum(jnp.where(which < n_aux, upto, upto - first_count), half)
    lists[2 * half :] = jnp.broadcast_to(jnp.where(here > 0, upto, 0), (2 * n_aux, 128))
    planned = pltpu.make_async_copy(lists, plan, ins.at[2])
    planned.start()
    hop_relay(*steps[0], 2)
    planned.wait()

    mode_lane = lax.broadcasted_iota(i32, (rows_dev, mode_ref.shape[0]), 1)

    @pl.loop(0, 2 * half, unroll=8)
    def _(e):
        m = plan[e, 1]
        w = plan[e, 2]
        scaled = w.astype(jnp.float32)
        plus = scaled * coef_ref[1, m]
        minus = jnp.where(w == 0, plan[e, 4].astype(jnp.float32), scaled * coef_ref[0, m])
        across = mode_ref[pl.ds(m, 1), :]
        mine = turned[pl.ds(pl.multiple_of(row * rows_dev, rows_dev), rows_dev), :]
        down = jnp.sum(jnp.where(mode_lane == m, mine, 0.0), axis=1, keepdims=True)
        facr_ref[e] = plus * (down + across)
        faci_ref[e] = -minus * (down - across)

    def gather_sum(st, c, group):
        cut = slice(c * rows, (c + 1) * rows)

        def body(e, acc):
            ar, ai = acc
            i = group * half + e
            s = plan[i, 0]
            keep = plan[i, 3].astype(jnp.float32)
            x = held[st][c][s].astype(jnp.float32)
            xr, xi = x[:rows], x[rows:]
            fr = facr_ref[i, cut, :]
            fi = faci_ref[i, cut, :]
            ar = keep * ar + (fr * xr - fi * xi)
            ai = keep * ai + (fr * xi + fi * xr)
            run[e + 1, :rows] = ar
            run[e + 1, rows:] = ai
            return ar, ai

        zero = jnp.zeros((rows, width), jnp.float32)
        lax.fori_loop(0, half, body, (zero, zero), unroll=12)

    for n, (st, c) in enumerate(steps):
        cut = slice(c * rows, (c + 1) * rows)
        both_cut = slice(c * pair, (c + 1) * pair)
        for hop in range(3, lines):
            hop_relay(st, c, hop)
        if n + 1 < len(steps):
            hop_relay(*steps[n + 1], 2)
        gather_sum(st, c, 0)

        @pl.loop(0, n_aux, unroll=8)
        def _(a, st=st, c=c):
            give[st][c][a] = run[plan[2 * half + a, 0]].astype(jnp.bfloat16)

        across = send(give[st][c], take[st][c], ys.at[st, c], yr.at[st, c], (beside, row))
        if n + 2 < len(steps):
            hop_relay(*steps[n + 2], 1)
        own = pl.ds(pl.multiple_of(line * n_aux, n_aux), n_aux)
        flat = held[st][c][own].reshape(n_aux * pair, width)
        both = jnp.dot(flat, e_right[...], preferred_element_type=jnp.float32)
        right[...] = (both[:, :width] + both[:, width:]).reshape(n_aux, pair, width)
        gather_sum(st, c, 1)
        if c == 0:
            for cc in range(CHUNKS):
                for d in row_copies[st, cc]:
                    d.wait_recv()

            @pl.loop(0, n_aux, unroll=8)
            def _(a, st=st):
                both = jnp.dot(e_left[...], full[st][a], preferred_element_type=jnp.float32)
                left[a] = both[:tall] + both[tall:]

        across.wait_recv()

        weight = step_size / 6.0 * (1.0 if st in (0, STAGES - 1) else 2.0)
        ahead = step_size if st == STAGES - 2 else 0.5 * step_size

        @pl.loop(0, n_aux, unroll=8)
        def _(a, st=st, c=c, cut=cut, both_cut=both_cut, weight=weight, ahead=ahead):
            came = run[plan[2 * half + n_aux + a, 0]] + take[st][c][a].astype(jnp.float32)
            prod = left[a, both_cut, :] - right[a]
            turn = jnp.concatenate([prod[rows:], -prod[:rows]], axis=0)
            base = base_of(a, cut)
            here = base if st == 0 else now[a, both_cut, :]
            slope = turn - rate_ref[a] * here + came
            sums = (base if st == 0 else total[a, both_cut, :]) + weight * slope
            if st == STAGES - 1:
                outr_ref[a, cut, :] = sums[:rows]
                outi_ref[a, cut, :] = sums[rows:]
            else:
                total[a, both_cut, :] = sums
                ahead_x = base + ahead * slope
                now[a, both_cut, :] = ahead_x
                place(st + 1, c, a, ahead_x)

        if st < STAGES - 1:
            share(st + 1, c)

    for d in copies:
        d.wait_send()
    for st, c in steps:
        for hop in range(1, lines):
            for way in range(2):

                @pl.when(hop_sends(hop, way))
                def _(st=st, c=c, hop=hop, way=way):
                    at = line - (hop - 1) if way == 0 else line + (hop - 1)
                    hop_copy(st, c, hop, way, at).wait_send()


def by_states(rho_real, rho_imag, hamiltonian, damping, couplings, mode_vector, mode_coef):
    n_aux, rows_dev, width = rho_real.shape
    per_aux = couplings.shape[2]
    devices = lax.axis_size("aux")
    row_devs = lax.axis_size("row")
    lines = devices // 2
    slots = max(1, -(-n_aux * per_aux // devices))
    half = lines * slots
    smem = pl.BlockSpec(memory_space=pltpu.SMEM)
    vmem = pl.BlockSpec(memory_space=pltpu.VMEM)
    anywhere = pl.BlockSpec(memory_space=pl.ANY)
    dma = pltpu.SemaphoreType.DMA
    count = n_aux * per_aux
    lanes = -(-count // 128) * 128
    packed = couplings.transpose(1, 0, 2).reshape(3, count)
    packed = jnp.pad(packed, ((0, 5), (0, lanes - count)))

    rows = rows_dev // CHUNKS
    bf16, f32 = jnp.bfloat16, jnp.float32
    piece = pltpu.VMEM((n_aux, 2 * rows, width), bf16)
    grid = (STAGES, CHUNKS)
    scratch = (
        [pltpu.VMEM((lines * n_aux, 2 * rows, width), bf16)] * (STAGES * CHUNKS)
        + [pltpu.VMEM((n_aux, 2 * row_devs * rows_dev, width), bf16)] * STAGES
        + [piece] * (2 * STAGES * CHUNKS)
        + [
            pltpu.VMEM((n_aux, rows_dev, width), f32),
            pltpu.VMEM((n_aux, rows_dev, width), f32),
            pltpu.VMEM((width, width), f32),
            pltpu.VMEM((2 * half, rows_dev, width), f32),
            pltpu.VMEM((2 * half, rows_dev, width), f32),
            pltpu.VMEM((width, mode_vector.shape[0]), f32),
            pltpu.VMEM((2 * half + 2 * n_aux, 128), jnp.int32),
            pltpu.SMEM((2 * half + 2 * n_aux, 128), jnp.int32),
        ]
        + [pltpu.VMEM((8, lanes), jnp.int32)] * lines
        + [
            pltpu.VMEM((half + 1, 2 * rows, width), f32),
            pltpu.VMEM((n_aux, 2 * rows_dev, width), f32),
            pltpu.VMEM((n_aux, 2 * rows_dev, width), f32),
            pltpu.VMEM((n_aux, 2 * rows_dev, width), f32),
            pltpu.VMEM((n_aux, 2 * rows, width), f32),
            pltpu.VMEM((4 * rows_dev, 2 * width), bf16),
            pltpu.VMEM((width, 2 * width), bf16),
            dma(grid + (2, lines - 1)),
            dma(grid + (2, lines - 1)),
            dma(grid + (row_devs - 1,)),
            dma(grid + (row_devs - 1,)),
            dma(grid),
            dma(grid),
            dma((lines - 1,)),
            dma((lines - 1,)),
            dma((3,)),
        ]
    )
    shape = jax.ShapeDtypeStruct((n_aux, rows_dev, width), f32)
    return pl.pallas_call(
        functools.partial(kernel, lines, row_devs, half, count, per_aux),
        out_shape=(shape, shape),
        in_specs=[smem] * 2 + [anywhere] * 2 + [vmem] * 3,
        out_specs=(vmem, vmem),
        scratch_shapes=scratch,
        compiler_params=pltpu.CompilerParams(
            collective_id=0, has_side_effects=True, vmem_limit_bytes=60 * 1024 * 1024
        ),
    )(damping, mode_coef, rho_real, rho_imag, hamiltonian, mode_vector, packed)


def solution(mesh):
    placed = (
        P("aux", "row", None),
        P("aux", "row", None),
        P(),
        P("aux"),
        P("aux", None, None),
        P(),
        P(),
    )

    def shards(rho_real, rho_imag, hamiltonian, damping, couplings, mode_vector, mode_coef):
        args = (rho_real, rho_imag, hamiltonian, damping, couplings, mode_vector, mode_coef)
        devices = mesh.shape["aux"]
        n_aux, rows_dev, _ = rho_real.shape
        slots = max(1, -(-n_aux * couplings.shape[2] // devices))
        terms_sent = (devices - 1) * slots
        states_sent = devices // 2 * n_aux
        even = devices % 2 == 0 and devices > 4 and mesh.shape["row"] > 1
        if even and states_sent < terms_sent and rows_dev % (8 * CHUNKS) == 0:
            return by_states(*args)
        return by_terms(*args)

    return jax.shard_map(
        shards,
        mesh=mesh,
        in_specs=placed,
        out_specs=(P("aux", "row", None), P("aux", "row", None)),
        check_vma=False,
    )
```
